128 devices in a mesh: seq: 8 (over y_lo, x), head: 16 (over z, y_hi, core).
Axes of the slice: x: 4, y: 4 (y_hi: 2, y_lo: 2; y = y_hi * 2 + y_lo), z: 4, core: 2. Of those that a mesh axis runs over, the one named last changes fastest.
Arguments:
- block_in: bfloat16 [16384, 2048], P('seq', 'head'), may hold values from -6 to 6
- cotangent: bfloat16 [16384, 2048], P('seq', 'head'), may hold values from -6 to 6
- norm_one: float32 [2048], P('head'), may hold values from 0.1 to 1.9
- rec_in: bfloat16 [2048, 2560], P('seq', 'head'), may hold values from -0.125 to 0.125
- rec_gate: bfloat16 [2048, 2560], P('seq', 'head'), may hold values from -0.125 to 0.125
- conv_weight: float32 [4, 2560], P(None, 'head'), may hold values from -3 to 3
- conv_bias: float32 [2560], P('head'), may hold values from -2 to 2
- rate_weight: float32 [16, 160, 160], P('head'), may hold values from -0.5 to 0.5
- rate_bias: float32 [2560], P('head'), may hold values from -3 to 3
- input_weight: float32 [16, 160, 160], P('head'), may hold values from -0.5 to 0.5
- input_bias: float32 [2560], P('head'), may hold values from -3 to 3
- decay_code: int32 [2560], P('head'), may hold values from 920 to 3071, as said below
- rec_out: bfloat16 [2560, 2048], P('head', 'seq'), may hold values from -0.125 to 0.125
- norm_two: float32 [2048], P('head'), may hold values from 0.1 to 1.9
- mlp_gate: bfloat16 [2048, 6144], P('seq', 'head'), may hold values from -0.125 to 0.125
- mlp_up: bfloat16 [2048, 6144], P('seq', 'head'), may hold values from -0.125 to 0.125
- mlp_down: bfloat16 [6144, 2048], P('head', 'seq'), may hold values from -0.15625 to 0.15625
Outputs:
- block_out: bfloat16 [16384, 2048], P('seq', 'head')
- grad_block_in: float32 [16384, 2048], P('seq', 'head')
- grad_norm_one: float32 [2048], P('head')
- grad_rec_in: float32 [2048, 2560], P('seq', 'head')
- grad_rec_gate: float32 [2048, 2560], P('seq', 'head')
- grad_conv_weight: float32 [4, 2560], P(None, 'head')
- grad_conv_bias: float32 [2560], P('head')
- grad_rate_weight: float32 [16, 160, 160], P('head')
- grad_rate_bias: float32 [2560], P('head')
- grad_input_weight: float32 [16, 160, 160], P('head')
- grad_input_bias: float32 [2560], P('head')
- grad_decay_param: float32 [2560], P('head')
- grad_rec_out: float32 [2560, 2048], P('head', 'seq')
- grad_norm_two: float32 [2048], P('head')
- grad_mlp_gate: float32 [2048, 6144], P('seq', 'head')
- grad_mlp_up: float32 [2048, 6144], P('seq', 'head')
- grad_mlp_down: float32 [6144, 2048], P('head', 'seq')
The draws below stay inside these ranges and needn't reach their ends.
Inputs may be any that keep to these rules, and one draw needn't show every extreme that they name: `decay_code`: lambda = code / 256 for each channel.
All inputs are finite; a program needn't handle non-finite values.
Results may differ from the reference program's by a relative error of at most 0.015.
Values may be sent and summed in bfloat16 or wider, within the bound.
A program may use at most 256 MiB of HBM per device.

```python
import jax
import jax.numpy as jnp
from jax import lax

D = 2048
H = 16
HW = 160
FF = 6144
CONV = 4
R = 2560
SEQLEN = 16384


def draw_decay_code(key, part):
    pick_key = jax.random.fold_in(key, 11)
    slow_key = jax.random.fold_in(key, 12)
    fast_key = jax.random.fold_in(key, 13)
    place_key = jax.random.fold_in(key, 14)
    other_key = jax.random.fold_in(key, 15)
    slow_codes = jax.random.randint(slow_key, (R,), 2560, 3072)
    fast_codes = jax.random.randint(fast_key, (R,), 920, 1130)
    picked = jax.random.randint(pick_key, (R,), 0, 2)
    codes = jnp.where(picked == 1, slow_codes, fast_codes).astype(jnp.int32)
    low_place = jax.random.randint(place_key, (), 0, R)
    high_place = (low_place + 1 + jax.random.randint(other_key, (), 0, R - 1)) % R
    codes = codes.at[low_place].set(920)
    codes = codes.at[high_place].set(3071)
    return codes.astype(jnp.int32)


def block_scale(stream_key, dims, shards, least, top_value):
    def one(dim, parts):
        draws = jax.random.uniform(jax.random.fold_in(jax.random.fold_in(stream_key, 6), dim), (parts,), jnp.float32, least / len(shards), top_value / len(shards))
        return jnp.repeat(jnp.exp(draws), dims[dim] // parts).reshape((-1,) + (1,) * (len(dims) - dim - 1))

    loudness = one(*shards[0])
    for cut in shards[1:]:
        loudness = loudness * one(*cut)
    return loudness


def normal_values(rng, extent, spread, most, shards=(), dtype=jnp.bfloat16):
    level = block_scale(rng, extent, shards, -0.22, 0.18) if shards else 1.0
    values = jax.random.normal(rng, extent, jnp.float32) * spread * level
    return jnp.minimum(jnp.maximum(values, -most), most).astype(dtype)


def setup_inputs(seed: int = 0) -> dict:
    seeds = jax.random.split(jax.random.key(seed), 18)
    return {
        "block_in": normal_values(seeds[0], (SEQLEN, D), 1.0, 6.0, ((0, 8), (1, 16))),
        "cotangent": normal_values(seeds[1], (SEQLEN, D), 1.0, 6.0, ((0, 8), (1, 16))),
        "norm_one": jnp.clip(1.0 + 0.18 * jax.random.normal(seeds[2], (D,), jnp.float32), 0.1, 1.9),
        "rec_in": normal_values(seeds[3], (D, R), D ** -0.5, 0.125, ((0, 8), (1, 16))),
        "rec_gate": normal_values(seeds[4], (D, R), D ** -0.5, 0.125, ((0, 8), (1, 16))),
        "conv_weight": normal_values(seeds[5], (CONV, R), 0.5, 3.0, ((1, 16),), jnp.float32),
        "conv_bias": normal_values(seeds[6], (R,), 0.3, 2.0, ((0, 16),), jnp.float32),
        "rate_weight": normal_values(seeds[7], (H, HW, HW), HW ** -0.5, 0.5, ((0, 16),), jnp.float32),
        "rate_bias": normal_values(seeds[8], (R,), 0.5, 3.0, ((0, 16),), jnp.float32),
        "input_weight": normal_values(seeds[9], (H, HW, HW), HW ** -0.5, 0.5, ((0, 16),), jnp.float32),
        "input_bias": normal_values(seeds[10], (R,), 0.5, 3.0, ((0, 16),), jnp.float32),
        "decay_code": draw_decay_code(jax.random.fold_in(seeds[17], 71), 0),
        "rec_out": normal_values(seeds[12], (R, D), R ** -0.5, 0.125, ((0, 16), (1, 8))),
        "norm_two": jnp.clip(1.0 + 0.18 * jax.random.normal(seeds[13], (D,), jnp.float32), 0.1, 1.9),
        "mlp_gate": normal_values(seeds[14], (D, FF), D ** -0.5, 0.125, ((0, 8), (1, 16))),
        "mlp_up": normal_values(seeds[15], (D, FF), D ** -0.5, 0.125, ((0, 8), (1, 16))),
        "mlp_down": normal_values(seeds[16], (FF, D), (FF // 4) ** -0.5, 0.15625, ((0, 16), (1, 8))),
    }


@jax.custom_vjp
def low(v):
    return lax.optimization_barrier(v.astype(jnp.bfloat16)).astype(jnp.float32)

@jax.custom_vjp
def low_back(v):
    return v

def low_keep(v):
    return (low(v), None)

def low_pass(kept, grad):
    return (grad,)

def back_keep(v):
    return (v, None)

def back_low(kept, grad):
    return (low(grad),)
low.defvjp(low_keep, low_pass)
low_back.defvjp(back_keep, back_low)
HIGH = lax.Precision.HIGHEST
EPS = 1e-06

def pair_combine(earlier, later):
    return (earlier[0] * later[0], later[0] * earlier[1] + later[1])

def rms_norm(values, gain_vec):
    inv_rms = lax.rsqrt(lax.optimization_barrier(jnp.mean(values * values, axis=1, keepdims=True)) + EPS)
    return values * inv_rms * gain_vec[None, :]

def exact_gelu(values):
    return jax.nn.gelu(values, approximate=False)

def forward(block_in, norm_one, rec_in, rec_gate, conv_weight, conv_bias, rate_weight, rate_bias, input_weight, input_bias, decay_param, rec_out, norm_two, mlp_gate, mlp_up, mlp_down):
    normed_one = low(rms_norm(block_in, norm_one))
    x_branch = low_back(jnp.dot(normed_one, rec_in, precision=HIGH))
    y_branch = low_back(jnp.dot(normed_one, rec_gate, precision=HIGH))
    x_sent = low(x_branch)
    seq_len = x_sent.shape[0]
    padded = jnp.concatenate([jnp.zeros((CONV - 1, x_sent.shape[1]), jnp.float32), x_sent], axis=0)
    conv_out = conv_bias[None, :] + jnp.zeros_like(x_sent)
    for offset in range(CONV):
        conv_out = conv_out + conv_weight[offset][None, :] * padded[CONV - 1 - offset:CONV - 1 - offset + seq_len]
    split_in = conv_out.reshape(seq_len, H, HW)
    rate_gate = jax.nn.sigmoid(jnp.einsum('lhi,hij->lhj', split_in, rate_weight, precision=HIGH).reshape(seq_len, H * HW) + rate_bias[None, :])
    input_gate = jax.nn.sigmoid(jnp.einsum('lhi,hij->lhj', split_in, input_weight, precision=HIGH).reshape(seq_len, H * HW) + input_bias[None, :])
    log_decay = -8.0 * rate_gate * jax.nn.softplus(-decay_param)[None, :]
    decay = jnp.exp(log_decay)
    source = jnp.sqrt(-jnp.expm1(2.0 * log_decay)) * input_gate * conv_out
    running, state = lax.associative_scan(pair_combine, (decay, source), axis=0)
    gated = low(state * exact_gelu(y_branch))
    mixed = low_back(jnp.dot(gated, rec_out, precision=HIGH))
    resid = block_in + mixed
    normed_two = low(rms_norm(resid, norm_two))
    gate_pre = low_back(jnp.dot(normed_two, mlp_gate, precision=HIGH))
    up_pre = low_back(jnp.dot(normed_two, mlp_up, precision=HIGH))
    act_rows = low(exact_gelu(gate_pre) * up_pre)
    mlp_out = low_back(jnp.dot(act_rows, mlp_down, precision=HIGH))
    return resid + mlp_out

def reference(block_in, cotangent, norm_one, rec_in, rec_gate, conv_weight, conv_bias, rate_weight, rate_bias, input_weight, input_bias, decay_code, rec_out, norm_two, mlp_gate, mlp_up, mlp_down):
    decay_param = decay_code.astype(jnp.float32) / 256.0
    result, pullback = jax.vjp(forward, block_in.astype(jnp.float32), norm_one, rec_in.astype(jnp.float32), rec_gate.astype(jnp.float32), conv_weight, conv_bias, rate_weight, rate_bias, input_weight, input_bias, decay_param, rec_out.astype(jnp.float32), norm_two, mlp_gate.astype(jnp.float32), mlp_up.astype(jnp.float32), mlp_down.astype(jnp.float32))
    grads = pullback(cotangent.astype(jnp.float32))
    return (result.astype(jnp.bfloat16), grads[0], grads[1], grads[2], grads[3], grads[4], grads[5], grads[6], grads[7], grads[8], grads[9], grads[10], grads[11], grads[12], grads[13], grads[14], grads[15])
```

```python
import jax
import jax.numpy as jnp
from jax import lax
from jax.experimental import pallas as pl
from jax.experimental.pallas import tpu as pltpu
from jax.sharding import Mesh, PartitionSpec as P

D = 2048
CONV = 4
EPS = 1e-06
TOK = 512
CH = 640
HW = 160
MESH = pl.DeviceIdType.MESH
SEQ = ("ylo", "x")
HEAD = ("z", "yhi", "core")
QUAD = ("yhi", "core")
PLANE = ("ylo", "x", "yhi", "core")
bf = jnp.bfloat16
f32 = jnp.float32
VMEM = pl.BlockSpec(memory_space=pltpu.VMEM)


def shape(dims, dtype):
    return jax.ShapeDtypeStruct(dims, dtype)


def params(cid):
    return pltpu.CompilerParams(
        collective_id=cid, has_side_effects=True, vmem_limit_bytes=56 * 2**20
    )


def quad_device(index):
    return {"yhi": index // 2, "core": lax.rem(index, 2)}


def plane_device(block):
    return {
        "ylo": block // 16,
        "x": lax.rem(block // 4, 4),
        "yhi": lax.rem(block // 2, 2),
        "core": lax.rem(block, 2),
    }


def meet(devices):
    barrier = pltpu.get_barrier_semaphore()
    for device in devices:
        pl.semaphore_signal(barrier, inc=1, device_id=device, device_id_type=MESH)
    pl.semaphore_wait(barrier, len(devices))


def ring_gather(full, width, send, recv, base):
    z = lax.axis_index("z")
    right, left = lax.rem(z + 1, 4), lax.rem(z + 3, 4)
    half = full.shape[0] // 2

    def part(row, block):
        return full.at[pl.ds(row, half), pl.ds(pl.multiple_of(block * width, 128), width)]

    def start(i, row, block, to):
        copy = pltpu.make_async_remote_copy(
            src_ref=part(row, block),
            dst_ref=part(row, block),
            send_sem=send.at[base + i],
            recv_sem=recv.at[base + i],
            device_id={"z": to},
            device_id_type=MESH,
        )
        copy.start()
        return copy

    c0 = start(0, 0, z, right)
    c1 = start(1, half, z, left)
    c2 = start(2, half, z, right)
    c3 = start(3, 0, z, left)
    c0.wait_recv()
    c4 = start(4, 0, left, right)
    c1.wait_recv()
    c5 = start(5, half, right, left)
    for copy in (c2, c3, c4, c5):
        copy.wait_recv()
    for copy in (c0, c1, c2, c3, c4, c5):
        copy.wait_send()


def ring_sum(part, out, got, sent, send, recv, base):
    z = lax.axis_index("z")
    right, left, far = lax.rem(z + 1, 4), lax.rem(z + 3, 4), lax.rem(z + 2, 4)
    half = part.shape[0] // 2
    width = part.shape[1] // 4
    lo, hi = pl.ds(0, half), pl.ds(half, half)

    def cols(block):
        return pl.ds(pl.multiple_of(block * width, 128), width)

    def start(i, source, to):
        copy = pltpu.make_async_remote_copy(
            src_ref=source,
            dst_ref=got.at[i],
            send_sem=send.at[base + i],
            recv_sem=recv.at[base + i],
            device_id={"z": to},
            device_id_type=MESH,
        )
        copy.start()
        return copy

    c0 = start(0, part.at[lo, cols(far)], right)
    c1 = start(1, part.at[hi, cols(far)], left)
    c2 = start(2, part.at[hi, cols(right)], right)
    c3 = start(3, part.at[lo, cols(left)], left)
    c0.wait_recv()
    sent[0] = (got[0].astype(f32) + part[lo, cols(right)].astype(f32)).astype(bf)
    c4 = start(4, sent.at[0], right)
    c1.wait_recv()
    sent[1] = (got[1].astype(f32) + part[hi, cols(left)].astype(f32)).astype(bf)
    c5 = start(5, sent.at[1], left)
    c3.wait_recv()
    c4.wait_recv()
    out[lo, :] = part[lo, cols(z)].astype(f32) + got[3].astype(f32) + got[4].astype(f32)
    c2.wait_recv()
    c5.wait_recv()
    out[hi, :] = part[hi, cols(z)].astype(f32) + got[2].astype(f32) + got[5].astype(f32)
    for copy in (c0, c1, c2, c3, c4, c5):
        copy.wait_send()


def z_others():
    z = lax.axis_index("z")
    return [{"z": lax.rem(z + j, 4)} for j in (1, 2, 3)]


def quad_others():
    me = lax.axis_index("yhi") * 2 + lax.axis_index("core")
    return [quad_device(lax.rem(me + j, 4)) for j in (1, 2, 3)]


def quad_gather_tokens(tokens, full, send, recv, base):
    z = lax.axis_index("z")
    me = lax.axis_index("yhi") * 2 + lax.axis_index("core")
    mine = pl.ds(pl.multiple_of(z * 512 + me * 128, 128), 128)
    copies = []
    for j in (1, 2, 3):
        peer = lax.rem(me + j, 4)
        copy = pltpu.make_async_remote_copy(
            src_ref=tokens.at[pl.ds(pl.multiple_of(peer * TOK, TOK), TOK), :],
            dst_ref=full.at[:, mine],
            send_sem=send.at[base + j - 1],
            recv_sem=recv.at[base + j - 1],
            device_id=quad_device(peer),
            device_id_type=MESH,
        )
        copy.start()
        copies.append(copy)
    full[:, mine] = tokens[pl.ds(pl.multiple_of(me * TOK, TOK), TOK), :]
    return copies


def entry_kernel(
    tokens, rate_w, input_w, vectors, norms,
    full, rate_all, input_all, vectors_all, norms_all,
    send, recv,
):
    z = lax.axis_index("z")
    me = lax.axis_index("yhi") * 2 + lax.axis_index("core")
    meet(quad_others() + z_others())
    copies = quad_gather_tokens(tokens, full, send, recv, 0)
    small = []
    for k, (source, target) in enumerate(
        (
            (norms, norms_all.at[z, me]),
            (vectors, vectors_all.at[me]),
            (rate_w, rate_all.at[me]),
            (input_w, input_all.at[me]),
        )
    ):
        for j in (1, 2, 3):
            copy = pltpu.make_async_remote_copy(
                src_ref=source,
                dst_ref=target,
                send_sem=send.at[9 + 3 * k + j - 1],
                recv_sem=recv.at[9 + 3 * k + j - 1],
                device_id=quad_device(lax.rem(me + j, 4)),
                device_id_type=MESH,
            )
            copy.start()
            small.append(copy)
    norms_all[z, me] = norms[...]
    vectors_all[me] = vectors[...]
    rate_all[me] = rate_w[...]
    input_all[me] = input_w[...]
    for copy in copies:
        copy.wait_recv()
    for copy in small[:3]:
        copy.wait_recv()
    for j in (1, 2, 3):
        copy = pltpu.make_async_remote_copy(
            src_ref=norms_all.at[z],
            dst_ref=norms_all.at[z],
            send_sem=send.at[21 + j - 1],
            recv_sem=recv.at[21 + j - 1],
            device_id={"z": lax.rem(z + j, 4)},
            device_id_type=MESH,
        )
        copy.start()
        small.append(copy)
    ring_gather(full, 512, send, recv, 3)
    for copy in small[3:]:
        copy.wait_recv()
    for copy in copies + small:
        copy.wait_send()


def entry(tokens, rate_w, input_w, vectors, norms):
    return pl.pallas_call(
        entry_kernel,
        out_shape=(
            shape((TOK, D), bf),
            shape((4, HW, HW), f32),
            shape((4, HW, HW), f32),
            shape((4, 16, HW), f32),
            shape((4, 4, 8, 128), f32),
        ),
        in_specs=[VMEM] * 5,
        out_specs=[VMEM] * 5,
        scratch_shapes=[pltpu.SemaphoreType.DMA((24,)), pltpu.SemaphoreType.DMA((24,))],
        compiler_params=params(0),
        name="entry",
    )(tokens, rate_w, input_w, vectors, norms)


def gather_kernel(tokens, full, send, recv):
    meet(quad_others() + z_others())
    copies = quad_gather_tokens(tokens, full, send, recv, 0)
    for copy in copies:
        copy.wait_recv()
    ring_gather(full, 512, send, recv, 3)
    for copy in copies:
        copy.wait_send()


def gather_tokens(tokens):
    return pl.pallas_call(
        gather_kernel,
        out_shape=shape((TOK, D), bf),
        in_specs=[VMEM],
        out_specs=VMEM,
        scratch_shapes=[pltpu.SemaphoreType.DMA((9,)), pltpu.SemaphoreType.DMA((9,))],
        compiler_params=params(1),
        name="gather_tokens",
    )(tokens)


def allsum_kernel(part, full, own, got, sent, send, recv):
    z = lax.axis_index("z")
    meet(z_others())
    ring_sum(part, own, got, sent, send, recv, 0)
    full[:, pl.ds(pl.multiple_of(z * 512, 128), 512)] = own[...].astype(bf)
    ring_gather(full, 512, send, recv, 6)


def allsum(part):
    return pl.pallas_call(
        allsum_kernel,
        out_shape=(shape((TOK, D), bf), shape((TOK, 512), f32)),
        in_specs=[VMEM],
        out_specs=[VMEM] * 2,
        scratch_shapes=[
            pltpu.VMEM((6, TOK // 2, 512), bf),
            pltpu.VMEM((2, TOK // 2, 512), bf),
            pltpu.SemaphoreType.DMA((12,)),
            pltpu.SemaphoreType.DMA((12,)),
        ],
        compiler_params=params(2),
        name="allsum",
    )(part)


def sum_kernel(part, own, got, sent, send, recv):
    meet(z_others())
    ring_sum(part, own, got, sent, send, recv, 0)


def ownsum(part):
    return pl.pallas_call(
        sum_kernel,
        out_shape=shape((TOK, 512), f32),
        in_specs=[VMEM],
        out_specs=VMEM,
        scratch_shapes=[
            pltpu.VMEM((6, TOK // 2, 512), bf),
            pltpu.VMEM((2, TOK // 2, 512), bf),
            pltpu.SemaphoreType.DMA((6,)),
            pltpu.SemaphoreType.DMA((6,)),
        ],
        compiler_params=params(3),
        name="ownsum",
    )(part)


def line_devices():
    ylo, x = lax.axis_index("ylo"), lax.axis_index("x")
    row = ylo * 4 + x
    rows = [
        {"ylo": lax.rem(row + j, 8) // 4, "x": lax.rem(row + j, 4)} for j in range(1, 8)
    ]
    return quad_others() + rows


def my_block():
    row = lax.axis_index("ylo") * 4 + lax.axis_index("x")
    return row * 4 + lax.axis_index("yhi") * 2 + lax.axis_index("core")


def line_prefix(mine, quad, rows, total, send, recv, base, backward):
    me = lax.axis_index("yhi") * 2 + lax.axis_index("core")
    row = lax.axis_index("ylo") * 4 + lax.axis_index("x")
    copies = []
    for j in (1, 2, 3):
        copy = pltpu.make_async_remote_copy(
            src_ref=mine,
            dst_ref=quad.at[me],
            send_sem=send.at[base + j - 1],
            recv_sem=recv.at[base + j - 1],
            device_id=quad_device(lax.rem(me + j, 4)),
            device_id_type=MESH,
        )
        copy.start()
        copies.append(copy)
    quad[me] = mine[...]
    for copy in copies:
        copy.wait_recv()
    ones = jnp.ones((1, CH), f32)
    zeros = jnp.zeros((1, CH), f32)
    prod, end, prod_all, end_all = ones, zeros, ones, zeros
    for turn in range(4):
        q = 3 - turn if backward else turn
        a, b = quad[q, 0:1, :], quad[q, 1:2, :]
        end_all = a * end_all + b
        prod_all = a * prod_all
        take = (q > me) if backward else (q < me)
        end = jnp.where(take, a * end + b, end)
        prod = jnp.where(take, a * prod, prod)
    total[0:1, :] = prod_all
    total[1:2, :] = end_all
    for j in range(1, 8):
        other = lax.rem(row + j, 8)
        copy = pltpu.make_async_remote_copy(
            src_ref=total,
            dst_ref=rows.at[row],
            send_sem=send.at[base + 2 + j],
            recv_sem=recv.at[base + 2 + j],
            device_id={"ylo": other // 4, "x": lax.rem(other, 4)},
            device_id_type=MESH,
        )
        copy.start()
        copies.append(copy)
    rows[row] = total[...]
    for copy in copies[3:]:
        copy.wait_recv()
    came = zeros
    for turn in range(8):
        r = 7 - turn if backward else turn
        a, b = rows[r, 0:1, :], rows[r, 1:2, :]
        take = (r > row) if backward else (r < row)
        came = jnp.where(take, a * came + b, came)
    for copy in copies:
        copy.wait_send()
    return prod * came + end


def split(values):
    high = values.astype(bf)
    return high, (values - high.astype(f32)).astype(bf)


def dot3(a, b, dims):
    (ah, al), (bh, bl) = a, b

    def one(p, q):
        return lax.dot_general(p, q, (dims, ((), ())), preferred_element_type=f32)

    return one(ah, bh) + (one(al, bh) + one(ah, bl))


def minus_expm1(v):
    near = -v * (
        1.0
        + v * (1 / 2) * (1.0 + v * (1 / 3) * (1.0 + v * (1 / 4) * (1.0 + v * (1 / 5) * (1.0 + v * (1 / 6)))))
    )
    return jnp.where(v > -0.3, near, 1.0 - jnp.exp(v))


def gelu_parts(v):
    cdf = 0.5 * (1.0 + lax.erf(v * 0.7071067811865476))
    pdf = 0.3989422804014327 * jnp.exp(-0.5 * v * v)
    return v * cdf, cdf + v * pdf


def shifted(values, by, fill, reverse):
    rows = lax.broadcasted_iota(jnp.int32, values.shape, 0)
    size = values.shape[0]
    if reverse:
        return jnp.where(rows < size - by, pltpu.roll(values, size - by, 0), fill)
    return jnp.where(rows >= by, pltpu.roll(values, by, 0), fill)


def behind(near, by):
    return near[8:24, :] if by == 0 else pltpu.roll(near, by, 0)[8:24, :]


def ahead(near, by):
    size = near.shape[0]
    return pltpu.roll(near, size - by, 0)[0 : size - 8, :]


def scan8(a, b, reverse):
    for by in (1, 2, 4):
        b = b + a * shifted(b, by, 0.0, reverse)
        a = a * shifted(a, by, 1.0, reverse)
    return a, b


def loop(count, body):
    def one(i, carry):
        body(i)
        return carry

    lax.fori_loop(0, count, one, 0)


def forward_kernel(
    xs, yb, gate_hi, gate_lo, vec,
    c, rate, gin, a, m, h, hy, ext, state_in, total_a,
    halo, pre, prod, mine, quad, rows, total, send, recv,
):
    block = my_block()
    after, before = lax.rem(block + 1, 32), lax.rem(block + 31, 32)
    meet(line_devices() + [plane_device(after), plane_device(before)])
    edge = pltpu.make_async_remote_copy(
        src_ref=xs.at[pl.ds(TOK - 16, 16), :],
        dst_ref=halo,
        send_sem=send.at[10],
        recv_sem=recv.at[10],
        device_id=plane_device(after),
        device_id_type=MESH,
    )
    edge.start()

    def widen(i):
        ext[pl.ds(pl.multiple_of(8 + i * 16, 8), 16), :] = xs[
            pl.ds(pl.multiple_of(i * 16, 16), 16), :
        ].astype(f32)

    loop(TOK // 16, widen)
    edge.wait_recv()
    ext[0:8, :] = jnp.where(block > 0, halo[8:16, :].astype(f32), 0.0)

    def conv(i):
        r = i * 16
        near = ext[pl.ds(pl.multiple_of(r, 16), 24), :]
        acc = vec[4:5, :] + vec[0:1, :] * near[8:24, :]
        for k in (1, 2, 3):
            acc = acc + vec[k : k + 1, :] * behind(near, k)
        c[pl.ds(pl.multiple_of(r, 16), 16), :] = acc

    loop(TOK // 16, conv)

    def gates(i):
        r = pl.ds(pl.multiple_of(i * 128, 128), 128)
        pre[r, :] = dot3(split(c[r, :]), (gate_hi[...], gate_lo[...]), ((1,), (0,)))

    loop(TOK // 128, gates)

    def point(i, carry):
        prod_in, state = carry
        r = pl.ds(pl.multiple_of(i * 8, 8), 8)
        rr = jax.nn.sigmoid(pre[r, 0:CH] + vec[5:6, :])
        gg = jax.nn.sigmoid(pre[r, CH:] + vec[6:7, :])
        log_a = -8.0 * rr * vec[7:8, :]
        aa = jnp.exp(log_a)
        mm = jnp.sqrt(minus_expm1(2.0 * log_a))
        rate[r, :] = rr
        gin[r, :] = gg
        a[r, :] = aa
        m[r, :] = mm
        pa, hb = scan8(aa, mm * gg * c[r, :], False)
        hb = hb + pa * state
        pa = pa * prod_in
        h[r, :] = hb
        prod[r, :] = pa
        return pa[7:8, :], hb[7:8, :]

    last = lax.fori_loop(
        0, TOK // 8, point, (jnp.ones((1, CH), f32), jnp.zeros((1, CH), f32))
    )
    mine[...] = jnp.zeros((8, CH), f32)
    total[...] = jnp.zeros((8, CH), f32)
    mine[0:1, :] = last[0]
    mine[1:2, :] = last[1]
    came = line_prefix(mine, quad, rows, total, send, recv, 0, False)
    state_in[...] = jnp.broadcast_to(came, (8, CH))
    total_a[...] = jnp.broadcast_to(last[0], (8, CH))

    def finish(i):
        r = pl.ds(pl.multiple_of(i * 16, 16), 16)
        hh = h[r, :] + prod[r, :] * came
        h[r, :] = hh
        hy[r, :] = (hh * gelu_parts(yb[r, :])[0]).astype(bf)

    loop(TOK // 16, finish)
    edge.wait_send()


def forward_scan(xs, yb, gate_hi, gate_lo, vec):
    wide = shape((TOK, CH), f32)
    return pl.pallas_call(
        forward_kernel,
        out_shape=(
            wide, wide, wide, wide, wide, wide,
            shape((TOK, CH), bf),
            shape((TOK + 8, CH), f32),
            shape((8, CH), f32),
            shape((8, CH), f32),
        ),
        in_specs=[VMEM] * 5,
        out_specs=[VMEM] * 10,
        scratch_shapes=[
            pltpu.VMEM((16, CH), bf),
            pltpu.VMEM((TOK, 2 * CH), f32),
            pltpu.VMEM((TOK, CH), f32),
            pltpu.VMEM((8, CH), f32),
            pltpu.VMEM((4, 8, CH), f32),
            pltpu.VMEM((8, 8, CH), f32),
            pltpu.VMEM((8, CH), f32),
            pltpu.SemaphoreType.DMA((11,)),
            pltpu.SemaphoreType.DMA((11,)),
        ],
        compiler_params=params(4),
        name="forward_scan",
    )(xs, yb, gate_hi, gate_lo, vec)


def backward_kernel(
    dhy, yb, gate_hi, gate_lo, vec, c, rate, gin, a, m, h, ext, state_in, total_a,
    dxb, dyb, dgate, sums,
    e, apad, hpad, q, prod, pri, dc, halo, mine, quad, rows, total, send, recv,
):
    block = my_block()
    after, before = lax.rem(block + 1, 32), lax.rem(block + 31, 32)
    meet(line_devices() + [plane_device(after), plane_device(before)])

    def direct(i):
        r = pl.ds(pl.multiple_of(i * 16, 16), 16)
        value, slope = gelu_parts(yb[r, :])
        grad = dhy[r, :]
        hh = h[r, :]
        e[r, :] = grad * value
        dyb[r, :] = (grad * hh * slope).astype(bf)
        apad[r, :] = a[r, :]
        hpad[pl.ds(pl.multiple_of(i * 16 + 8, 8), 16), :] = hh

    loop(TOK // 16, direct)
    apad[TOK : TOK + 8, :] = jnp.ones((8, CH), f32)
    hpad[0:8, :] = state_in[...]

    def adjoint(i, carry):
        prod_in, state = carry
        r0 = TOK - 8 - i * 8
        r = pl.ds(pl.multiple_of(r0, 8), 8)
        next_a = ahead(apad[pl.ds(pl.multiple_of(r0, 8), 16), :], 1)
        pa, qb = scan8(next_a, e[r, :], True)
        qb = qb + pa * state
        pa = pa * prod_in
        q[r, :] = qb
        prod[r, :] = pa
        return pa[0:1, :], qb[0:1, :]

    last = lax.fori_loop(
        0, TOK // 8, adjoint, (jnp.ones((1, CH), f32), jnp.zeros((1, CH), f32))
    )
    mine[...] = jnp.zeros((8, CH), f32)
    total[...] = jnp.zeros((8, CH), f32)
    mine[0:1, :] = total_a[0:1, :]
    mine[1:2, :] = a[0:1, :] * last[1]
    came = line_prefix(mine, quad, rows, total, send, recv, 0, True)

    def point(i, carry):
        s_rate, s_input, s_decay = carry
        r = pl.ds(pl.multiple_of(i * 8, 8), 8)
        qq = q[r, :] + prod[r, :] * came
        aa, rr, gg, mm, cc = a[r, :], rate[r, :], gin[r, :], m[r, :], c[r, :]
        earlier = pltpu.roll(hpad[pl.ds(pl.multiple_of(i * 8, 8), 16), :], 1, 0)[8:16, :]
        grad_log = aa * (qq * earlier - qq * gg * cc * aa / mm)
        pr = -8.0 * vec[7:8, :] * grad_log * rr * (1.0 - rr)
        pi = qq * mm * cc * gg * (1.0 - gg)
        pri[r, 0:CH] = pr
        pri[r, CH:] = pi
        dc[r, :] = qq * mm * gg
        return s_rate + pr, s_input + pi, s_decay + 8.0 * rr * vec[8:9, :] * grad_log

    none = jnp.zeros((8, CH), f32)
    s_rate, s_input, s_decay = lax.fori_loop(0, TOK // 8, point, (none, none, none))

    def spread(i):
        r = pl.ds(pl.multiple_of(i * 128, 128), 128)
        dc[r, :] = dc[r, :] + dot3(split(pri[r, :]), (gate_hi[...], gate_lo[...]), ((1,), (1,)))

    loop(TOK // 128, spread)
    edge = pltpu.make_async_remote_copy(
        src_ref=dc.at[pl.ds(0, 8), :],
        dst_ref=halo,
        send_sem=send.at[10],
        recv_sem=recv.at[10],
        device_id=plane_device(before),
        device_id_type=MESH,
    )
    edge.start()
    dgate[...] = dot3(split(c[...]), split(pri[...]), ((0,), (0,)))
    edge.wait_recv()
    dc[TOK : TOK + 8, :] = jnp.where(block < 31, halo[...], 0.0)

    def taps(i, carry):
        r = i * 16
        here = pl.ds(pl.multiple_of(r, 16), 16)
        later = dc[pl.ds(pl.multiple_of(r, 16), 24), :]
        near = ext[pl.ds(pl.multiple_of(r, 16), 24), :]
        dd = later[0:16, :]
        out = vec[0:1, :] * dd
        for k in (1, 2, 3):
            out = out + vec[k : k + 1, :] * ahead(later, k)
        dxb[here, :] = out.astype(bf)

        def fold(v):
            return v[0:8, :] + v[8:16, :]

        got = [carry[0] + fold(dd)]
        for k in range(4):
            got.append(carry[1 + k] + fold(dd * behind(near, k)))
        return tuple(got)

    s_bias, *s_taps = lax.fori_loop(0, TOK // 16, taps, (none,) * 5)

    def put(row, value):
        sums[row : row + 1, :] = jnp.sum(value, axis=0, keepdims=True)

    for k in range(4):
        put(k, s_taps[k])
    put(4, s_bias)
    put(5, s_rate)
    put(6, s_input)
    put(7, s_decay)
    edge.wait_send()


def backward_scan(dhy, yb, gate_hi, gate_lo, vec, c, rate, gin, a, m, h, ext, state_in, total_a):
    return pl.pallas_call(
        backward_kernel,
        out_shape=(
            shape((TOK, CH), bf),
            shape((TOK, CH), bf),
            shape((CH, 2 * CH), f32),
            shape((8, CH), f32),
        ),
        in_specs=[VMEM] * 14,
        out_specs=[VMEM] * 4,
        scratch_shapes=[
            pltpu.VMEM((TOK, CH), f32),
            pltpu.VMEM((TOK + 8, CH), f32),
            pltpu.VMEM((TOK + 8, CH), f32),
            pltpu.VMEM((TOK, CH), f32),
            pltpu.VMEM((TOK, CH), f32),
            pltpu.VMEM((TOK, 2 * CH), f32),
            pltpu.VMEM((TOK + 8, CH), f32),
            pltpu.VMEM((8, CH), f32),
            pltpu.VMEM((8, CH), f32),
            pltpu.VMEM((4, 8, CH), f32),
            pltpu.VMEM((8, 8, CH), f32),
            pltpu.VMEM((8, CH), f32),
            pltpu.SemaphoreType.DMA((11,)),
            pltpu.SemaphoreType.DMA((11,)),
        ],
        compiler_params=params(5),
        name="backward_scan",
    )(dhy, yb, gate_hi, gate_lo, vec, c, rate, gin, a, m, h, ext, state_in, total_a)


def dot(p, q):
    return jnp.dot(p, q, preferred_element_type=f32)


def dot_t0(p, q):
    return lax.dot_general(p, q, (((0,), (0,)), ((), ())), preferred_element_type=f32)


def dot_t1(p, q):
    return lax.dot_general(p, q, (((1,), (1,)), ((), ())), preferred_element_type=f32)


def place():
    ylo, x, yhi, core = (lax.axis_index(n) for n in ("ylo", "x", "yhi", "core"))
    return ylo, x, yhi, core

def x_device(i):
    return {"x": i}

def y_device(i):
    return {"yhi": i // 2, "ylo": lax.rem(i, 2)}

def around(i):
    return lax.rem(i + 1, 4), lax.rem(i + 3, 4), lax.rem(i + 2, 4)

def plane_neighbours():
    ylo, x, yhi, core = place()
    y = yhi * 2 + ylo
    xr, xl, _ = around(x)
    yr, yl, _ = around(y)
    return [x_device(xr), x_device(xl), y_device(yr), y_device(yl), {"core": 1 - core}]

class Sender:
    def __init__(self, send, recv, base):
        self.send, self.recv, self.next, self.all = send, recv, base, []
    def __call__(self, source, target, device):
        copy = pltpu.make_async_remote_copy(
            src_ref=source, dst_ref=target, send_sem=self.send.at[self.next], recv_sem=self.recv.at[self.next],
            device_id=device, device_id_type=MESH)
        copy.start()
        self.next += 1
        self.all.append(copy)
        return copy
    def drain(self):
        for copy in self.all:
            copy.wait_send()

def got(copies):
    for copy in copies:
        copy.wait_recv()

GATHER_COPIES = 32
def cut(r):
    a = (r // 32) * 16
    a1 = ((a // 16 + 1) // 2) * 16
    b1 = (((r - a) // 16 + 1) // 2) * 16
    return a, a1, b1

def plane_gather(own, full, send, recv, base, local):
    put = Sender(send, recv, base)
    k, r, _ = own.shape
    ylo, x, yhi, core = place()
    y = yhi * 2 + ylo
    xr, xl, xf = around(x)
    yr, yl, yf = around(y)
    a, a1, b1 = cut(r)
    top, bottom = pl.ds(0, a), pl.ds(a, r - a)
    top1, top2 = pl.ds(0, a1), pl.ds(a1, a - a1)
    bot1, bot2 = pl.ds(a, b1), pl.ds(a + b1, r - a - b1)
    sib = {"core": 1 - core}
    def cols(lo, xx):
        return pl.ds(pl.multiple_of(lo * 1024 + xx * 256, 256), 256)
    def one(rows, yy, xx):
        return full.at[:, (yy // 2) * 2 + core, rows, cols(lax.rem(yy, 2), xx)]
    def row(rows, yy):
        return full.at[:, (yy // 2) * 2 + core, rows, pl.ds(pl.multiple_of(lax.rem(yy, 2) * 1024, 1024), 1024)]
    keep = pltpu.make_async_copy(own, one(pl.ds(0, r), y, x), local)
    keep.start()
    ha, hb = own.at[:, top, :], own.at[:, bottom, :]
    p = [put(ha, one(top, y, x), x_device(xr)), put(ha, one(top, y, x), x_device(xl)),
         put(hb, one(bottom, y, x), y_device(yr)), put(hb, one(bottom, y, x), y_device(yl))]
    yield
    got(p)
    keep.wait()
    p = [put(one(top1, y, xl), one(top1, y, xl), x_device(xr)), put(one(top2, y, xr), one(top2, y, xr), x_device(xl)),
         put(one(bot1, yl, x), one(bot1, yl, x), y_device(yr)), put(one(bot2, yr, x), one(bot2, yr, x), y_device(yl))]
    yield
    got(p)
    def pieces(rows, xx):
        out = []
        for lo in (0, 1):
            for hi in (0, 1):
                out.append(full.at[:, 2 * hi + core, rows, cols(lo, xx)])
        return out
    def send_row(rows, yy, device):
        return [put(row(rows, yy), row(rows, yy), device)]
    def send_col(rows, xx, device):
        return [put(s, s, device) for s in pieces(rows, xx)]
    p = send_row(top, y, y_device(yr)) + send_row(top, y, y_device(yl))
    p += send_col(bottom, x, x_device(xr)) + send_col(bottom, x, x_device(xl))
    s = send_row(top, y, sib) + send_col(bottom, x, sib)
    yield
    got(p)
    p = send_row(top1, yl, y_device(yr)) + send_row(top2, yr, y_device(yl))
    p += send_col(bot1, xl, x_device(xr)) + send_col(bot2, xr, x_device(xl))
    s += send_row(top, yl, sib) + send_row(top, yr, sib) + send_col(bottom, xl, sib) + send_col(bottom, xr, sib)
    yield
    got(p)
    s += send_row(top, yf, sib) + send_col(bottom, xf, sib)
    yield
    got(s)
    put.drain()
    assert put.next - base <= 56, put.next - base


def run_all(steps):
    for _ in steps:
        pass


def weights_kernel(own, full, send, recv, local):
    meet(plane_neighbours())
    run_all(plane_gather(own, full, send, recv, 0, local))


def gather_weights(own, cid):
    k, r, _ = own.shape
    return pl.pallas_call(
        weights_kernel,
        out_shape=shape((k, 4, r, D), bf),
        in_specs=[pl.BlockSpec(memory_space=pl.ANY)],
        out_specs=pl.BlockSpec(memory_space=pl.ANY),
        scratch_shapes=[
            pltpu.SemaphoreType.DMA((56,)),
            pltpu.SemaphoreType.DMA((56,)),
            pltpu.SemaphoreType.DMA,
        ],
        compiler_params=params(cid),
        name="gather_weights",
    )(own)


def plane_sum(part, out, fold, ga, gb, ha, hb, sa, sb, ra2, rb2, send, recv, base):
    put = Sender(send, recv, base)
    _, r, _ = part.shape
    ylo, x, yhi, core = place()
    y = yhi * 2 + ylo
    xr, xl, xf = around(x)
    yr, yl, yf = around(y)
    a = -(-r // 64) * 32
    h, g = a // 2, (r - a) // 2
    sib = {"core": 1 - core}
    p = []
    for hi in (0, 1):
        p.append(put(part.at[2 * hi + 1 - core], fold.at[hi], sib))
    yield
    for hi in (0, 1):
        p[hi].wait_recv()
        def body(i, carry, hi=hi):
            rr = pl.ds(pl.multiple_of(i * 16, 16), 16)
            fold[hi, rr, :] = (fold[hi, rr, :].astype(f32) + part[2 * hi + core, rr, :].astype(f32)).astype(bf)
            return carry
        lax.fori_loop(0, r // 16, body, 0)
    def ycols(yy):
        return pl.ds(pl.multiple_of(lax.rem(yy, 2) * 1024, 1024), 1024)
    def a_block(yy, first):
        return fold.at[yy // 2, pl.ds(0 if first else h, h), ycols(yy)]
    def b_block(xx, first, l):
        return fold.at[:, pl.ds(a + (0 if first else g), g), pl.ds(pl.multiple_of(l * 1024 + xx * 256, 256), 256)]
    yR, yL, xR, xL = y_device(yr), y_device(yl), x_device(xr), x_device(xl)
    def sendb(i, xx, first, dev):
        return [put(b_block(xx, first, l), gb.at[i, l], dev) for l in (0, 1)]
    pa = [put(a_block(yf, True), ga.at[0], yR), put(a_block(yf, False), ga.at[1], yL)]
    pb = [sendb(0, xf, True, xR), sendb(1, xf, False, xL)]
    pa += [put(a_block(yr, False), ga.at[2], yR), put(a_block(yl, True), ga.at[3], yL)]
    pb += [sendb(2, xr, False, xR), sendb(3, xl, True, xL)]
    yield
    def add_a(dst, i, block, n):
        def body(j, carry):
            rr = pl.ds(pl.multiple_of(j * 16, 16), 16)
            dst[rr, :] = (ga[i, rr, :].astype(f32) + block[rr, :].astype(f32)).astype(bf)
            return carry
        lax.fori_loop(0, n // 16, body, 0)
    def add_b(dst, i, xx, first):
        for l in (0, 1):
            for hi in (0, 1):
                block = fold.at[hi, pl.ds(a + (0 if first else g), g), pl.ds(pl.multiple_of(l * 1024 + xx * 256, 256), 256)]
                def body(j, carry):
                    rr = pl.ds(pl.multiple_of(j * 16, 16), 16)
                    dst[l, hi, rr, :] = (gb[i, l, hi, rr, :].astype(f32) + block[rr, :].astype(f32)).astype(bf)
                    return carry
                lax.fori_loop(0, g // 16, body, 0)
    pa[0].wait_recv()
    add_a(sa.at[0], 0, a_block(yr, True), h)
    pa.append(put(sa.at[0], ga.at[4], yR))
    got(pb[0])
    add_b(sb.at[0], 0, xr, True)
    pb.append([put(sb.at[0], gb.at[4], xR)])
    pa[1].wait_recv()
    add_a(sa.at[1], 1, a_block(yl, False), h)
    pa.append(put(sa.at[1], ga.at[5], yL))
    got(pb[1])
    add_b(sb.at[1], 1, xl, False)
    pb.append([put(sb.at[1], gb.at[5], xL)])
    yield
    def fin_a(first, i, j):
        def body(n, carry):
            rr = pl.ds(pl.multiple_of(n * 16, 16), 16)
            block = a_block(y, first)
            ra2[pl.ds(pl.multiple_of((0 if first else h) + n * 16, 16), 16), :] = (
                block[rr, :].astype(f32) + ga[i, rr, :].astype(f32) + ga[j, rr, :].astype(f32)).astype(bf)
            return carry
        lax.fori_loop(0, h // 16, body, 0)
    def fin_b(first, i, j):
        for l in (0, 1):
            for hi in (0, 1):
                block = fold.at[hi, pl.ds(a + (0 if first else g), g), pl.ds(pl.multiple_of(l * 1024 + x * 256, 256), 256)]
                def body(n, carry):
                    rr = pl.ds(pl.multiple_of(n * 16, 16), 16)
                    rb2[l, hi, pl.ds(pl.multiple_of((0 if first else g) + n * 16, 16), 16), :] = (
                        block[rr, :].astype(f32) + gb[i, l, hi, rr, :].astype(f32) + gb[j, l, hi, rr, :].astype(f32)).astype(bf)
                    return carry
                lax.fori_loop(0, g // 16, body, 0)
    got([pa[3], pa[4]])
    fin_a(True, 3, 4)
    got([pa[2], pa[5]])
    fin_a(False, 2, 5)
    got(pb[3] + pb[4])
    fin_b(True, 3, 4)
    got(pb[2] + pb[5])
    fin_b(False, 2, 5)
    def a2(xx, first):
        return ra2.at[pl.ds(0 if first else h, h), pl.ds(pl.multiple_of(xx * 256, 256), 256)]
    def b2(yy, first):
        return rb2.at[lax.rem(yy, 2), yy // 2, pl.ds(0 if first else g, g), :]
    qa = [put(a2(xf, True), ha.at[0], xR), put(a2(xf, False), ha.at[1], xL), put(a2(xr, False), ha.at[2], xR), put(a2(xl, True), ha.at[3], xL)]
    qb = [put(b2(yf, True), hb.at[0], yR), put(b2(yf, False), hb.at[1], yL), put(b2(yr, False), hb.at[2], yR), put(b2(yl, True), hb.at[3], yL)]
    yield
    sa2, sb2 = ha.at[pl.ds(6, 2)], hb.at[pl.ds(6, 2)]
    qa[0].wait_recv()
    sa2[0] = (ha[0].astype(f32) + a2(xr, True)[...].astype(f32)).astype(bf)
    qa.append(put(sa2.at[0], ha.at[4], xR))
    qb[0].wait_recv()
    sb2[0] = (hb[0].astype(f32) + b2(yr, True)[...].astype(f32)).astype(bf)
    qb.append(put(sb2.at[0], hb.at[4], yR))
    qa[1].wait_recv()
    sa2[1] = (ha[1].astype(f32) + a2(xl, False)[...].astype(f32)).astype(bf)
    qa.append(put(sa2.at[1], ha.at[5], xL))
    qb[1].wait_recv()
    sb2[1] = (hb[1].astype(f32) + b2(yl, False)[...].astype(f32)).astype(bf)
    qb.append(put(sb2.at[1], hb.at[5], yL))
    yield
    got(qa[2:] + qb[2:])
    def w(v): return v.astype(f32)
    out[0:h, :] = w(a2(x, True)[...]) + w(ha[3]) + w(ha[4])
    out[h:a, :] = w(a2(x, False)[...]) + w(ha[2]) + w(ha[5])
    out[a:a + g, :] = w(b2(y, True)[...]) + w(hb[3]) + w(hb[4])
    out[a + g:, :] = w(b2(y, False)[...]) + w(hb[2]) + w(hb[5])
    put.drain()


def sum_scratch(r):
    a = -(-r // 64) * 32
    h, g = a // 2, (r - a) // 2
    V = pltpu.VMEM
    return [V((2, r, 2048), bf), V((6, h, 1024), bf), V((6, 2, 2, g, 256), bf), V((8, h, 256), bf), V((8, g, 256), bf),
            V((2, h, 1024), bf), V((2, 2, 2, g, 256), bf), V((a, 1024), bf), V((2, 2, r - a, 256), bf)]


def grads_kernel(part, out, *rest):
    meet(plane_neighbours())
    run_all(plane_sum(part, out, *rest, 0))


def sum_grads(part, cid):
    _, r, _ = part.shape
    return pl.pallas_call(
        grads_kernel,
        out_shape=shape((r, 256), f32),
        in_specs=[VMEM],
        out_specs=VMEM,
        scratch_shapes=sum_scratch(r)
        + [pltpu.SemaphoreType.DMA((30,)), pltpu.SemaphoreType.DMA((30,))],
        compiler_params=params(cid),
        name="sum_grads",
    )(part)


def small_kernel(blocks, gains, small, gain, zgot, qgot, qgain, rgot, rgain, mine, send, recv):
    z = lax.axis_index("z")
    me = lax.axis_index("yhi") * 2 + lax.axis_index("core")
    row = lax.axis_index("ylo") * 4 + lax.axis_index("x")
    meet(line_devices() + z_others())
    put = Sender(send, recv, 0)
    zs, qs = [], []
    for j in (1, 2, 3):
        to = lax.rem(z + j, 4)
        zs.append(put(gains.at[to], zgot.at[j - 1], {"z": to}))
    for j in (1, 2, 3):
        to = lax.rem(me + j, 4)
        qs.append(put(blocks.at[to], qgot.at[j - 1], quad_device(to)))
    got(zs)
    qgain[3] = gains[z] + zgot[0] + zgot[1] + zgot[2]
    for j in (1, 2, 3):
        to = lax.rem(me + j, 4)
        qs.append(put(qgain.at[3, to], qgain.at[j - 1, 0], quad_device(to)))
    got(qs)
    mine[...] = blocks[me] + qgot[0] + qgot[1] + qgot[2]
    rgain[7] = qgain[3, me] + qgain[0, 0] + qgain[1, 0] + qgain[2, 0]
    rs = []

    def seq(j):
        to = lax.rem(row + j, 8)
        return to, {"ylo": to // 4, "x": lax.rem(to, 4)}

    for j in range(1, 8):
        to, device = seq(j)
        rs.append(put(mine.at[pl.ds(pl.multiple_of(to * 48, 8), 48), :], rgot.at[j - 1], device))
        rs.append(put(rgain.at[7], rgain.at[j - 1], device))
    got(rs)
    own = pl.ds(pl.multiple_of(row * 48, 8), 48)
    total = mine[own, :]
    gain_total = rgain[7]
    for j in range(7):
        total = total + rgot[j]
        gain_total = gain_total + rgain[j]
    small[own, :] = total
    gain[...] = gain_total
    ag = []
    for j in range(1, 8):
        _, device = seq(j)
        ag.append(put(small.at[own, :], small.at[own, :], device))
    got(ag)
    put.drain()


def small_sums(blocks, gains):
    return pl.pallas_call(
        small_kernel,
        out_shape=(shape((384, HW), f32), shape((8, 128), f32)),
        in_specs=[VMEM] * 2,
        out_specs=[VMEM] * 2,
        scratch_shapes=[
            pltpu.VMEM((3, 4, 8, 128), f32),
            pltpu.VMEM((3, 384, HW), f32),
            pltpu.VMEM((4, 4, 8, 128), f32),
            pltpu.VMEM((7, 48, HW), f32),
            pltpu.VMEM((8, 8, 128), f32),
            pltpu.VMEM((384, HW), f32),
            pltpu.SemaphoreType.DMA((30,)),
            pltpu.SemaphoreType.DMA((30,)),
        ],
        compiler_params=params(8),
        name="small_sums",
    )(blocks, gains)


def to_tokens(own):
    return lax.all_to_all(own, QUAD, split_axis=1, concat_axis=0, tiled=True)


def block_diagonal(blocks):
    rows = [
        jnp.concatenate(
            [jnp.zeros((HW, HW * i), f32), blocks[i], jnp.zeros((HW, HW * (3 - i)), f32)], axis=1
        )
        for i in range(4)
    ]
    return jnp.concatenate(rows, axis=0)


def per_device(
    block_in, cotangent, norm_one, rec_in, rec_gate, conv_weight, conv_bias,
    rate_weight, rate_bias, input_weight, input_bias, decay_code, rec_out,
    norm_two, mlp_gate, mlp_up, mlp_down,
):
    decay = decay_code.astype(f32) / 256.0
    vectors = jnp.concatenate(
        [
            conv_weight,
            conv_bias[None],
            rate_bias[None],
            input_bias[None],
            jax.nn.softplus(-decay)[None],
            jax.nn.sigmoid(-decay)[None],
            jnp.zeros((7, HW), f32),
        ],
        axis=0,
    )
    norms = jnp.concatenate([norm_one[None], norm_two[None], jnp.zeros((6, 128), f32)], axis=0)
    x_full, rate_all, input_all, vec_all, norms_all = entry(
        block_in, rate_weight[0], input_weight[0], vectors, norms
    )
    w_rec = gather_weights(jnp.stack([rec_in.T, rec_gate.T, rec_out]), 6).reshape(3, CH, D)
    w_mlp = gather_weights(jnp.stack([mlp_gate.T, mlp_up.T, mlp_down]), 7).reshape(3, 1536, D)
    w_in, w_gate_rec, w_out = w_rec[0], w_rec[1], w_rec[2]
    w_gate, w_up, w_down = w_mlp[0], w_mlp[1], w_mlp[2]
    vec = vec_all.transpose(1, 0, 2).reshape(16, CH)
    gains = norms_all.reshape(16, 8, 128)
    gain_one = gains[:, 0].reshape(1, D)
    gain_two = gains[:, 1].reshape(1, D)
    gate_hi, gate_lo = split(
        jnp.concatenate([block_diagonal(rate_all), block_diagonal(input_all)], axis=1)
    )

    x_rows = x_full.astype(f32)
    inv_one = lax.rsqrt(jnp.mean(x_rows * x_rows, axis=1, keepdims=True) + EPS)
    n_one = (x_rows * inv_one * gain_one).astype(bf)
    xb = dot_t1(n_one, w_in)
    yb = dot_t1(n_one, w_gate_rec)
    c, rate, gin, a, m, h, hy, ext, state_in, total_a = forward_scan(
        xb.astype(bf), yb, gate_hi, gate_lo, vec
    )
    mix_full, mix_own = allsum(dot(hy, w_out).astype(bf))
    z = lax.axis_index("z")
    x_own = lax.dynamic_slice(x_full, (0, z * 512), (TOK, 512)).astype(f32)
    z_rows = x_rows + mix_full.astype(f32)
    z_own = x_own + mix_own
    inv_two = lax.rsqrt(jnp.mean(z_rows * z_rows, axis=1, keepdims=True) + EPS)
    n_two = (z_rows * inv_two * gain_two).astype(bf)

    g = dot_t1(n_two, w_gate)
    u = dot_t1(n_two, w_up)
    gelu_g, slope_g = gelu_parts(g)
    act = (gelu_g * u).astype(bf)
    cot_full = gather_tokens(cotangent)
    dact = dot_t1(cot_full, w_down)
    dg = (dact * u * slope_g).astype(bf)
    du = (dact * gelu_g).astype(bf)
    inner_two = jnp.sum(dg.astype(f32) * g + du.astype(f32) * u, axis=1, keepdims=True)
    dn_two = dot(dg, w_gate) + dot(du, w_up)
    step_two = dn_two * inv_two * gain_two - z_rows * (inv_two * inv_two * inner_two / D)
    gain_two_sums = jnp.sum(dn_two * z_rows * inv_two, axis=0)
    back_full, back_own = allsum(step_two.astype(bf))
    dmix = (cot_full.astype(f32) + back_full.astype(f32)).astype(bf)
    cot_own = lax.dynamic_slice(cot_full, (0, z * 512), (TOK, 512)).astype(f32)
    dz_own = cot_own + back_own

    mlp_own = ownsum(dot(act, w_down).astype(bf))
    block_out = to_tokens((z_own + mlp_own).astype(bf))
    grad_down = sum_grads(dot_t0(act, cot_full).astype(bf).reshape(4, 384, D), 9)
    grad_gate = sum_grads(dot_t0(dg, n_two).astype(bf).reshape(4, 384, D), 9).T
    grad_up = sum_grads(dot_t0(du, n_two).astype(bf).reshape(4, 384, D), 9).T

    dhy = dot_t1(dmix, w_out)
    dxb, dyb, dgate, sums = backward_scan(
        dhy, yb, gate_hi, gate_lo, vec, c, rate, gin, a, m, h, ext, state_in, total_a
    )
    inner_one = jnp.sum(dxb.astype(f32) * xb + dyb.astype(f32) * yb, axis=1, keepdims=True)
    dn_one = dot(dxb, w_in) + dot(dyb, w_gate_rec)
    step_one = dn_one * inv_one * gain_one - x_rows * (inv_one * inv_one * inner_one / D)
    gain_one_sums = jnp.sum(dn_one * x_rows * inv_one, axis=0)
    grad_own = dz_own + ownsum(step_one.astype(bf))
    grad_in = to_tokens(grad_own.astype(bf)).astype(f32)
    grad_rec = jnp.concatenate(
        [dot_t0(p, q).astype(bf).reshape(4, HW, D) for p, q in ((dxb, n_one), (dyb, n_one), (hy, dmix))],
        axis=1,
    )
    grad_rec = sum_grads(grad_rec, 10)
    grad_rec_in, grad_rec_gate, grad_out = grad_rec[:HW].T, grad_rec[HW : 2 * HW].T, grad_rec[2 * HW :]

    blocks = [
        jnp.concatenate(
            [
                dgate[HW * i : HW * (i + 1), HW * i : HW * (i + 1)],
                dgate[HW * i : HW * (i + 1), CH + HW * i : CH + HW * (i + 1)],
                sums[:, HW * i : HW * (i + 1)],
                jnp.zeros((56, HW), f32),
            ],
            axis=0,
        )
        for i in range(4)
    ]
    gains = jnp.stack([gain_one_sums.reshape(4, 4, 128), gain_two_sums.reshape(4, 4, 128)], axis=2)
    gains = jnp.concatenate([gains, jnp.zeros((4, 4, 6, 128), f32)], axis=2)
    small, gain_sums = small_sums(jnp.stack(blocks), gains)
    vector_grads = small[2 * HW : 2 * HW + 8]
    return (
        block_out,
        grad_in,
        gain_sums[0],
        grad_rec_in,
        grad_rec_gate,
        vector_grads[0:4],
        vector_grads[4],
        small[:HW][None],
        vector_grads[5],
        small[HW : 2 * HW][None],
        vector_grads[6],
        vector_grads[7],
        grad_out,
        gain_sums[1],
        grad_gate,
        grad_up,
        grad_down,
    )


def solution(mesh):
    fine = Mesh(mesh.devices.reshape(2, 4, 4, 2, 2), ("ylo", "x", "z", "yhi", "core"))
    both = P(SEQ, HEAD)
    swap = P(HEAD, SEQ)
    vector = P(HEAD)
    stack = P(HEAD, None, None)
    taps = P(None, HEAD)
    return jax.shard_map(
        per_device,
        mesh=fine,
        in_specs=(
            both, both, vector, both, both, taps, vector, stack, vector, stack, vector, vector,
            swap, vector, both, both, swap,
        ),
        out_specs=(
            both, both, vector, both, both, taps, vector, stack, vector, stack, vector, vector,
            swap, vector, both, both, swap,
        ),
        check_vma=False,
    )
```

```python
import jax
import jax.numpy as jnp
from jax import lax
from jax.experimental import pallas as pl
from jax.experimental.pallas import tpu as pltpu
from jax.sharding import Mesh, PartitionSpec as P

D = 2048
CONV = 4
EPS = 1e-06
TOK = 512
CH = 640
HW = 160
MESH = pl.DeviceIdType.MESH
SEQ = ("ylo", "x")
HEAD = ("z", "yhi", "core")
QUAD = ("yhi", "core")
PLANE = ("ylo", "x", "yhi", "core")
bf = jnp.bfloat16
f32 = jnp.float32
VMEM = pl.BlockSpec(memory_space=pltpu.VMEM)
ANY = pl.BlockSpec(memory_space=pl.ANY)


def shape(dims, dtype):
    return jax.ShapeDtypeStruct(dims, dtype)


def params(cid):
    return pltpu.CompilerParams(
        collective_id=cid, has_side_effects=True, vmem_limit_bytes=56 * 2**20
    )


def quad_device(index):
    return {"yhi": index // 2, "core": lax.rem(index, 2)}


def plane_device(block):
    return {
        "ylo": block // 16,
        "x": lax.rem(block // 4, 4),
        "yhi": lax.rem(block // 2, 2),
        "core": lax.rem(block, 2),
    }


def meet(devices):
    barrier = pltpu.get_barrier_semaphore()
    for device in devices:
        pl.semaphore_signal(barrier, inc=1, device_id=device, device_id_type=MESH)
    pl.semaphore_wait(barrier, len(devices))


def place():
    ylo, x, yhi, core = (lax.axis_index(n) for n in ("ylo", "x", "yhi", "core"))
    return ylo, x, yhi, core

def x_device(i):
    return {"x": i}

def y_device(i):
    return {"yhi": i // 2, "ylo": lax.rem(i, 2)}

def around(i):
    return lax.rem(i + 1, 4), lax.rem(i + 3, 4), lax.rem(i + 2, 4)

def plane_neighbours():
    ylo, x, yhi, core = place()
    y = yhi * 2 + ylo
    xr, xl, _ = around(x)
    yr, yl, _ = around(y)
    return [x_device(xr), x_device(xl), y_device(yr), y_device(yl), {"core": 1 - core}]

class Sender:
    def __init__(self, send, recv):
        self.send, self.recv, self.all = send, recv, []

    def __call__(self, source, target, device):
        i = len(self.all)
        copy = pltpu.make_async_remote_copy(
            src_ref=source,
            dst_ref=target,
            send_sem=self.send.at[i],
            recv_sem=self.recv.at[i],
            device_id=device,
            device_id_type=MESH,
        )
        copy.start()
        self.all.append(copy)
        return copy

    def drain(self, skip=None):
        for copy in self.all:
            if copy is not skip:
                copy.wait_send()


class Keeper:
    def __init__(self, done):
        self.done, self.count, self.open = done, 0, []

    def __call__(self, source, target):
        copy = pltpu.make_async_copy(source, target, self.done.at[self.count])
        copy.start()
        self.count += 1
        self.open.append(copy)
        return copy

    def wait(self, copy):
        self.open = [c for c in self.open if c is not copy]
        copy.wait()

    def drain(self):
        for copy in self.open:
            copy.wait()


def semaphores(count):
    return [pltpu.SemaphoreType.DMA((count,)), pltpu.SemaphoreType.DMA((count,))]


def got(copies):
    for copy in copies:
        copy.wait_recv()


def step(*plans):
    for plan in plans:
        next(plan, None)


def finish(*plans):
    for plan in plans:
        for _ in plan:
            pass


def z_columns(block):
    return pl.ds(pl.multiple_of(block * 512, 512), 512)


def ring_gather(full, put):
    z = lax.axis_index("z")
    right, left, _ = around(z)
    half = full.shape[0] // 2

    def start(row, block, to):
        part = full.at[pl.ds(row, half), z_columns(block)]
        return put(part, part, {"z": to})

    c0 = start(0, z, right)
    c1 = start(half, z, left)
    c2 = start(half, z, right)
    c3 = start(0, z, left)
    yield
    c0.wait_recv()
    c4 = start(0, left, right)
    c1.wait_recv()
    c5 = start(half, right, left)
    yield
    got([c2, c3, c4, c5])


def ring_sum(part, out, came, sent, put, produce=lambda block: None):
    z = lax.axis_index("z")
    right, left, far = around(z)
    half = part.shape[0] // 2
    lo, hi = pl.ds(0, half), pl.ds(half, half)
    cols = z_columns

    def start(i, source, to):
        return put(source, came.at[i], {"z": to})

    produce(far)
    c0 = start(0, part.at[lo, cols(far)], right)
    c1 = start(1, part.at[hi, cols(far)], left)
    produce(right)
    c2 = start(2, part.at[hi, cols(right)], right)
    produce(left)
    c3 = start(3, part.at[lo, cols(left)], left)
    produce(z)
    yield
    c0.wait_recv()
    sent[0] = (came[0].astype(f32) + part[lo, cols(right)].astype(f32)).astype(bf)
    c4 = start(4, sent.at[0], right)
    c1.wait_recv()
    sent[1] = (came[1].astype(f32) + part[hi, cols(left)].astype(f32)).astype(bf)
    c5 = start(5, sent.at[1], left)
    yield
    got([c3, c4])
    out[lo, :] = part[lo, cols(z)].astype(f32) + came[3].astype(f32) + came[4].astype(f32)
    got([c2, c5])
    out[hi, :] = part[hi, cols(z)].astype(f32) + came[2].astype(f32) + came[5].astype(f32)


def ring_scratch():
    return [pltpu.VMEM((6, TOK // 2, 512), bf), pltpu.VMEM((2, TOK // 2, 512), bf)]


def z_others():
    z = lax.axis_index("z")
    return [{"z": lax.rem(z + j, 4)} for j in (1, 2, 3)]


def quad_others():
    me = lax.axis_index("yhi") * 2 + lax.axis_index("core")
    return [quad_device(lax.rem(me + j, 4)) for j in (1, 2, 3)]


def quad_gather(tokens, full, put, keep):
    z = lax.axis_index("z")
    me = lax.axis_index("yhi") * 2 + lax.axis_index("core")
    mine = pl.ds(pl.multiple_of(z * 512 + me * 128, 128), 128)
    copies = []
    for j in (1, 2, 3):
        peer = lax.rem(me + j, 4)
        source = tokens.at[pl.ds(pl.multiple_of(peer * TOK, TOK), TOK), :]
        copies.append(put(source, full.at[:, mine], quad_device(peer)))
    own = keep(tokens.at[pl.ds(pl.multiple_of(me * TOK, TOK), TOK), :], full.at[:, mine])
    return copies, own


def token_gather(tokens, full, put, keep):
    copies, own = quad_gather(tokens, full, put, keep)
    yield
    got(copies)
    keep.wait(own)
    yield from ring_gather(full, put)


def quad_scatter(own, tokens, put):
    me = lax.axis_index("yhi") * 2 + lax.axis_index("core")
    rows = pl.ds(pl.multiple_of(me * TOK, TOK), TOK)
    copies = []
    for j in (1, 2, 3):
        peer = lax.rem(me + j, 4)
        source = own.at[:, pl.ds(pl.multiple_of(peer * 128, 128), 128)]
        copies.append(put(source, tokens.at[rows, :], quad_device(peer)))
    tokens[rows, :] = own[:, pl.ds(pl.multiple_of(me * 128, 128), 128)]
    return copies


GATHER_COPIES = 48
SUM_COPIES = 30


def resid_kernel(part, down, gate, full, own, down_sum, gate_sum, *rest):
    z = lax.axis_index("z")
    meet(z_others() + plane_neighbours())
    (came, sent), rest = rest[:2], rest[2:]
    a, b = rest[:SUM_SCRATCH], rest[SUM_SCRATCH : 2 * SUM_SCRATCH]
    put = Sender(*rest[2 * SUM_SCRATCH :])
    total = ring_sum(part, own, came, sent, put)
    plane_a = plane_sum(down, down_sum, a, put)
    plane_b = plane_sum(gate, gate_sum, b, put)
    step(total, plane_a, plane_b)
    step(total, plane_a)
    finish(total)
    full[:, z_columns(z)] = own[...].astype(bf)
    spread = ring_gather(full, put)
    step(spread, plane_b, plane_a, spread, plane_b, plane_a, plane_b, plane_a, plane_b)
    finish(spread, plane_a, plane_b)
    put.drain()


def resid_sum(part, down, gate):
    r = down.shape[1]
    return pl.pallas_call(
        resid_kernel,
        out_shape=(
            shape((TOK, D), bf),
            shape((TOK, 512), f32),
            shape((r, 256), f32),
            shape((r, 256), f32),
        ),
        in_specs=[VMEM] * 3,
        out_specs=[VMEM] * 4,
        scratch_shapes=ring_scratch()
        + sum_scratch(r)
        + sum_scratch(r)
        + semaphores(12 + 2 * SUM_COPIES),
        compiler_params=params(3),
        name="resid_sum",
    )(part, down, gate)


def cut(r):
    a = (r // 32) * 16
    a1 = ((a // 16 + 1) // 2) * 16
    b1 = (((r - a) // 16 + 1) // 2) * 16
    return a, a1, b1

def plane_gather(own, full, put, keep):
    k, r, _ = own.shape
    ylo, x, yhi, core = place()
    y = yhi * 2 + ylo
    xr, xl, xf = around(x)
    yr, yl, yf = around(y)
    a, a1, b1 = cut(r)
    top, bottom = (0, a), (a, r - a)
    top1, top2 = (0, a1), (a1, a - a1)
    bot1, bot2 = (a, b1), (a + b1, r - a - b1)

    def span(quarter, rows):
        return pl.ds(pl.multiple_of(quarter * r + rows[0], 16), rows[1])

    sib = {"core": 1 - core}
    def cols(lo, xx):
        return pl.ds(pl.multiple_of(lo * 1024 + xx * 256, 256), 256)
    def one(rows, yy, xx):
        return full.at[:, span((yy // 2) * 2 + core, rows), cols(lax.rem(yy, 2), xx)]
    def row(rows, yy):
        return full.at[:, span((yy // 2) * 2 + core, rows), pl.ds(pl.multiple_of(lax.rem(yy, 2) * 1024, 1024), 1024)]
    kept = keep(own, one((0, r), y, x))
    ha, hb = own.at[:, pl.ds(*top), :], own.at[:, pl.ds(*bottom), :]
    p = [put(ha, one(top, y, x), x_device(xr)), put(ha, one(top, y, x), x_device(xl)),
         put(hb, one(bottom, y, x), y_device(yr)), put(hb, one(bottom, y, x), y_device(yl))]
    yield
    got(p)
    keep.wait(kept)
    p = [put(one(top1, y, xl), one(top1, y, xl), x_device(xr)), put(one(top2, y, xr), one(top2, y, xr), x_device(xl)),
         put(one(bot1, yl, x), one(bot1, yl, x), y_device(yr)), put(one(bot2, yr, x), one(bot2, yr, x), y_device(yl))]
    yield
    got(p)
    def pieces(rows, xx):
        out = []
        for lo in (0, 1):
            for hi in (0, 1):
                out.append(full.at[:, span(2 * hi + core, rows), cols(lo, xx)])
        return out
    def send_row(rows, yy, device):
        return [put(row(rows, yy), row(rows, yy), device)]
    def send_col(rows, xx, device):
        return [put(s, s, device) for s in pieces(rows, xx)]
    p = send_row(top, y, y_device(yr)) + send_row(top, y, y_device(yl))
    p += send_col(bottom, x, x_device(xr)) + send_col(bottom, x, x_device(xl))
    s = send_row(top, y, sib) + send_col(bottom, x, sib)
    yield
    got(p)
    p = send_row(top1, yl, y_device(yr)) + send_row(top2, yr, y_device(yl))
    p += send_col(bot1, xl, x_device(xr)) + send_col(bot2, xr, x_device(xl))
    s += send_row(top, yl, sib) + send_row(top, yr, sib) + send_col(bottom, xl, sib) + send_col(bottom, xr, sib)
    yield
    got(p)
    s += send_row(top, yf, sib) + send_col(bottom, xf, sib)
    yield
    got(s)


def plane_sum(part, out, scratch, put):
    fold, ga, gb, ha, hb, sa, sb, ra2, rb2 = scratch
    _, r, _ = part.shape
    ylo, x, yhi, core = place()
    y = yhi * 2 + ylo
    xr, xl, xf = around(x)
    yr, yl, yf = around(y)
    a = -(-r // 64) * 32
    h, g = a // 2, (r - a) // 2
    sib = {"core": 1 - core}
    p = []
    for hi in (0, 1):
        p.append(put(part.at[2 * hi + 1 - core], fold.at[hi], sib))
    yield
    for hi in (0, 1):
        p[hi].wait_recv()
        def body(i, carry, hi=hi):
            rr = pl.ds(pl.multiple_of(i * 16, 16), 16)
            fold[hi, rr, :] = (fold[hi, rr, :].astype(f32) + part[2 * hi + core, rr, :].astype(f32)).astype(bf)
            return carry
        lax.fori_loop(0, r // 16, body, 0)
    def ycols(yy):
        return pl.ds(pl.multiple_of(lax.rem(yy, 2) * 1024, 1024), 1024)
    def a_block(yy, first):
        return fold.at[yy // 2, pl.ds(0 if first else h, h), ycols(yy)]
    def b_block(xx, first, l):
        return fold.at[:, pl.ds(a + (0 if first else g), g), pl.ds(pl.multiple_of(l * 1024 + xx * 256, 256), 256)]
    yR, yL, xR, xL = y_device(yr), y_device(yl), x_device(xr), x_device(xl)
    def sendb(i, xx, first, dev):
        return [put(b_block(xx, first, l), gb.at[i, l], dev) for l in (0, 1)]
    pa = [put(a_block(yf, True), ga.at[0], yR), put(a_block(yf, False), ga.at[1], yL)]
    pb = [sendb(0, xf, True, xR), sendb(1, xf, False, xL)]
    pa += [put(a_block(yr, False), ga.at[2], yR), put(a_block(yl, True), ga.at[3], yL)]
    pb += [sendb(2, xr, False, xR), sendb(3, xl, True, xL)]
    yield
    def add_a(dst, i, block, n):
        def body(j, carry):
            rr = pl.ds(pl.multiple_of(j * 16, 16), 16)
            dst[rr, :] = (ga[i, rr, :].astype(f32) + block[rr, :].astype(f32)).astype(bf)
            return carry
        lax.fori_loop(0, n // 16, body, 0)
    def add_b(dst, i, xx, first):
        for l in (0, 1):
            for hi in (0, 1):
                block = fold.at[hi, pl.ds(a + (0 if first else g), g), pl.ds(pl.multiple_of(l * 1024 + xx * 256, 256), 256)]
                def body(j, carry):
                    rr = pl.ds(pl.multiple_of(j * 16, 16), 16)
                    dst[l, hi, rr, :] = (gb[i, l, hi, rr, :].astype(f32) + block[rr, :].astype(f32)).astype(bf)
                    return carry
                lax.fori_loop(0, g // 16, body, 0)
    pa[0].wait_recv()
    add_a(sa.at[0], 0, a_block(yr, True), h)
    pa.append(put(sa.at[0], ga.at[4], yR))
    got(pb[0])
    add_b(sb.at[0], 0, xr, True)
    pb.append([put(sb.at[0], gb.at[4], xR)])
    pa[1].wait_recv()
    add_a(sa.at[1], 1, a_block(yl, False), h)
    pa.append(put(sa.at[1], ga.at[5], yL))
    got(pb[1])
    add_b(sb.at[1], 1, xl, False)
    pb.append([put(sb.at[1], gb.at[5], xL)])
    yield
    def fin_a(first, i, j):
        def body(n, carry):
            rr = pl.ds(pl.multiple_of(n * 16, 16), 16)
            block = a_block(y, first)
            ra2[pl.ds(pl.multiple_of((0 if first else h) + n * 16, 16), 16), :] = (
                block[rr, :].astype(f32) + ga[i, rr, :].astype(f32) + ga[j, rr, :].astype(f32)).astype(bf)
            return carry
        lax.fori_loop(0, h // 16, body, 0)
    def fin_b(first, i, j):
        for l in (0, 1):
            for hi in (0, 1):
                block = fold.at[hi, pl.ds(a + (0 if first else g), g), pl.ds(pl.multiple_of(l * 1024 + x * 256, 256), 256)]
                def body(n, carry):
                    rr = pl.ds(pl.multiple_of(n * 16, 16), 16)
                    rb2[l, hi, pl.ds(pl.multiple_of((0 if first else g) + n * 16, 16), 16), :] = (
                        block[rr, :].astype(f32) + gb[i, l, hi, rr, :].astype(f32) + gb[j, l, hi, rr, :].astype(f32)).astype(bf)
                    return carry
                lax.fori_loop(0, g // 16, body, 0)
    got([pa[3], pa[4]])
    fin_a(True, 3, 4)
    got([pa[2], pa[5]])
    fin_a(False, 2, 5)
    got(pb[3] + pb[4])
    fin_b(True, 3, 4)
    got(pb[2] + pb[5])
    fin_b(False, 2, 5)
    def a2(xx, first):
        return ra2.at[pl.ds(0 if first else h, h), pl.ds(pl.multiple_of(xx * 256, 256), 256)]
    def b2(yy, first):
        return rb2.at[lax.rem(yy, 2), yy // 2, pl.ds(0 if first else g, g), :]
    qa = [put(a2(xf, True), ha.at[0], xR), put(a2(xf, False), ha.at[1], xL), put(a2(xr, False), ha.at[2], xR), put(a2(xl, True), ha.at[3], xL)]
    qb = [put(b2(yf, True), hb.at[0], yR), put(b2(yf, False), hb.at[1], yL), put(b2(yr, False), hb.at[2], yR), put(b2(yl, True), hb.at[3], yL)]
    yield
    sa2, sb2 = ha.at[pl.ds(6, 2)], hb.at[pl.ds(6, 2)]
    qa[0].wait_recv()
    sa2[0] = (ha[0].astype(f32) + a2(xr, True)[...].astype(f32)).astype(bf)
    qa.append(put(sa2.at[0], ha.at[4], xR))
    qb[0].wait_recv()
    sb2[0] = (hb[0].astype(f32) + b2(yr, True)[...].astype(f32)).astype(bf)
    qb.append(put(sb2.at[0], hb.at[4], yR))
    qa[1].wait_recv()
    sa2[1] = (ha[1].astype(f32) + a2(xl, False)[...].astype(f32)).astype(bf)
    qa.append(put(sa2.at[1], ha.at[5], xL))
    qb[1].wait_recv()
    sb2[1] = (hb[1].astype(f32) + b2(yl, False)[...].astype(f32)).astype(bf)
    qb.append(put(sb2.at[1], hb.at[5], yL))
    yield
    got(qa[2:] + qb[2:])
    def w(v): return v.astype(f32)
    out[0:h, :] = w(a2(x, True)[...]) + w(ha[3]) + w(ha[4])
    out[h:a, :] = w(a2(x, False)[...]) + w(ha[2]) + w(ha[5])
    out[a:a + g, :] = w(b2(y, True)[...]) + w(hb[3]) + w(hb[4])
    out[a + g:, :] = w(b2(y, False)[...]) + w(hb[2]) + w(hb[5])


SUM_SCRATCH = 9


def sum_scratch(r):
    a = -(-r // 64) * 32
    h, g = a // 2, (r - a) // 2
    V = pltpu.VMEM
    return [V((2, r, 2048), bf), V((6, h, 1024), bf), V((6, 2, 2, g, 256), bf), V((8, h, 256), bf), V((8, g, 256), bf),
            V((2, h, 1024), bf), V((2, 2, 2, g, 256), bf), V((a, 1024), bf), V((2, 2, r - a, 256), bf)]


def small_sums(blocks, gains, small, gain, scratch, put):
    zgot, qgot, qgain, rgot, rgain, mine = scratch
    z = lax.axis_index("z")
    me = lax.axis_index("yhi") * 2 + lax.axis_index("core")
    row = lax.axis_index("ylo") * 4 + lax.axis_index("x")
    zs, qs = [], []
    for j in (1, 2, 3):
        to = lax.rem(z + j, 4)
        zs.append(put(gains.at[to], zgot.at[j - 1], {"z": to}))
    for j in (1, 2, 3):
        to = lax.rem(me + j, 4)
        qs.append(put(blocks.at[to], qgot.at[j - 1], quad_device(to)))
    yield
    got(zs)
    qgain[3] = gains[z] + zgot[0] + zgot[1] + zgot[2]
    for j in (1, 2, 3):
        to = lax.rem(me + j, 4)
        qs.append(put(qgain.at[3, to], qgain.at[j - 1, 0], quad_device(to)))
    got(qs)
    mine[...] = blocks[me] + qgot[0] + qgot[1] + qgot[2]
    rgain[7] = qgain[3, me] + qgain[0, 0] + qgain[1, 0] + qgain[2, 0]
    rs = []

    def seq(j):
        to = lax.rem(row + j, 8)
        return to, {"ylo": to // 4, "x": lax.rem(to, 4)}

    for j in range(1, 8):
        to, device = seq(j)
        rs.append(put(mine.at[pl.ds(pl.multiple_of(to * 48, 8), 48), :], rgot.at[j - 1], device))
        rs.append(put(rgain.at[7], rgain.at[j - 1], device))
    yield
    got(rs)
    own = pl.ds(pl.multiple_of(row * 48, 8), 48)
    total = mine[own, :]
    gain_total = rgain[7]
    for j in range(7):
        total = total + rgot[j]
        gain_total = gain_total + rgain[j]
    small[own, :] = total
    gain[...] = gain_total
    ag = []
    for j in range(1, 8):
        _, device = seq(j)
        ag.append(put(small.at[own, :], small.at[own, :], device))
    yield
    got(ag)


SMALL_SCRATCH = 6


def small_scratch():
    return [
        pltpu.VMEM((3, 4, 8, 128), f32),
        pltpu.VMEM((3, 384, HW), f32),
        pltpu.VMEM((4, 4, 8, 128), f32),
        pltpu.VMEM((7, 48, HW), f32),
        pltpu.VMEM((8, 8, 128), f32),
        pltpu.VMEM((384, HW), f32),
    ]


def last_kernel(part, dz, rec, blocks, gains, grad_in, rec_sum, small, gain, own, low, *rest):
    meet(z_others() + plane_neighbours() + line_devices())
    (came, sent), rest = rest[:2], rest[2:]
    plane_refs, rest = rest[:SUM_SCRATCH], rest[SUM_SCRATCH:]
    small_refs, rest = rest[:SMALL_SCRATCH], rest[SMALL_SCRATCH:]
    put = Sender(*rest)
    total = ring_sum(part, own, came, sent, put)
    little = small_sums(blocks, gains, small, gain, small_refs, put)
    plane = plane_sum(rec, rec_sum, plane_refs, put)
    step(total, little, plane)
    step(total, plane, little)
    finish(total)
    low[...] = (own[...] + dz[...]).astype(bf)
    back = quad_scatter(low, grad_in, put)
    step(plane, little)
    finish(plane, little)
    got(back)
    put.drain()


def last_sums(part, dz, rec, blocks, gains):
    r = rec.shape[1]
    return pl.pallas_call(
        last_kernel,
        out_shape=(
            shape((4 * TOK, 128), bf),
            shape((r, 256), f32),
            shape((384, HW), f32),
            shape((8, 128), f32),
        ),
        in_specs=[VMEM] * 5,
        out_specs=[VMEM] * 4,
        scratch_shapes=[pltpu.VMEM((TOK, 512), f32), pltpu.VMEM((TOK, 512), bf)]
        + ring_scratch()
        + sum_scratch(r)
        + small_scratch()
        + semaphores(6 + 3 + SUM_COPIES + 30),
        compiler_params=params(5),
        name="last_sums",
    )(part, dz, rec, blocks, gains)


def line_devices():
    ylo, x = lax.axis_index("ylo"), lax.axis_index("x")
    row = ylo * 4 + x
    rows = [
        {"ylo": lax.rem(row + j, 8) // 4, "x": lax.rem(row + j, 4)} for j in range(1, 8)
    ]
    return quad_others() + rows


def my_block():
    row = lax.axis_index("ylo") * 4 + lax.axis_index("x")
    return row * 4 + lax.axis_index("yhi") * 2 + lax.axis_index("core")


def line_prefix(mine, quad, rows, total, put, backward):
    me = lax.axis_index("yhi") * 2 + lax.axis_index("core")
    row = lax.axis_index("ylo") * 4 + lax.axis_index("x")
    copies = []
    for j in (1, 2, 3):
        copies.append(put(mine, quad.at[me], quad_device(lax.rem(me + j, 4))))
    quad[me] = mine[...]
    got(copies)
    ones = jnp.ones((1, CH), f32)
    zeros = jnp.zeros((1, CH), f32)
    prod, end, prod_all, end_all = ones, zeros, ones, zeros
    for turn in range(4):
        q = 3 - turn if backward else turn
        a, b = quad[q, 0:1, :], quad[q, 1:2, :]
        end_all = a * end_all + b
        prod_all = a * prod_all
        take = (q > me) if backward else (q < me)
        end = jnp.where(take, a * end + b, end)
        prod = jnp.where(take, a * prod, prod)
    total[0:1, :] = prod_all
    total[1:2, :] = end_all
    copies = []
    for j in range(1, 8):
        other = lax.rem(row + j, 8)
        copies.append(put(total, rows.at[row], {"ylo": other // 4, "x": lax.rem(other, 4)}))
    rows[row] = total[...]
    got(copies)
    came = zeros
    for turn in range(8):
        r = 7 - turn if backward else turn
        a, b = rows[r, 0:1, :], rows[r, 1:2, :]
        take = (r > row) if backward else (r < row)
        came = jnp.where(take, a * came + b, came)
    return prod * came + end


def pack_square(weight):
    tail = jnp.pad(weight[:, 128:], ((0, 32), (0, 0))).reshape(4, 48, 32)
    return jnp.concatenate([weight[:, :128], tail.transpose(1, 0, 2).reshape(48, 128)], axis=0)


def unpack_square(packed):
    tail = packed[160:208].reshape(48, 4, 32).transpose(1, 0, 2).reshape(192, 32)[:HW]
    return jnp.concatenate([packed[:HW], tail], axis=1)


TAILS = ((0, 48), (48, 48), (96, 48), (144, 16))
SQUARE = 208
PACKED = 2 * SQUARE + 32


def split(values):
    high = values.astype(bf)
    return high, (values - high.astype(f32)).astype(bf)


def dot3(a, b, dims):
    (ah, al), (bh, bl) = a, b

    def one(p, q):
        return lax.dot_general(p, q, (dims, ((), ())), preferred_element_type=f32)

    return one(ah, bh) + (one(al, bh) + one(ah, bl))


def minus_expm1(v):
    near = -v * (
        1.0
        + v * (1 / 2) * (1.0 + v * (1 / 3) * (1.0 + v * (1 / 4) * (1.0 + v * (1 / 5) * (1.0 + v * (1 / 6)))))
    )
    return jnp.where(v > -0.3, near, 1.0 - jnp.exp(v))


def gelu_parts(v):
    cdf = 0.5 * (1.0 + lax.erf(v * 0.7071067811865476))
    pdf = 0.3989422804014327 * jnp.exp(-0.5 * v * v)
    return v * cdf, cdf + v * pdf


def shifted(values, by, fill, reverse):
    rows = lax.broadcasted_iota(jnp.int32, values.shape, 0)
    size = values.shape[0]
    if reverse:
        return jnp.where(rows < size - by, pltpu.roll(values, size - by, 0), fill)
    return jnp.where(rows >= by, pltpu.roll(values, by, 0), fill)


def behind(near, by):
    return near[8:24, :] if by == 0 else pltpu.roll(near, by, 0)[8:24, :]


def ahead(near, by):
    size = near.shape[0]
    return pltpu.roll(near, size - by, 0)[0 : size - 8, :]


def scan8(a, b, reverse):
    for by in (1, 2, 4):
        b = b + a * shifted(b, by, 0.0, reverse)
        a = a * shifted(a, by, 1.0, reverse)
    return a, b


def loop(count, body):
    def one(i, carry):
        body(i)
        return carry

    lax.fori_loop(0, count, one, 0)


def front_kernel(
    tokens, cotangent, packed, norms, own_rec, own_gate, own_up, own_down,
    x_out, n_out, xb_out, yb_out, c_out, rate_out, gin_out, a_out, m_out, h_out, hy_out, ext_out, hi_out, lo_out,
    mix_out, own_out, cot, rec_out, w_gate, w_up, w_down,
    inv, gains, vec, state_in, total_a,
    full, normed, weights, params_all, norms_all,
    xb, yb, c, rate, gin, a, m, h, hy, ext, gate_hi, gate_lo, pre, prod, part, mixed, mix_own,
    halo, mine, quad, rows, total, came_z, sent_z, send, recv, done,
):
    z = lax.axis_index("z")
    me = lax.axis_index("yhi") * 2 + lax.axis_index("core")
    block = my_block()
    after, before = lax.rem(block + 1, 32), lax.rem(block + 31, 32)
    meet(
        line_devices()
        + [plane_device(after), plane_device(before)]
        + plane_neighbours()
        + z_others()
    )
    put = Sender(send, recv)
    keep = Keeper(done)
    params_all[me] = packed[...]
    tokens_in = token_gather(tokens, full, put, keep)
    plane = plane_gather(own_rec, weights, put, keep)
    step(tokens_in, plane)
    small = []
    for j in (1, 2, 3):
        small.append(put(norms, norms_all.at[z, me], quad_device(lax.rem(me + j, 4))))
    norms_all[z, me] = norms[...]
    gate_hi[...] = jnp.zeros((CH, 2 * CH), bf)
    gate_lo[...] = jnp.zeros((CH, 2 * CH), bf)
    step(plane, tokens_in)
    got(small)
    small = []
    for j in (1, 2, 3):
        small.append(put(norms_all.at[z], norms_all.at[z], {"z": lax.rem(z + j, 4)}))
    step(plane, tokens_in)
    got(small)
    for i in range(4):
        for j in range(4):
            gains[:, 128 * (4 * i + j) : 128 * (4 * i + j + 1)] = norms_all[i, j]
    step(plane)
    finish(tokens_in)
    keep(full, x_out)
    other = token_gather(cotangent, cot, put, keep)
    plane_a = plane_gather(own_gate, w_gate, put, keep)
    plane_b = plane_gather(own_up, w_up, put, keep)
    plane_c = plane_gather(own_down, w_down, put, keep)
    core, yhi = lax.axis_index("core"), lax.axis_index("yhi")
    own_params = params_all.at[me]
    near = put(own_params, own_params, {"core": 1 - core})
    across = put(own_params, own_params, {"yhi": 1 - yhi})
    step(plane, other, plane_a)

    def norm(i):
        r = pl.ds(pl.multiple_of(i * 16, 16), 16)
        values = full[r, :].astype(f32)
        mean = jnp.sum(values * values, axis=1, keepdims=True) * (1.0 / D)
        scale = lax.rsqrt(mean + EPS)
        inv[r, :] = jnp.broadcast_to(scale, (16, 128))
        normed[r, :] = (values * scale * gains[0:1, :]).astype(bf)

    loop(TOK // 16, norm)
    keep(normed, n_out)
    finish(plane)
    keep(weights, rec_out)
    across.wait_recv()
    peer_params = params_all.at[lax.rem(me + 2, 4)]
    passed = put(peer_params, peer_params, {"core": 1 - core})
    step(plane_a, other)
    for i, into in ((0, xb), (1, yb)):
        for at, width in ((0, 256), (256, 256), (512, 128)):
            into[:, at : at + width] = lax.dot_general(
                normed[...],
                weights[i, at : at + width, :],
                (((1,), (1,)), ((), ())),
                preferred_element_type=f32,
            )
        if i == 0:
            halo_out = pl.ds(TOK - 16, 16)
            hy[halo_out, :] = xb[halo_out, :].astype(bf)
            edge = put(hy.at[halo_out, :], halo, plane_device(after))
            step(plane_a, plane_b)
    keep(xb, xb_out)
    keep(yb, yb_out)
    step(other)

    def widen(i):
        r = pl.multiple_of(i * 16, 16)
        ext[pl.ds(pl.multiple_of(8 + r, 8), 16), :] = xb[pl.ds(r, 16), :].astype(bf).astype(f32)

    loop(TOK // 16, widen)
    got([near, passed])
    for i in range(4):
        there = HW * i
        vec[:, there : there + 128] = params_all[i, 2 * SQUARE : 2 * SQUARE + 16, :]
        vec[:, there + 128 : there + HW] = params_all[i, 2 * SQUARE + 16 : PACKED, 0:32]
        for k in (0, 1):
            top = SQUARE * k
            high, low = split(params_all[i, top : top + HW, :])
            over = CH * k + HW * i
            gate_hi[there : there + HW, over : over + 128] = high
            gate_lo[there : there + HW, over : over + 128] = low
            for j, (at, size) in enumerate(TAILS):
                high, low = split(params_all[i, top + HW : top + HW + size, 32 * j : 32 * j + 32])
                rows_here = slice(there + at, there + at + size)
                gate_hi[rows_here, over + 128 : over + HW] = high
                gate_lo[rows_here, over + 128 : over + HW] = low
    keep(gate_hi, hi_out)
    keep(gate_lo, lo_out)
    edge.wait_recv()
    ext[0:8, :] = jnp.where(block > 0, halo[8:16, :].astype(f32), 0.0)

    def conv(i):
        r = i * 16
        near = ext[pl.ds(pl.multiple_of(r, 16), 24), :]
        acc = vec[4:5, :] + vec[0:1, :] * near[8:24, :]
        for k in (1, 2, 3):
            acc = acc + vec[k : k + 1, :] * behind(near, k)
        c[pl.ds(pl.multiple_of(r, 16), 16), :] = acc

    loop(TOK // 16, conv)
    keep(ext, ext_out)
    keep(c, c_out)
    step(plane_b)

    def gates(i):
        r = pl.ds(pl.multiple_of(i * 128, 128), 128)
        pre[r, :] = dot3(split(c[r, :]), (gate_hi[...], gate_lo[...]), ((1,), (0,)))

    loop(TOK // 128, gates)
    step(plane_a, other, plane_b, plane_c)

    def point(i, carry):
        prod_in, state = carry
        r = pl.ds(pl.multiple_of(i * 8, 8), 8)
        rr = jax.nn.sigmoid(pre[r, 0:CH] + vec[5:6, :])
        gg = jax.nn.sigmoid(pre[r, CH:] + vec[6:7, :])
        log_a = -8.0 * rr * vec[7:8, :]
        aa = jnp.exp(log_a)
        mm = jnp.sqrt(minus_expm1(2.0 * log_a))
        rate[r, :] = rr
        gin[r, :] = gg
        a[r, :] = aa
        m[r, :] = mm
        pa, hb = scan8(aa, mm * gg * c[r, :], False)
        hb = hb + pa * state
        pa = pa * prod_in
        h[r, :] = hb
        prod[r, :] = pa
        return pa[7:8, :], hb[7:8, :]

    last = (jnp.ones((1, CH), f32), jnp.zeros((1, CH), f32))
    last = lax.fori_loop(0, TOK // 16, point, last)
    step(plane_a, plane_c)
    last = lax.fori_loop(TOK // 16, TOK // 8, point, last)
    for source, target in ((rate, rate_out), (gin, gin_out), (a, a_out), (m, m_out)):
        keep(source, target)
    mine[...] = jnp.zeros((8, CH), f32)
    total[...] = jnp.zeros((8, CH), f32)
    mine[0:1, :] = last[0]
    mine[1:2, :] = last[1]
    came = line_prefix(mine, quad, rows, total, put, False)
    state_in[...] = jnp.broadcast_to(came, (8, CH))
    total_a[...] = jnp.broadcast_to(last[0], (8, CH))
    step(plane_b, plane_c)
    finish(plane_a, other)
    edge.wait_send()

    def complete(i):
        r = pl.ds(pl.multiple_of(i * 16, 16), 16)
        hh = h[r, :] + prod[r, :] * came
        h[r, :] = hh
        hy[r, :] = (hh * gelu_parts(yb[r, :])[0]).astype(bf)

    loop(TOK // 16, complete)
    keep(h, h_out)
    keep(hy, hy_out)

    def produce(at):
        part[:, z_columns(at)] = jnp.dot(
            hy[...], weights[2, :, z_columns(at)], preferred_element_type=f32
        ).astype(bf)

    whole = ring_sum(part, mix_own, came_z, sent_z, put, produce)
    step(whole, plane_b, whole, plane_c)
    finish(whole)
    mixed[:, z_columns(z)] = mix_own[...].astype(bf)
    keep(mix_own, own_out)
    spread = ring_gather(mixed, put)
    step(spread, plane_b, spread, plane_c)
    finish(spread)
    keep(mixed, mix_out)
    finish(plane_b, plane_c)
    put.drain(skip=edge)
    keep.drain()


def front(*operands):
    wide = shape((TOK, CH), f32)
    rows = shape((TOK, D), bf)
    mlp = shape((1, 1536, D), bf)
    gate = shape((CH, 2 * CH), bf)
    out = (
        rows, rows, wide, wide, wide, wide, wide, wide, wide, wide,
        shape((TOK, CH), bf), shape((TOK + 8, CH), f32), gate, gate,
        rows, shape((TOK, 512), f32), rows, shape((3, CH, D), bf), mlp, mlp, mlp,
    )
    little = (
        shape((TOK, 128), f32), shape((8, D), f32), shape((16, CH), f32),
        shape((8, CH), f32), shape((8, CH), f32),
    )
    tall = pltpu.VMEM((TOK, CH), f32)
    return pl.pallas_call(
        front_kernel,
        out_shape=out + little,
        in_specs=[VMEM] * 4 + [ANY] * 4,
        out_specs=[ANY] * len(out) + [VMEM] * len(little),
        scratch_shapes=[
            pltpu.VMEM((TOK, D), bf),
            pltpu.VMEM((TOK, D), bf),
            pltpu.VMEM((3, CH, D), bf),
            pltpu.VMEM((4, PACKED, 128), f32),
            pltpu.VMEM((4, 4, 8, 128), f32),
            tall, tall, tall, tall, tall, tall, tall, tall,
            pltpu.VMEM((TOK, CH), bf),
            pltpu.VMEM((TOK + 8, CH), f32),
            pltpu.VMEM((CH, 2 * CH), bf),
            pltpu.VMEM((CH, 2 * CH), bf),
            pltpu.VMEM((TOK, 2 * CH), f32),
            tall,
            pltpu.VMEM((TOK, D), bf),
            pltpu.VMEM((TOK, D), bf),
            pltpu.VMEM((TOK, 512), f32),
            pltpu.VMEM((16, CH), bf),
            pltpu.VMEM((8, CH), f32),
            pltpu.VMEM((4, 8, CH), f32),
            pltpu.VMEM((8, 8, CH), f32),
            pltpu.VMEM((8, CH), f32),
        ]
        + ring_scratch()
        + semaphores(18 + 9 + 11 + 12 + 4 * GATHER_COPIES)
        + [pltpu.SemaphoreType.DMA((26,))],
        compiler_params=params(0),
        name="front",
    )(*operands)


def backward_kernel(
    dhy, yb, gate_hi, gate_lo, vec, c, rate, gin, a, m, h, ext, state_in, total_a,
    mlp_part, z_own, up,
    dxb, dyb, dgate, sums, block_out, up_sum,
    e, apad, hpad, q, prod, pri, dc, halo, mine, quad, rows, total, own, low, came_z, sent_z, *rest,
):
    block = my_block()
    after, before = lax.rem(block + 1, 32), lax.rem(block + 31, 32)
    meet(
        line_devices()
        + [plane_device(after), plane_device(before)]
        + plane_neighbours()
        + z_others()
    )
    put = Sender(*rest[SUM_SCRATCH:])
    whole = ring_sum(mlp_part, own, came_z, sent_z, put)
    plane = plane_sum(up, up_sum, rest[:SUM_SCRATCH], put)
    step(whole, plane)

    def direct(i):
        r = pl.ds(pl.multiple_of(i * 16, 16), 16)
        value, slope = gelu_parts(yb[r, :])
        grad = dhy[r, :]
        hh = h[r, :]
        e[r, :] = grad * value
        dyb[r, :] = (grad * hh * slope).astype(bf)
        apad[r, :] = a[r, :]
        hpad[pl.ds(pl.multiple_of(i * 16 + 8, 8), 16), :] = hh

    loop(TOK // 16, direct)
    apad[TOK : TOK + 8, :] = jnp.ones((8, CH), f32)
    hpad[0:8, :] = state_in[...]
    step(whole)

    def adjoint(i, carry):
        prod_in, state = carry
        r0 = TOK - 8 - i * 8
        r = pl.ds(pl.multiple_of(r0, 8), 8)
        next_a = ahead(apad[pl.ds(pl.multiple_of(r0, 8), 16), :], 1)
        pa, qb = scan8(next_a, e[r, :], True)
        qb = qb + pa * state
        pa = pa * prod_in
        q[r, :] = qb
        prod[r, :] = pa
        return pa[0:1, :], qb[0:1, :]

    last = lax.fori_loop(
        0, TOK // 8, adjoint, (jnp.ones((1, CH), f32), jnp.zeros((1, CH), f32))
    )
    mine[...] = jnp.zeros((8, CH), f32)
    total[...] = jnp.zeros((8, CH), f32)
    mine[0:1, :] = total_a[0:1, :]
    mine[1:2, :] = a[0:1, :] * last[1]
    came = line_prefix(mine, quad, rows, total, put, True)
    step(plane)

    def point(i, carry):
        s_rate, s_input, s_decay = carry
        r = pl.ds(pl.multiple_of(i * 8, 8), 8)
        qq = q[r, :] + prod[r, :] * came
        aa, rr, gg, mm, cc = a[r, :], rate[r, :], gin[r, :], m[r, :], c[r, :]
        earlier = pltpu.roll(hpad[pl.ds(pl.multiple_of(i * 8, 8), 16), :], 1, 0)[8:16, :]
        grad_log = aa * (qq * earlier - qq * gg * cc * aa / mm)
        pr = -8.0 * vec[7:8, :] * grad_log * rr * (1.0 - rr)
        pi = qq * mm * cc * gg * (1.0 - gg)
        pri[r, 0:CH] = pr
        pri[r, CH:] = pi
        dc[r, :] = qq * mm * gg
        return s_rate + pr, s_input + pi, s_decay + 8.0 * rr * vec[8:9, :] * grad_log

    none = jnp.zeros((8, CH), f32)
    s_rate, s_input, s_decay = lax.fori_loop(0, TOK // 8, point, (none, none, none))
    step(plane)

    def spread(i):
        r = pl.ds(pl.multiple_of(i * 128, 128), 128)
        dc[r, :] = dc[r, :] + dot3(split(pri[r, :]), (gate_hi[...], gate_lo[...]), ((1,), (1,)))

    loop(TOK // 128, spread)
    edge = put(dc.at[pl.ds(0, 8), :], halo, plane_device(before))
    finish(whole)
    low[...] = (own[...] + z_own[...]).astype(bf)
    back = quad_scatter(low, block_out, put)
    step(plane)
    dgate[...] = dot3(split(c[...]), split(pri[...]), ((0,), (0,)))
    step(plane)
    edge.wait_recv()
    dc[TOK : TOK + 8, :] = jnp.where(block < 31, halo[...], 0.0)

    def taps(i, carry):
        r = i * 16
        here = pl.ds(pl.multiple_of(r, 16), 16)
        later = dc[pl.ds(pl.multiple_of(r, 16), 24), :]
        near = ext[pl.ds(pl.multiple_of(r, 16), 24), :]
        dd = later[0:16, :]
        out = vec[0:1, :] * dd
        for k in (1, 2, 3):
            out = out + vec[k : k + 1, :] * ahead(later, k)
        dxb[here, :] = out.astype(bf)

        def fold(v):
            return v[0:8, :] + v[8:16, :]

        new = [carry[0] + fold(dd)]
        for k in range(4):
            new.append(carry[1 + k] + fold(dd * behind(near, k)))
        return tuple(new)

    s_bias, *s_taps = lax.fori_loop(0, TOK // 16, taps, (none,) * 5)

    def place_sum(row, value):
        sums[row : row + 1, :] = jnp.sum(value, axis=0, keepdims=True)

    for k in range(4):
        place_sum(k, s_taps[k])
    place_sum(4, s_bias)
    place_sum(5, s_rate)
    place_sum(6, s_input)
    place_sum(7, s_decay)
    finish(plane)
    got(back)
    put.drain()


def backward_scan(*operands):
    r = operands[-1].shape[1]
    return pl.pallas_call(
        backward_kernel,
        out_shape=(
            shape((TOK, CH), bf),
            shape((TOK, CH), bf),
            shape((CH, 2 * CH), f32),
            shape((8, CH), f32),
            shape((4 * TOK, 128), bf),
            shape((r, 256), f32),
        ),
        in_specs=[VMEM] * 17,
        out_specs=[VMEM] * 6,
        scratch_shapes=[
            pltpu.VMEM((TOK, CH), f32),
            pltpu.VMEM((TOK + 8, CH), f32),
            pltpu.VMEM((TOK + 8, CH), f32),
            pltpu.VMEM((TOK, CH), f32),
            pltpu.VMEM((TOK, CH), f32),
            pltpu.VMEM((TOK, 2 * CH), f32),
            pltpu.VMEM((TOK + 8, CH), f32),
            pltpu.VMEM((8, CH), f32),
            pltpu.VMEM((8, CH), f32),
            pltpu.VMEM((4, 8, CH), f32),
            pltpu.VMEM((8, 8, CH), f32),
            pltpu.VMEM((8, CH), f32),
            pltpu.VMEM((TOK, 512), f32),
            pltpu.VMEM((TOK, 512), bf),
        ]
        + ring_scratch()
        + sum_scratch(r)
        + semaphores(11 + 6 + 3 + SUM_COPIES),
        compiler_params=params(4),
        name="backward_scan",
    )(*operands)


def dot(p, q):
    return jnp.dot(p, q, preferred_element_type=f32)


def dot_t0(p, q):
    return lax.dot_general(p, q, (((0,), (0,)), ((), ())), preferred_element_type=f32)


def dot_t1(p, q):
    return lax.dot_general(p, q, (((1,), (1,)), ((), ())), preferred_element_type=f32)


def per_device(
    block_in, cotangent, norm_one, rec_in, rec_gate, conv_weight, conv_bias,
    rate_weight, rate_bias, input_weight, input_bias, decay_code, rec_out,
    norm_two, mlp_gate, mlp_up, mlp_down,
):
    decay = decay_code.astype(f32) / 256.0
    vectors = jnp.concatenate(
        [
            conv_weight,
            conv_bias[None],
            rate_bias[None],
            input_bias[None],
            jax.nn.softplus(-decay)[None],
            jax.nn.sigmoid(-decay)[None],
            jnp.zeros((7, HW), f32),
        ],
        axis=0,
    )
    packed = jnp.concatenate(
        [
            pack_square(rate_weight[0]),
            pack_square(input_weight[0]),
            vectors[:, :128],
            jnp.pad(vectors[:, 128:], ((0, 0), (0, 96))),
        ],
        axis=0,
    )
    norms = jnp.concatenate([norm_one[None], norm_two[None], jnp.zeros((6, 128), f32)], axis=0)
    (
        x_full, n_one, xb, yb, c, rate, gin, a, m, h, hy, ext, gate_hi, gate_lo,
        mix_full, mix_own, cot_full, w_rec, w_gate, w_up, w_down,
        inv_one, gains, vec, state_in, total_a,
    ) = front(
        block_in, cotangent, packed, norms,
        jnp.stack([rec_in.T, rec_gate.T, rec_out]), mlp_gate.T[None], mlp_up.T[None], mlp_down[None],
    )
    w_in, w_gate_rec, w_out = w_rec[0], w_rec[1], w_rec[2]
    w_gate, w_up, w_down = w_gate[0], w_up[0], w_down[0]
    gain_one, gain_two = gains[0:1], gains[1:2]
    inv_one = inv_one[:, :1]
    x_rows = x_full.astype(f32)
    z = lax.axis_index("z")
    x_own = lax.dynamic_slice(x_full, (0, z * 512), (TOK, 512)).astype(f32)
    z_rows = x_rows + mix_full.astype(f32)
    z_own = x_own + mix_own
    inv_two = lax.rsqrt(jnp.mean(z_rows * z_rows, axis=1, keepdims=True) + EPS)
    n_two = (z_rows * inv_two * gain_two).astype(bf)

    g = dot_t1(n_two, w_gate)
    u = dot_t1(n_two, w_up)
    gelu_g, slope_g = gelu_parts(g)
    act = (gelu_g * u).astype(bf)
    dact = dot_t1(cot_full, w_down)
    dg = (dact * u * slope_g).astype(bf)
    du = (dact * gelu_g).astype(bf)
    inner_two = jnp.sum(dg.astype(f32) * g + du.astype(f32) * u, axis=1, keepdims=True)
    dn_two = dot(dg, w_gate) + dot(du, w_up)
    step_two = dn_two * inv_two * gain_two - z_rows * (inv_two * inv_two * inner_two / D)
    gain_two_sums = jnp.sum(dn_two * z_rows * inv_two, axis=0)
    part_down = dot_t0(act, cot_full).astype(bf).reshape(4, 384, D)
    part_gate = dot_t0(dg, n_two).astype(bf).reshape(4, 384, D)
    part_up = dot_t0(du, n_two).astype(bf).reshape(4, 384, D)
    back_full, back_own, grad_down, grad_gate = resid_sum(
        step_two.astype(bf), part_down, part_gate
    )
    dmix = (cot_full.astype(f32) + back_full.astype(f32)).astype(bf)
    cot_own = lax.dynamic_slice(cot_full, (0, z * 512), (TOK, 512)).astype(f32)
    dz_own = cot_own + back_own

    dhy = dot_t1(dmix, w_out)
    dxb, dyb, dgate, sums, block_out, grad_up = backward_scan(
        dhy, yb, gate_hi, gate_lo, vec, c, rate, gin, a, m, h, ext, state_in, total_a,
        dot(act, w_down).astype(bf), z_own, part_up,
    )
    inner_one = jnp.sum(dxb.astype(f32) * xb + dyb.astype(f32) * yb, axis=1, keepdims=True)
    dn_one = dot(dxb, w_in) + dot(dyb, w_gate_rec)
    step_one = dn_one * inv_one * gain_one - x_rows * (inv_one * inv_one * inner_one / D)
    gain_one_sums = jnp.sum(dn_one * x_rows * inv_one, axis=0)
    part_rec = jnp.concatenate(
        [dot_t0(p, q).astype(bf).reshape(4, HW, D) for p, q in ((dxb, n_one), (dyb, n_one), (hy, dmix))],
        axis=1,
    )
    blocks = [
        jnp.concatenate(
            [
                dgate[HW * i : HW * (i + 1), HW * i : HW * (i + 1)],
                dgate[HW * i : HW * (i + 1), CH + HW * i : CH + HW * (i + 1)],
                sums[:, HW * i : HW * (i + 1)],
                jnp.zeros((56, HW), f32),
            ],
            axis=0,
        )
        for i in range(4)
    ]
    gains = jnp.stack([gain_one_sums.reshape(4, 4, 128), gain_two_sums.reshape(4, 4, 128)], axis=2)
    gains = jnp.concatenate([gains, jnp.zeros((4, 4, 6, 128), f32)], axis=2)
    grad_in, grad_rec, small, gain_sums = last_sums(
        step_one.astype(bf), dz_own, part_rec, jnp.stack(blocks), gains
    )
    grad_rec_in, grad_rec_gate, grad_out = grad_rec[:HW].T, grad_rec[HW : 2 * HW].T, grad_rec[2 * HW :]
    vector_grads = small[2 * HW : 2 * HW + 8]
    return (
        block_out,
        grad_in.astype(f32),
        gain_sums[0],
        grad_rec_in,
        grad_rec_gate,
        vector_grads[0:4],
        vector_grads[4],
        small[:HW][None],
        vector_grads[5],
        small[HW : 2 * HW][None],
        vector_grads[6],
        vector_grads[7],
        grad_out,
        gain_sums[1],
        grad_gate.T,
        grad_up.T,
        grad_down,
    )


def solution(mesh):
    fine = Mesh(mesh.devices.reshape(2, 4, 4, 2, 2), ("ylo", "x", "z", "yhi", "core"))
    both = P(SEQ, HEAD)
    swap = P(HEAD, SEQ)
    vector = P(HEAD)
    stack = P(HEAD, None, None)
    taps = P(None, HEAD)
    return jax.shard_map(
        per_device,
        mesh=fine,
        in_specs=(
            both, both, vector, both, both, taps, vector, stack, vector, stack, vector, vector,
            swap, vector, both, both, swap,
        ),
        out_specs=(
            both, both, vector, both, both, taps, vector, stack, vector, stack, vector, vector,
            swap, vector, both, both, swap,
        ),
        check_vma=False,
    )
```

```python
import jax
import jax.numpy as jnp
from jax import lax
from jax.experimental import pallas as pl
from jax.experimental.pallas import tpu as pltpu
from jax.sharding import Mesh, PartitionSpec as P

D = 2048
CONV = 4
EPS = 1e-06
TOK = 512
CH = 640
HW = 160
TAILS = ((0, 48), (48, 48), (96, 48), (144, 16))
SQUARE = 208
PACKED = 2 * SQUARE + 32
MESH = pl.DeviceIdType.MESH
SEQ = ("ylo", "x")
HEAD = ("z", "yhi", "core")
QUAD = ("yhi", "core")
PLANE = ("ylo", "x", "yhi", "core")
bf = jnp.bfloat16
f32 = jnp.float32
VMEM = pl.BlockSpec(memory_space=pltpu.VMEM)
ANY = pl.BlockSpec(memory_space=pl.ANY)


def shape(dims, dtype):
    return jax.ShapeDtypeStruct(dims, dtype)


def params(cid):
    return pltpu.CompilerParams(
        collective_id=cid, has_side_effects=True, vmem_limit_bytes=60 * 2**20
    )


def quad_device(index):
    return {"yhi": index // 2, "core": lax.rem(index, 2)}


def plane_device(block):
    return {
        "ylo": block // 16,
        "x": lax.rem(block // 4, 4),
        "yhi": lax.rem(block // 2, 2),
        "core": lax.rem(block, 2),
    }


def meet(devices):
    barrier = pltpu.get_barrier_semaphore()
    for device in devices:
        pl.semaphore_signal(barrier, inc=1, device_id=device, device_id_type=MESH)
    pl.semaphore_wait(barrier, len(devices))


def place():
    ylo, x, yhi, core = (lax.axis_index(n) for n in ("ylo", "x", "yhi", "core"))
    return ylo, x, yhi, core

def x_device(i):
    return {"x": i}

def y_device(i):
    return {"yhi": i // 2, "ylo": lax.rem(i, 2)}

def around(i):
    return lax.rem(i + 1, 4), lax.rem(i + 3, 4), lax.rem(i + 2, 4)

def plane_neighbours():
    ylo, x, yhi, core = place()
    y = yhi * 2 + ylo
    xr, xl, _ = around(x)
    yr, yl, _ = around(y)
    return [x_device(xr), x_device(xl), y_device(yr), y_device(yl), {"core": 1 - core}]

class Sender:
    def __init__(self, send, recv, base=0):
        self.send, self.recv, self.base, self.all = send, recv, base, []

    def __call__(self, source, target, device):
        i = self.base + len(self.all)
        copy = pltpu.make_async_remote_copy(
            src_ref=source,
            dst_ref=target,
            send_sem=self.send.at[i],
            recv_sem=self.recv.at[i],
            device_id=device,
            device_id_type=MESH,
        )
        copy.start()
        self.all.append(copy)
        return copy

    def drain(self, skip=None):
        for copy in self.all:
            if copy is not skip:
                copy.wait_send()


class Keeper:
    def __init__(self, done):
        self.done, self.count, self.open = done, 0, []

    def __call__(self, source, target):
        copy = pltpu.make_async_copy(source, target, self.done.at[self.count])
        copy.start()
        self.count += 1
        self.open.append(copy)
        return copy

    def wait(self, copy):
        self.open = [c for c in self.open if c is not copy]
        copy.wait()

    def drain(self):
        for copy in self.open:
            copy.wait()


def semaphores(count):
    return [pltpu.SemaphoreType.DMA((count,)), pltpu.SemaphoreType.DMA((count,))]


def got(copies):
    for copy in copies:
        copy.wait_recv()


def step(*plans):
    for plan in plans:
        next(plan, None)


def finish(*plans):
    for plan in plans:
        for _ in plan:
            pass


def z_columns(block):
    return pl.ds(pl.multiple_of(block * 512, 512), 512)


def ring_gather(full, put):
    z = lax.axis_index("z")
    right, left, _ = around(z)
    half = full.shape[0] // 2

    def start(row, block, to):
        part = full.at[pl.ds(row, half), z_columns(block)]
        return put(part, part, {"z": to})

    c0 = start(0, z, right)
    c1 = start(half, z, left)
    c2 = start(half, z, right)
    c3 = start(0, z, left)
    yield
    c0.wait_recv()
    c4 = start(0, left, right)
    c1.wait_recv()
    c5 = start(half, right, left)
    yield
    got([c2, c3, c4, c5])


def ring_sum(part, out, came, sent, put, produce=lambda block: None):
    z = lax.axis_index("z")
    right, left, far = around(z)
    half = part.shape[0] // 2
    lo, hi = pl.ds(0, half), pl.ds(half, half)
    cols = z_columns

    def start(i, source, to):
        return put(source, came.at[i], {"z": to})

    produce(far)
    c0 = start(0, part.at[lo, cols(far)], right)
    c1 = start(1, part.at[hi, cols(far)], left)
    produce(right)
    c2 = start(2, part.at[hi, cols(right)], right)
    produce(left)
    c3 = start(3, part.at[lo, cols(left)], left)
    produce(z)
    yield
    c0.wait_recv()
    sent[0] = came[0] + part[lo, cols(right)]
    c4 = start(4, sent.at[0], right)
    c1.wait_recv()
    sent[1] = came[1] + part[hi, cols(left)]
    c5 = start(5, sent.at[1], left)
    yield
    got([c3, c4])
    out[lo, :] = part[lo, cols(z)].astype(f32) + came[3].astype(f32) + came[4].astype(f32)
    got([c2, c5])
    out[hi, :] = part[hi, cols(z)].astype(f32) + came[2].astype(f32) + came[5].astype(f32)


def ring_scratch():
    return [pltpu.VMEM((6, TOK // 2, 512), bf), pltpu.VMEM((2, TOK // 2, 512), bf)]


def z_others():
    z = lax.axis_index("z")
    return [{"z": lax.rem(z + j, 4)} for j in (1, 2, 3)]


def quad_others():
    me = lax.axis_index("yhi") * 2 + lax.axis_index("core")
    return [quad_device(lax.rem(me + j, 4)) for j in (1, 2, 3)]


def quad_gather(tokens, full, put, keep):
    z = lax.axis_index("z")
    me = lax.axis_index("yhi") * 2 + lax.axis_index("core")
    mine = pl.ds(pl.multiple_of(z * 512 + me * 128, 128), 128)
    copies = []
    for j in (1, 2, 3):
        peer = lax.rem(me + j, 4)
        source = tokens.at[pl.ds(pl.multiple_of(peer * TOK, TOK), TOK), :]
        copies.append(put(source, full.at[:, mine], quad_device(peer)))
    own = keep(tokens.at[pl.ds(pl.multiple_of(me * TOK, TOK), TOK), :], full.at[:, mine])
    return copies, own


def token_gather(tokens, full, put, keep):
    copies, own = quad_gather(tokens, full, put, keep)
    yield
    got(copies)
    keep.wait(own)
    yield from ring_gather(full, put)


def quad_scatter(own, tokens, put, keep):
    me = lax.axis_index("yhi") * 2 + lax.axis_index("core")
    rows = pl.ds(pl.multiple_of(me * TOK, TOK), TOK)
    copies = []
    for j in (1, 2, 3):
        peer = lax.rem(me + j, 4)
        source = own.at[:, pl.ds(pl.multiple_of(peer * 128, 128), 128)]
        copies.append(put(source, tokens.at[rows, :], quad_device(peer)))
    mine = keep(own.at[:, pl.ds(pl.multiple_of(me * 128, 128), 128)], tokens.at[rows, :])
    return copies, mine


GATHER_COPIES = 48
SUM_COPIES = 36
SUM_KEEPS = 8


HALF = TOK // 2
UNIT = 256


def middle_kernel(
    hy_in, rec_in, x_in, cot_in, gate_in, up_in, own_down, gains,
    zown_out, dz_out, dmix_out, mlp_out, down_grad, gate_grad, up_grad, gain_sums,
    hy, w_out, x, cot, w_gate, w_up, w_down, normed, mixed, part, part_two, back, act, dg, du, mlp,
    own_one, own_two, inv, inner, *rest,
):
    rings, (send, recv, done) = rest[:8], rest[8:]
    z = lax.axis_index("z")
    keep = Keeper(done)
    load_mix = [keep(hy_in, hy), keep(rec_in.at[2], w_out)]
    load_norm = [keep(x_in, x)]
    load_mlp = [keep(gate_in, w_gate), keep(up_in, w_up), keep(cot_in, cot)]
    meet(z_others() + plane_neighbours())
    put = Sender(send, recv)
    plane = plane_gather(own_down, w_down, put, keep)
    step(plane)
    puts = [Sender(send, recv, GATHER_COPIES + 12 * i) for i in range(4)]

    def rows_of(half):
        return pl.ds(HALF * half, HALF)

    def view(ref, half):
        return ref.at[rows_of(half), :]

    def wide(ref, rows, times):
        return jnp.concatenate([ref[rows, :]] * times, axis=1)

    def mix_block(half):
        def produce(at):
            part[rows_of(half), z_columns(at)] = jnp.dot(
                hy[rows_of(half), :], w_out[:, z_columns(at)], preferred_element_type=f32
            ).astype(bf)

        return produce

    def sums(i, half, source, own, produce):
        return ring_sum(
            view(source, half), view(own, half), rings[2 * i], rings[2 * i + 1], puts[i], produce
        )

    def spread(i, half, full, own):
        full[rows_of(half), z_columns(z)] = own[rows_of(half), :].astype(bf)
        return ring_gather(view(full, half), puts[i])

    def norm(half):
        def body(i):
            r = pl.ds(pl.multiple_of(HALF * half + i * 16, 16), 16)
            values = x[r, :].astype(f32) + mixed[r, :].astype(f32)
            mean = jnp.sum(values * values, axis=1, keepdims=True) * (1.0 / D)
            scale = lax.rsqrt(mean + EPS)
            inv[r, :] = jnp.broadcast_to(scale, (16, 128))
            normed[r, :] = (values * scale * gains[1:2, :]).astype(bf)

        loop(HALF // 16, body)

    def hidden(half, first, count):
        r = rows_of(half)

        def body(j):
            at = pl.ds(pl.multiple_of((first + j) * UNIT, UNIT), UNIT)

            def against(left, right):
                return lax.dot_general(
                    left, right[at, :], (((1,), (1,)), ((), ())), preferred_element_type=f32
                )

            g = against(normed[r, :], w_gate)
            u = against(normed[r, :], w_up)
            da = against(cot[r, :], w_down)
            value, slope = gelu_parts(g)
            act[r, at] = (value * u).astype(bf)
            low_g = (da * u * slope).astype(bf)
            low_u = (da * value).astype(bf)
            dg[r, at] = low_g
            du[r, at] = low_u
            t = low_g.astype(f32) * g + low_u.astype(f32) * u
            inner[r, :] = inner[r, :] + (t[:, :128] + t[:, 128:])

        loop(count, body)

    def close(half):
        r = rows_of(half)
        total = jnp.sum(inner[r, :], axis=1, keepdims=True) * (1.0 / D)
        inner[r, :] = inv[r, :] * inv[r, :] * total

    def back_block(half):
        r = rows_of(half)

        def produce(at):
            cols = z_columns(at)
            dn = jnp.dot(dg[r, :], w_gate[:, cols], preferred_element_type=f32)
            dn = dn + jnp.dot(du[r, :], w_up[:, cols], preferred_element_type=f32)
            values = x[r, cols].astype(f32) + mixed[r, cols].astype(f32)
            scaled = dn * wide(inv, r, 4)
            part_two[r, cols] = (scaled * gains[1:2, cols] - values * wide(inner, r, 4)).astype(bf)
            gain_sums[:, cols] = gain_sums[:, cols] + jnp.sum(
                (scaled * values).reshape(HALF // 8, 8, 512), axis=0
            )

        return produce

    def mlp_blocks():
        for at in range(4):
            cols = slice(512 * at, 512 * at + 512)
            mlp[:, cols] = jnp.dot(act[...], w_down[:, cols], preferred_element_type=f32).astype(bf)

    def weight_grad(left, right, into, target):
        def body(j):
            at = pl.ds(pl.multiple_of(j * UNIT, UNIT), UNIT)
            for k in range(4):
                cols = slice(512 * k, 512 * k + 512)
                into[at, cols] = lax.dot_general(
                    left[:, at], right[:, cols], (((0,), (0,)), ((), ())), preferred_element_type=f32
                ).astype(bf)

        loop(1536 // UNIT, body)
        keep(into, target)

    def add_own(half, whole, own):
        r = rows_of(half)
        own[r, :] = own[r, :] + whole[r, z_columns(z)].astype(f32)

    def add_cotangent(half):
        def body(i):
            r = pl.ds(pl.multiple_of(HALF * half + i * 16, 16), 16)
            back[r, :] = cot[r, :] + back[r, :]

        loop(HALF // 16, body)

    for copy in load_mix:
        keep.wait(copy)
    inner[...] = jnp.zeros((TOK, 128), f32)
    gain_sums[...] = jnp.zeros((8, D), f32)
    sum_a = sums(0, 0, part, own_one, mix_block(0))
    sum_b = sums(1, 1, part, own_one, mix_block(1))
    step(sum_a, sum_a)
    step(plane, sum_b)
    finish(sum_a)
    spread_a = spread(0, 0, mixed, own_one)
    step(spread_a, sum_b, plane, spread_a)
    finish(sum_b)
    spread_b = spread(1, 1, mixed, own_one)
    step(spread_b)
    finish(spread_a)
    for copy in load_norm:
        keep.wait(copy)
    add_own(0, x, own_one)
    norm(0)
    step(spread_b, plane)
    for copy in load_mlp:
        keep.wait(copy)
    finish(plane)
    hidden(0, 0, 3)
    finish(spread_b)
    add_own(1, x, own_one)
    keep(own_one, zown_out)
    hidden(0, 3, 3)
    close(0)
    total_a = sums(2, 0, part_two, own_two, back_block(0))
    step(total_a)
    norm(1)
    step(total_a)
    hidden(1, 0, 3)
    finish(total_a)
    back_a = spread(2, 0, back, own_two)
    step(back_a)
    hidden(1, 3, 2)
    step(back_a)
    hidden(1, 5, 1)
    close(1)
    total_b = sums(3, 1, part_two, own_two, back_block(1))
    step(total_b)
    finish(back_a)
    puts[2].drain()
    add_cotangent(0)
    add_own(0, cot, own_two)
    step(total_b)
    mlp_blocks()
    keep(mlp, mlp_out)
    put.drain()
    finish(total_b)
    back_b = spread(3, 1, back, own_two)
    step(back_b)
    weight_grad(act, cot, w_down, down_grad)
    step(back_b)
    weight_grad(dg, normed, w_gate, gate_grad)
    finish(back_b)
    puts[3].drain()
    add_cotangent(1)
    keep(back, dmix_out)
    add_own(1, cot, own_two)
    keep(own_two, dz_out)
    weight_grad(du, normed, w_up, up_grad)
    puts[0].drain()
    puts[1].drain()
    keep.drain()


def middle(*operands):
    mlp = shape((1536, D), bf)
    rows = shape((TOK, D), bf)
    own = shape((TOK, 512), f32)
    row_scratch = pltpu.VMEM((TOK, D), bf)
    weight = pltpu.VMEM((1536, D), bf)
    unit = pltpu.VMEM((TOK, 1536), bf)
    return pl.pallas_call(
        middle_kernel,
        out_shape=(own, own, rows, rows, mlp, mlp, mlp, shape((8, D), f32)),
        in_specs=[ANY] * 7 + [VMEM],
        out_specs=[ANY] * 7 + [VMEM],
        scratch_shapes=[
            pltpu.VMEM((TOK, CH), bf),
            pltpu.VMEM((CH, D), bf),
            row_scratch,
            row_scratch,
            weight,
            weight,
            weight,
            row_scratch,
            row_scratch,
            row_scratch,
            row_scratch,
            row_scratch,
            unit,
            unit,
            unit,
            row_scratch,
            pltpu.VMEM((TOK, 512), f32),
            pltpu.VMEM((TOK, 512), f32),
            pltpu.VMEM((TOK, 128), f32),
            pltpu.VMEM((TOK, 128), f32),
        ]
        + 4 * [pltpu.VMEM((6, HALF // 2, 512), bf), pltpu.VMEM((2, HALF // 2, 512), bf)]
        + semaphores(GATHER_COPIES + 48)
        + [pltpu.SemaphoreType.DMA((16,))],
        compiler_params=params(3),
        name="middle",
    )(*operands)


def cut(r):
    a = (r // 32) * 16
    a1 = ((a // 16 + 1) // 2) * 16
    b1 = (((r - a) // 16 + 1) // 2) * 16
    return a, a1, b1

def plane_gather(own, full, put, keep):
    r = own.shape[-2]
    lead = (slice(None),) * (len(own.shape) - 2)
    ylo, x, yhi, core = place()
    y = yhi * 2 + ylo
    xr, xl, xf = around(x)
    yr, yl, yf = around(y)
    a, a1, b1 = cut(r)
    top, bottom = (0, a), (a, r - a)
    top1, top2 = (0, a1), (a1, a - a1)
    bot1, bot2 = (a, b1), (a + b1, r - a - b1)

    def span(quarter, rows):
        return pl.ds(pl.multiple_of(quarter * r + rows[0], 16), rows[1])

    sib = {"core": 1 - core}
    def cols(lo, xx):
        return pl.ds(pl.multiple_of(lo * 1024 + xx * 256, 256), 256)
    def one(rows, yy, xx):
        return full.at[lead + (span((yy // 2) * 2 + core, rows), cols(lax.rem(yy, 2), xx))]
    def row(rows, yy):
        return full.at[lead + (span((yy // 2) * 2 + core, rows), pl.ds(pl.multiple_of(lax.rem(yy, 2) * 1024, 1024), 1024))]
    kept = keep(own, one((0, r), y, x))
    ha, hb = own.at[lead + (pl.ds(*top),)], own.at[lead + (pl.ds(*bottom),)]
    p = [put(ha, one(top, y, x), x_device(xr)), put(ha, one(top, y, x), x_device(xl)),
         put(hb, one(bottom, y, x), y_device(yr)), put(hb, one(bottom, y, x), y_device(yl))]
    yield
    got(p)
    keep.wait(kept)
    p = [put(one(top1, y, xl), one(top1, y, xl), x_device(xr)), put(one(top2, y, xr), one(top2, y, xr), x_device(xl)),
         put(one(bot1, yl, x), one(bot1, yl, x), y_device(yr)), put(one(bot2, yr, x), one(bot2, yr, x), y_device(yl))]
    yield
    got(p)
    def pieces(rows, xx):
        out = []
        for lo in (0, 1):
            for hi in (0, 1):
                out.append(full.at[lead + (span(2 * hi + core, rows), cols(lo, xx))])
        return out
    def send_row(rows, yy, device):
        return [put(row(rows, yy), row(rows, yy), device)]
    def send_col(rows, xx, device):
        return [put(s, s, device) for s in pieces(rows, xx)]
    p = send_row(top, y, y_device(yr)) + send_row(top, y, y_device(yl))
    p += send_col(bottom, x, x_device(xr)) + send_col(bottom, x, x_device(xl))
    s = send_row(top, y, sib) + send_col(bottom, x, sib)
    yield
    got(p)
    p = send_row(top1, yl, y_device(yr)) + send_row(top2, yr, y_device(yl))
    p += send_col(bot1, xl, x_device(xr)) + send_col(bot2, xr, x_device(xl))
    s += send_row(top, yl, sib) + send_row(top, yr, sib) + send_col(bottom, xl, sib) + send_col(bottom, xr, sib)
    yield
    got(p)
    s += send_row(top, yf, sib) + send_col(bottom, xf, sib)
    yield
    got(s)


def plane_sum(parts, out, scratch, put, keep):
    own, fold, ga, gb, ha, hb, sa, sb, ra2, rb2 = scratch
    r = fold.shape[1]
    ylo, x, yhi, core = place()
    y = yhi * 2 + ylo
    xr, xl, xf = around(x)
    yr, yl, yf = around(y)
    a = -(-r // 64) * 32
    h, g = a // 2, (r - a) // 2
    sib = {"core": 1 - core}
    pieces = ([], [])
    at = 0
    for part in parts:
        size = part.shape[1]
        middle = min(max(a - at, 0), size)
        for group, first, count in ((0, 0, middle), (1, middle, size - middle)):
            if count:
                pieces[group].append((part, first, count, at + first))
        at += size
    came = ([], [])
    held = ([], [])
    for group in (0, 1):
        for part, first, count, to in pieces[group]:
            for hi in (0, 1):
                rows, into = pl.ds(first, count), pl.ds(to, count)
                came[group].append(put(part.at[2 * hi + 1 - core, rows, :], fold.at[hi, into, :], sib))
                held[group].append(keep(part.at[2 * hi + core, rows, :], own.at[hi, into, :]))
    yield

    def add_cores(group):
        got(came[group])
        for copy in held[group]:
            keep.wait(copy)
        first, count = ((0, a), (a, r - a))[group]
        for hi in (0, 1):

            def body(i, carry, hi=hi):
                rr = pl.ds(pl.multiple_of(first + i * 16, 16), 16)
                fold[hi, rr, :] = fold[hi, rr, :] + own[hi, rr, :]
                return carry

            lax.fori_loop(0, count // 16, body, 0)

    def ycols(yy):
        return pl.ds(pl.multiple_of(lax.rem(yy, 2) * 1024, 1024), 1024)
    def a_block(yy, first):
        return fold.at[yy // 2, pl.ds(0 if first else h, h), ycols(yy)]
    def b_block(xx, first, l):
        return fold.at[:, pl.ds(a + (0 if first else g), g), pl.ds(pl.multiple_of(l * 1024 + xx * 256, 256), 256)]
    yR, yL, xR, xL = y_device(yr), y_device(yl), x_device(xr), x_device(xl)
    def sendb(i, xx, first, dev):
        return [put(b_block(xx, first, l), gb.at[i, l], dev) for l in (0, 1)]
    add_cores(0)
    pa = [put(a_block(yf, True), ga.at[0], yR), put(a_block(yf, False), ga.at[1], yL)]
    pa += [put(a_block(yr, False), ga.at[2], yR), put(a_block(yl, True), ga.at[3], yL)]
    add_cores(1)
    pb = [sendb(0, xf, True, xR), sendb(1, xf, False, xL)]
    pb += [sendb(2, xr, False, xR), sendb(3, xl, True, xL)]
    yield

    def add_a(dst, i, block, n):
        def body(j, carry):
            rr = pl.ds(pl.multiple_of(j * 16, 16), 16)
            dst[rr, :] = ga[i, rr, :] + block[rr, :]
            return carry
        lax.fori_loop(0, n // 16, body, 0)
    def add_b(dst, i, xx, first):
        for l in (0, 1):
            for hi in (0, 1):
                block = fold.at[hi, pl.ds(a + (0 if first else g), g), pl.ds(pl.multiple_of(l * 1024 + xx * 256, 256), 256)]
                def body(j, carry):
                    rr = pl.ds(pl.multiple_of(j * 16, 16), 16)
                    dst[l, hi, rr, :] = gb[i, l, hi, rr, :] + block[rr, :]
                    return carry
                lax.fori_loop(0, g // 16, body, 0)
    pa[0].wait_recv()
    add_a(sa.at[0], 0, a_block(yr, True), h)
    pa.append(put(sa.at[0], ga.at[4], yR))
    got(pb[0])
    add_b(sb.at[0], 0, xr, True)
    pb.append([put(sb.at[0], gb.at[4], xR)])
    pa[1].wait_recv()
    add_a(sa.at[1], 1, a_block(yl, False), h)
    pa.append(put(sa.at[1], ga.at[5], yL))
    got(pb[1])
    add_b(sb.at[1], 1, xl, False)
    pb.append([put(sb.at[1], gb.at[5], xL)])
    yield
    def fin_a(first, i, j):
        def body(n, carry):
            rr = pl.ds(pl.multiple_of(n * 16, 16), 16)
            block = a_block(y, first)
            ra2[pl.ds(pl.multiple_of((0 if first else h) + n * 16, 16), 16), :] = (
                block[rr, :].astype(f32) + ga[i, rr, :].astype(f32) + ga[j, rr, :].astype(f32)).astype(bf)
            return carry
        lax.fori_loop(0, h // 16, body, 0)
    def fin_b(first, i, j):
        for l in (0, 1):
            for hi in (0, 1):
                block = fold.at[hi, pl.ds(a + (0 if first else g), g), pl.ds(pl.multiple_of(l * 1024 + x * 256, 256), 256)]
                def body(n, carry):
                    rr = pl.ds(pl.multiple_of(n * 16, 16), 16)
                    rb2[l, hi, pl.ds(pl.multiple_of((0 if first else g) + n * 16, 16), 16), :] = (
                        block[rr, :].astype(f32) + gb[i, l, hi, rr, :].astype(f32) + gb[j, l, hi, rr, :].astype(f32)).astype(bf)
                    return carry
                lax.fori_loop(0, g // 16, body, 0)
    got([pa[3], pa[4]])
    fin_a(True, 3, 4)
    got([pa[2], pa[5]])
    fin_a(False, 2, 5)
    got(pb[3] + pb[4])
    fin_b(True, 3, 4)
    got(pb[2] + pb[5])
    fin_b(False, 2, 5)
    def a2(xx, first):
        return ra2.at[pl.ds(0 if first else h, h), pl.ds(pl.multiple_of(xx * 256, 256), 256)]
    def b2(yy, first):
        return rb2.at[lax.rem(yy, 2), yy // 2, pl.ds(0 if first else g, g), :]
    qa = [put(a2(xf, True), ha.at[0], xR), put(a2(xf, False), ha.at[1], xL), put(a2(xr, False), ha.at[2], xR), put(a2(xl, True), ha.at[3], xL)]
    qb = [put(b2(yf, True), hb.at[0], yR), put(b2(yf, False), hb.at[1], yL), put(b2(yr, False), hb.at[2], yR), put(b2(yl, True), hb.at[3], yL)]
    yield
    sa2, sb2 = ha.at[pl.ds(6, 2)], hb.at[pl.ds(6, 2)]
    qa[0].wait_recv()
    sa2[0] = ha[0] + a2(xr, True)[...]
    qa.append(put(sa2.at[0], ha.at[4], xR))
    qb[0].wait_recv()
    sb2[0] = hb[0] + b2(yr, True)[...]
    qb.append(put(sb2.at[0], hb.at[4], yR))
    qa[1].wait_recv()
    sa2[1] = ha[1] + a2(xl, False)[...]
    qa.append(put(sa2.at[1], ha.at[5], xL))
    qb[1].wait_recv()
    sb2[1] = hb[1] + b2(yl, False)[...]
    qb.append(put(sb2.at[1], hb.at[5], yL))
    yield
    got(qa[2:] + qb[2:])
    def w(v): return v.astype(f32)
    out[0:h, :] = w(a2(x, True)[...]) + w(ha[3]) + w(ha[4])
    out[h:a, :] = w(a2(x, False)[...]) + w(ha[2]) + w(ha[5])
    out[a:a + g, :] = w(b2(y, True)[...]) + w(hb[3]) + w(hb[4])
    out[a + g:, :] = w(b2(y, False)[...]) + w(hb[2]) + w(hb[5])


SUM_SCRATCH = 10


def sum_scratch(r):
    a = -(-r // 64) * 32
    h, g = a // 2, (r - a) // 2
    V = pltpu.VMEM
    return [V((2, r, 2048), bf), V((2, r, 2048), bf), V((6, h, 1024), bf), V((6, 2, 2, g, 256), bf), V((8, h, 256), bf), V((8, g, 256), bf),
            V((2, h, 1024), bf), V((2, 2, 2, g, 256), bf), V((a, 1024), bf), V((2, 2, r - a, 256), bf)]


def small_sums(blocks, gains, small, gain, scratch, put):
    zgot, sgot, pair, pgot, qgain, rgot, rgain, mine = scratch
    z = lax.axis_index("z")
    yhi, core = lax.axis_index("yhi"), lax.axis_index("core")
    me = yhi * 2 + core
    row = lax.axis_index("ylo") * 4 + lax.axis_index("x")
    zs = []
    near = [put(blocks.at[2 * hi + 1 - core], sgot.at[hi], {"core": 1 - core}) for hi in (0, 1)]
    for j in (1, 2, 3):
        to = lax.rem(z + j, 4)
        zs.append(put(gains.at[to], zgot.at[j - 1], {"z": to}))
    yield
    got(near)
    for hi in (0, 1):
        pair[hi] = blocks[2 * hi + core] + sgot[hi]
    across = put(pair.at[1 - yhi], pgot, {"yhi": 1 - yhi})
    got(zs)
    qgain[3] = gains[z] + zgot[0] + zgot[1] + zgot[2]
    qs = []
    for j in (1, 2, 3):
        to = lax.rem(me + j, 4)
        qs.append(put(qgain.at[3, to], qgain.at[j - 1, 0], quad_device(to)))
    yield
    got(qs)
    across.wait_recv()
    mine[...] = pair[yhi] + pgot[...]
    rgain[7] = qgain[3, me] + qgain[0, 0] + qgain[1, 0] + qgain[2, 0]
    rs = []
    size = PACKED // 8

    def seq(j):
        to = lax.rem(row + j, 8)
        return to, {"ylo": to // 4, "x": lax.rem(to, 4)}

    for j in range(1, 8):
        to, device = seq(j)
        rs.append(put(mine.at[pl.ds(pl.multiple_of(to * size, 8), size), :], rgot.at[j - 1], device))
        rs.append(put(rgain.at[7], rgain.at[j - 1], device))
    yield
    got(rs)
    own = pl.ds(pl.multiple_of(row * size, 8), size)
    total = mine[own, :]
    gain_total = rgain[7]
    for j in range(7):
        total = total + rgot[j]
        gain_total = gain_total + rgain[j]
    small[own, :] = total
    gain[...] = gain_total
    ag = []
    for j in range(1, 8):
        _, device = seq(j)
        ag.append(put(small.at[own, :], small.at[own, :], device))
    yield
    got(ag)


SMALL_SCRATCH = 8
SMALL_COPIES = 30


def small_scratch():
    return [
        pltpu.VMEM((3, 4, 8, 128), f32),
        pltpu.VMEM((2, PACKED, 128), f32),
        pltpu.VMEM((2, PACKED, 128), f32),
        pltpu.VMEM((PACKED, 128), f32),
        pltpu.VMEM((4, 4, 8, 128), f32),
        pltpu.VMEM((7, PACKED // 8, 128), f32),
        pltpu.VMEM((8, 8, 128), f32),
        pltpu.VMEM((PACKED, 128), f32),
    ]


def last_kernel(
    part, dz, rec_in, rec_gate, rec_out, up, blocks, gains,
    grad_in, rec_sum, up_sum, small, gain,
    own, low, *rest,
):
    meet(z_others() + plane_neighbours() + line_devices())
    (came, sent), rest = rest[:2], rest[2:]
    plane_refs, rest = rest[:SUM_SCRATCH], rest[SUM_SCRATCH:]
    up_refs, rest = rest[:SUM_SCRATCH], rest[SUM_SCRATCH:]
    small_refs, rest = rest[:SMALL_SCRATCH], rest[SMALL_SCRATCH:]
    send, recv, done = rest
    put = Sender(send, recv)
    keep = Keeper(done)
    total = ring_sum(part, own, came, sent, put)
    little = small_sums(blocks, gains, small, gain, small_refs, put)
    plane = plane_sum([rec_in, rec_gate, rec_out], rec_sum, plane_refs, put, keep)
    plane_up = plane_sum([up], up_sum, up_refs, put, keep)
    step(total, little, plane_up, plane)
    step(little, plane_up, total, plane, little, plane_up)
    finish(total)
    low[...] = (own[...] + dz[...]).astype(bf)
    back, mine = quad_scatter(low, grad_in, put, keep)
    step(plane, plane_up, little, plane, plane_up)
    finish(little, plane_up, plane)
    got(back)
    keep.wait(mine)
    put.drain()
    keep.drain()


def last_sums(*operands):
    return pl.pallas_call(
        last_kernel,
        out_shape=(
            shape((4 * TOK, 128), bf),
            shape((3 * HW, 256), f32),
            shape((384, 256), f32),
            shape((PACKED, 128), f32),
            shape((8, 128), f32),
        ),
        in_specs=[VMEM] * 2 + [ANY] * 4 + [VMEM] * 2,
        out_specs=[VMEM] * 5,
        scratch_shapes=[pltpu.VMEM((TOK, 512), f32), pltpu.VMEM((TOK, 512), bf)]
        + ring_scratch()
        + sum_scratch(3 * HW)
        + sum_scratch(384)
        + small_scratch()
        + semaphores(6 + 3 + 2 * SUM_COPIES + SMALL_COPIES)
        + [pltpu.SemaphoreType.DMA((2 * SUM_KEEPS + 1,))],
        compiler_params=params(5),
        name="last_sums",
    )(*operands)


def line_devices():
    ylo, x = lax.axis_index("ylo"), lax.axis_index("x")
    row = ylo * 4 + x
    rows = [
        {"ylo": lax.rem(row + j, 8) // 4, "x": lax.rem(row + j, 4)} for j in range(1, 8)
    ]
    return quad_others() + rows


def my_block():
    row = lax.axis_index("ylo") * 4 + lax.axis_index("x")
    return row * 4 + lax.axis_index("yhi") * 2 + lax.axis_index("core")


def line_prefix(mine, quad, rows, total, put, backward):
    me = lax.axis_index("yhi") * 2 + lax.axis_index("core")
    row = lax.axis_index("ylo") * 4 + lax.axis_index("x")
    copies = []
    for j in (1, 2, 3):
        copies.append(put(mine, quad.at[me], quad_device(lax.rem(me + j, 4))))
    quad[me] = mine[...]
    got(copies)
    ones = jnp.ones((1, CH), f32)
    zeros = jnp.zeros((1, CH), f32)
    prod, end, prod_all, end_all = ones, zeros, ones, zeros
    for turn in range(4):
        q = 3 - turn if backward else turn
        a, b = quad[q, 0:1, :], quad[q, 1:2, :]
        end_all = a * end_all + b
        prod_all = a * prod_all
        take = (q > me) if backward else (q < me)
        end = jnp.where(take, a * end + b, end)
        prod = jnp.where(take, a * prod, prod)
    total[0:1, :] = prod_all
    total[1:2, :] = end_all
    copies = []
    for j in range(1, 8):
        other = lax.rem(row + j, 8)
        copies.append(put(total, rows.at[row], {"ylo": other // 4, "x": lax.rem(other, 4)}))
    rows[row] = total[...]
    got(copies)
    came = zeros
    for turn in range(8):
        r = 7 - turn if backward else turn
        a, b = rows[r, 0:1, :], rows[r, 1:2, :]
        take = (r > row) if backward else (r < row)
        came = jnp.where(take, a * came + b, came)
    return prod * came + end


def pack_square(weight):
    tail = jnp.pad(weight[:, 128:], ((0, 32), (0, 0))).reshape(4, 48, 32)
    return jnp.concatenate([weight[:, :128], tail.transpose(1, 0, 2).reshape(48, 128)], axis=0)


def unpack_square(packed):
    tail = packed[160:208].reshape(48, 4, 32).transpose(1, 0, 2).reshape(192, 32)[:HW]
    return jnp.concatenate([packed[:HW], tail], axis=1)


def split(values):
    high = values.astype(bf)
    return high, (values - high.astype(f32)).astype(bf)


def dot3(a, b, dims):
    (ah, al), (bh, bl) = a, b

    def one(p, q):
        return lax.dot_general(p, q, (dims, ((), ())), preferred_element_type=f32)

    return one(ah, bh) + (one(al, bh) + one(ah, bl))


def minus_expm1(v):
    near = -v * (
        1.0
        + v * (1 / 2) * (1.0 + v * (1 / 3) * (1.0 + v * (1 / 4) * (1.0 + v * (1 / 5) * (1.0 + v * (1 / 6)))))
    )
    return jnp.where(v > -0.3, near, 1.0 - jnp.exp(v))


def gelu_parts(v):
    cdf = 0.5 * (1.0 + lax.erf(v * 0.7071067811865476))
    pdf = 0.3989422804014327 * jnp.exp(-0.5 * v * v)
    return v * cdf, cdf + v * pdf


def shifted(values, by, fill, reverse):
    rows = lax.broadcasted_iota(jnp.int32, values.shape, 0)
    size = values.shape[0]
    if reverse:
        return jnp.where(rows < size - by, pltpu.roll(values, size - by, 0), fill)
    return jnp.where(rows >= by, pltpu.roll(values, by, 0), fill)


def behind(near, by):
    return near[8:24, :] if by == 0 else pltpu.roll(near, by, 0)[8:24, :]


def ahead(near, by):
    size = near.shape[0]
    return pltpu.roll(near, size - by, 0)[0 : size - 8, :]


def scan8(a, b, reverse):
    for by in (1, 2, 4):
        b = b + a * shifted(b, by, 0.0, reverse)
        a = a * shifted(a, by, 1.0, reverse)
    return a, b


def loop(count, body):
    def one(i, carry):
        body(i)
        return carry

    lax.fori_loop(0, count, one, 0)


def front_kernel(
    tokens, cotangent, packed, norms, own_rec, own_gate, own_up,
    x_out, n_out, xb_out, yb_out, c_out, rate_out, gin_out, a_out, m_out, h_out, hy_out, ext_out, hi_out, lo_out,
    cot, rec_out, w_gate, w_up,
    inv, gains, vec, state_in, total_a,
    full, normed, weights, params_all, norms_all,
    xb, yb, c, rate, gin, a, m, h, hy, ext, gate_hi, gate_lo, pre, prod,
    halo, mine, quad, rows, total, send, recv, done,
):
    z = lax.axis_index("z")
    me = lax.axis_index("yhi") * 2 + lax.axis_index("core")
    block = my_block()
    after, before = lax.rem(block + 1, 32), lax.rem(block + 31, 32)
    meet(
        line_devices()
        + [plane_device(after), plane_device(before)]
        + plane_neighbours()
        + z_others()
    )
    put = Sender(send, recv)
    keep = Keeper(done)
    params_all[me] = packed[...]
    tokens_in = token_gather(tokens, full, put, keep)
    plane = plane_gather(own_rec, weights, put, keep)
    step(tokens_in, plane)
    small = []
    for j in (1, 2, 3):
        small.append(put(norms, norms_all.at[z, me], quad_device(lax.rem(me + j, 4))))
    norms_all[z, me] = norms[...]
    gate_hi[...] = jnp.zeros((CH, 2 * CH), bf)
    gate_lo[...] = jnp.zeros((CH, 2 * CH), bf)
    step(plane, tokens_in)
    got(small)
    small = []
    for j in (1, 2, 3):
        small.append(put(norms_all.at[z], norms_all.at[z], {"z": lax.rem(z + j, 4)}))
    step(plane, tokens_in)
    got(small)
    for i in range(4):
        for j in range(4):
            gains[:, 128 * (4 * i + j) : 128 * (4 * i + j + 1)] = norms_all[i, j]
    step(plane)
    finish(tokens_in)
    keep(full, x_out)
    other = token_gather(cotangent, cot, put, keep)
    plane_a = plane_gather(own_gate, w_gate, put, keep)
    plane_b = plane_gather(own_up, w_up, put, keep)
    core, yhi = lax.axis_index("core"), lax.axis_index("yhi")
    own_params = params_all.at[me]
    near = put(own_params, own_params, {"core": 1 - core})
    across = put(own_params, own_params, {"yhi": 1 - yhi})
    step(plane, other, plane_a)

    def norm(i):
        r = pl.ds(pl.multiple_of(i * 16, 16), 16)
        values = full[r, :].astype(f32)
        mean = jnp.sum(values * values, axis=1, keepdims=True) * (1.0 / D)
        scale = lax.rsqrt(mean + EPS)
        inv[r, :] = jnp.broadcast_to(scale, (16, 128))
        normed[r, :] = (values * scale * gains[0:1, :]).astype(bf)

    loop(TOK // 16, norm)
    keep(normed, n_out)
    finish(plane)
    keep(weights, rec_out)
    across.wait_recv()
    peer_params = params_all.at[lax.rem(me + 2, 4)]
    passed = put(peer_params, peer_params, {"core": 1 - core})
    step(plane_a, other)
    for i, into in ((0, xb), (1, yb)):
        for at, width in ((0, 256), (256, 256), (512, 128)):
            into[:, at : at + width] = lax.dot_general(
                normed[...],
                weights[i, at : at + width, :],
                (((1,), (1,)), ((), ())),
                preferred_element_type=f32,
            )
        if i == 0:
            halo_out = pl.ds(TOK - 16, 16)
            hy[halo_out, :] = xb[halo_out, :].astype(bf)
            edge = put(hy.at[halo_out, :], halo, plane_device(after))
            step(plane_a, plane_b)
    keep(xb, xb_out)
    keep(yb, yb_out)
    step(other)

    def widen(i):
        r = pl.multiple_of(i * 16, 16)
        ext[pl.ds(pl.multiple_of(8 + r, 8), 16), :] = xb[pl.ds(r, 16), :].astype(bf).astype(f32)

    loop(TOK // 16, widen)
    got([near, passed])
    for i in range(4):
        there = HW * i
        vec[:, there : there + 128] = params_all[i, 2 * SQUARE : 2 * SQUARE + 16, :]
        vec[:, there + 128 : there + HW] = params_all[i, 2 * SQUARE + 16 : PACKED, 0:32]
        for k in (0, 1):
            top = SQUARE * k
            high, low = split(params_all[i, top : top + HW, :])
            over = CH * k + HW * i
            gate_hi[there : there + HW, over : over + 128] = high
            gate_lo[there : there + HW, over : over + 128] = low
            for j, (at, size) in enumerate(TAILS):
                high, low = split(params_all[i, top + HW : top + HW + size, 32 * j : 32 * j + 32])
                rows_here = slice(there + at, there + at + size)
                gate_hi[rows_here, over + 128 : over + HW] = high
                gate_lo[rows_here, over + 128 : over + HW] = low
    keep(gate_hi, hi_out)
    keep(gate_lo, lo_out)
    edge.wait_recv()
    ext[0:8, :] = jnp.where(block > 0, halo[8:16, :].astype(f32), 0.0)

    def conv(i):
        r = i * 16
        near = ext[pl.ds(pl.multiple_of(r, 16), 24), :]
        acc = vec[4:5, :] + vec[0:1, :] * near[8:24, :]
        for k in (1, 2, 3):
            acc = acc + vec[k : k + 1, :] * behind(near, k)
        c[pl.ds(pl.multiple_of(r, 16), 16), :] = acc

    loop(TOK // 16, conv)
    keep(ext, ext_out)
    keep(c, c_out)
    step(plane_b)

    def gates(i):
        r = pl.ds(pl.multiple_of(i * 128, 128), 128)
        pre[r, :] = dot3(split(c[r, :]), (gate_hi[...], gate_lo[...]), ((1,), (0,)))

    loop(TOK // 128, gates)
    step(plane_a, other, plane_b)

    def point(i, carry):
        prod_in, state = carry
        r = pl.ds(pl.multiple_of(i * 8, 8), 8)
        rr = jax.nn.sigmoid(pre[r, 0:CH] + vec[5:6, :])
        gg = jax.nn.sigmoid(pre[r, CH:] + vec[6:7, :])
        log_a = -8.0 * rr * vec[7:8, :]
        aa = jnp.exp(log_a)
        mm = jnp.sqrt(minus_expm1(2.0 * log_a))
        rate[r, :] = rr
        gin[r, :] = gg
        a[r, :] = aa
        m[r, :] = mm
        pa, hb = scan8(aa, mm * gg * c[r, :], False)
        hb = hb + pa * state
        pa = pa * prod_in
        h[r, :] = hb
        prod[r, :] = pa
        return pa[7:8, :], hb[7:8, :]

    last = (jnp.ones((1, CH), f32), jnp.zeros((1, CH), f32))
    last = lax.fori_loop(0, TOK // 16, point, last)
    step(plane_a, plane_b)
    last = lax.fori_loop(TOK // 16, TOK // 8, point, last)
    for source, target in ((rate, rate_out), (gin, gin_out), (a, a_out), (m, m_out)):
        keep(source, target)
    mine[...] = jnp.zeros((8, CH), f32)
    total[...] = jnp.zeros((8, CH), f32)
    mine[0:1, :] = last[0]
    mine[1:2, :] = last[1]
    came = line_prefix(mine, quad, rows, total, put, False)
    state_in[...] = jnp.broadcast_to(came, (8, CH))
    total_a[...] = jnp.broadcast_to(last[0], (8, CH))
    step(plane_b)
    finish(plane_a, other)
    edge.wait_send()

    def complete(i):
        r = pl.ds(pl.multiple_of(i * 16, 16), 16)
        hh = h[r, :] + prod[r, :] * came
        h[r, :] = hh
        hy[r, :] = (hh * gelu_parts(yb[r, :])[0]).astype(bf)

    loop(TOK // 16, complete)
    keep(h, h_out)
    keep(hy, hy_out)

    finish(plane_b)
    put.drain(skip=edge)
    keep.drain()


def front(*operands):
    wide = shape((TOK, CH), f32)
    rows = shape((TOK, D), bf)
    mlp = shape((1536, D), bf)
    gate = shape((CH, 2 * CH), bf)
    out = (
        rows, rows, wide, wide, wide, wide, wide, wide, wide, wide,
        shape((TOK, CH), bf), shape((TOK + 8, CH), f32), gate, gate,
        rows, shape((3, CH, D), bf), mlp, mlp,
    )
    little = (
        shape((TOK, 128), f32), shape((8, D), f32), shape((16, CH), f32),
        shape((8, CH), f32), shape((8, CH), f32),
    )
    tall = pltpu.VMEM((TOK, CH), f32)
    return pl.pallas_call(
        front_kernel,
        out_shape=out + little,
        in_specs=[VMEM] * 4 + [ANY] * 3,
        out_specs=[ANY] * len(out) + [VMEM] * len(little),
        scratch_shapes=[
            pltpu.VMEM((TOK, D), bf),
            pltpu.VMEM((TOK, D), bf),
            pltpu.VMEM((3, CH, D), bf),
            pltpu.VMEM((4, PACKED, 128), f32),
            pltpu.VMEM((4, 4, 8, 128), f32),
            tall, tall, tall, tall, tall, tall, tall, tall,
            pltpu.VMEM((TOK, CH), bf),
            pltpu.VMEM((TOK + 8, CH), f32),
            pltpu.VMEM((CH, 2 * CH), bf),
            pltpu.VMEM((CH, 2 * CH), bf),
            pltpu.VMEM((TOK, 2 * CH), f32),
            tall,
            pltpu.VMEM((16, CH), bf),
            pltpu.VMEM((8, CH), f32),
            pltpu.VMEM((4, 8, CH), f32),
            pltpu.VMEM((8, 8, CH), f32),
            pltpu.VMEM((8, CH), f32),
        ]
        + semaphores(18 + 9 + 11 + 3 * GATHER_COPIES)
        + [pltpu.SemaphoreType.DMA((26,))],
        compiler_params=params(0),
        name="front",
    )(*operands)


def backward_kernel(
    dhy_in, yb_in, hi_in, lo_in, vec, c_in, rate_in, gin_in, a_in, m_in, h_in, ext_in, state_in, total_a,
    mlp_in, zown_in, down, gate,
    dxb, dyb, blocks, block_out, down_sum, gate_sum,
    e, apad, hpad, q, prod, pri, halo, mine, quad, rows, total, own, low, came_z, sent_z,
    yb, gate_hi, gate_lo, c, rate, gin, m, ext, mlp_part, z_own, dgate, sums, *rest,
):
    dc = q
    block = my_block()
    after, before = lax.rem(block + 1, 32), lax.rem(block + 31, 32)
    send, recv, done = rest[2 * SUM_SCRATCH :]
    keep = Keeper(done)
    load_mlp = keep(mlp_in, mlp_part)
    load_first = [
        keep(dhy_in, e),
        keep(yb_in, yb),
        keep(h_in, hpad.at[pl.ds(8, TOK), :]),
        keep(a_in, apad.at[pl.ds(0, TOK), :]),
    ]
    load_point = [keep(*pair) for pair in ((rate_in, rate), (gin_in, gin), (m_in, m), (c_in, c))]
    load_rest = [keep(*pair) for pair in ((hi_in, gate_hi), (lo_in, gate_lo), (ext_in, ext), (zown_in, z_own))]
    meet(
        line_devices()
        + [plane_device(after), plane_device(before)]
        + plane_neighbours()
        + z_others()
    )
    put = Sender(send, recv)
    whole = ring_sum(mlp_part, own, came_z, sent_z, put)
    plane = plane_sum([down], down_sum, rest[:SUM_SCRATCH], put, keep)
    plane_b = plane_sum([gate], gate_sum, rest[SUM_SCRATCH : 2 * SUM_SCRATCH], put, keep)
    keep.wait(load_mlp)
    step(whole, plane)
    for copy in load_first:
        keep.wait(copy)

    def direct(i):
        r = pl.ds(pl.multiple_of(i * 16, 16), 16)
        value, slope = gelu_parts(yb[r, :])
        grad = e[r, :]
        hh = hpad[pl.ds(pl.multiple_of(i * 16 + 8, 8), 16), :]
        e[r, :] = grad * value
        dyb[r, :] = (grad * hh * slope).astype(bf)

    loop(TOK // 16, direct)
    apad[TOK : TOK + 8, :] = jnp.ones((8, CH), f32)
    hpad[0:8, :] = state_in[...]
    step(whole, plane, plane_b)

    def adjoint(i, carry):
        prod_in, state = carry
        r0 = TOK - 8 - i * 8
        r = pl.ds(pl.multiple_of(r0, 8), 8)
        next_a = ahead(apad[pl.ds(pl.multiple_of(r0, 8), 16), :], 1)
        pa, qb = scan8(next_a, e[r, :], True)
        qb = qb + pa * state
        pa = pa * prod_in
        q[r, :] = qb
        prod[r, :] = pa
        return pa[0:1, :], qb[0:1, :]

    last = (jnp.ones((1, CH), f32), jnp.zeros((1, CH), f32))
    last = lax.fori_loop(0, TOK // 16, adjoint, last)
    step(plane_b)
    last = lax.fori_loop(TOK // 16, TOK // 8, adjoint, last)
    step(plane)
    mine[...] = jnp.zeros((8, CH), f32)
    total[...] = jnp.zeros((8, CH), f32)
    mine[0:1, :] = total_a[0:1, :]
    mine[1:2, :] = apad[0:1, :] * last[1]
    came = line_prefix(mine, quad, rows, total, put, True)
    step(plane)
    for copy in load_point:
        keep.wait(copy)

    def point(i, carry):
        s_rate, s_input, s_decay = carry
        r = pl.ds(pl.multiple_of(i * 8, 8), 8)
        qq = q[r, :] + prod[r, :] * came
        aa, rr, gg, mm, cc = apad[r, :], rate[r, :], gin[r, :], m[r, :], c[r, :]
        earlier = pltpu.roll(hpad[pl.ds(pl.multiple_of(i * 8, 8), 16), :], 1, 0)[8:16, :]
        grad_log = aa * (qq * earlier - qq * gg * cc * aa / mm)
        pr = -8.0 * vec[7:8, :] * grad_log * rr * (1.0 - rr)
        pi = qq * mm * cc * gg * (1.0 - gg)
        pri[r, 0:CH] = pr
        pri[r, CH:] = pi
        dc[r, :] = qq * mm * gg
        return s_rate + pr, s_input + pi, s_decay + 8.0 * rr * vec[8:9, :] * grad_log

    none = jnp.zeros((8, CH), f32)
    so_far = lax.fori_loop(0, TOK // 16, point, (none, none, none))
    step(plane_b)
    s_rate, s_input, s_decay = lax.fori_loop(TOK // 16, TOK // 8, point, so_far)
    step(plane)

    for copy in load_rest:
        keep.wait(copy)

    def spread(i):
        r = pl.ds(pl.multiple_of(i * 128, 128), 128)
        dc[r, :] = dc[r, :] + dot3(split(pri[r, :]), (gate_hi[...], gate_lo[...]), ((1,), (1,)))

    loop(TOK // 128, spread)
    edge = put(dc.at[pl.ds(0, 8), :], halo, plane_device(before))
    finish(whole)
    low[...] = (own[...] + z_own[...]).astype(bf)
    back, kept = quad_scatter(low, block_out, put, keep)
    step(plane_b)
    dgate[...] = dot3(split(c[...]), split(pri[...]), ((0,), (0,)))
    step(plane, plane_b)
    edge.wait_recv()
    dc[TOK : TOK + 8, :] = jnp.where(block < 31, halo[...], 0.0)

    def taps(i, carry):
        r = i * 16
        here = pl.ds(pl.multiple_of(r, 16), 16)
        later = dc[pl.ds(pl.multiple_of(r, 16), 24), :]
        near = ext[pl.ds(pl.multiple_of(r, 16), 24), :]
        dd = later[0:16, :]
        out = vec[0:1, :] * dd
        for k in (1, 2, 3):
            out = out + vec[k : k + 1, :] * ahead(later, k)
        dxb[here, :] = out.astype(bf)

        def fold(v):
            return v[0:8, :] + v[8:16, :]

        new = [carry[0] + fold(dd)]
        for k in range(4):
            new.append(carry[1 + k] + fold(dd * behind(near, k)))
        return tuple(new)

    s_bias, *s_taps = lax.fori_loop(0, TOK // 16, taps, (none,) * 5)

    def place_sum(row, value):
        sums[row : row + 1, :] = jnp.sum(value, axis=0, keepdims=True)

    for k in range(4):
        place_sum(k, s_taps[k])
    place_sum(4, s_bias)
    place_sum(5, s_rate)
    place_sum(6, s_input)
    place_sum(7, s_decay)
    for i in range(4):
        there = HW * i
        for k in (0, 1):
            top, over = SQUARE * k, CH * k + HW * i
            blocks[i, top : top + HW, :] = dgate[there : there + HW, over : over + 128]
            for j, (at, size) in enumerate(TAILS):
                blocks[i, top + HW : top + HW + size, 32 * j : 32 * j + 32] = dgate[
                    there + at : there + at + size, over + 128 : over + HW
                ]
            blocks[i, top + HW + 16 : top + SQUARE, 96:128] = jnp.zeros((32, 32), f32)
        blocks[i, 2 * SQUARE :, :] = jnp.zeros((32, 128), f32)
        blocks[i, 2 * SQUARE : 2 * SQUARE + 8, :] = sums[:, there : there + 128]
        blocks[i, 2 * SQUARE + 16 : 2 * SQUARE + 24, 0:32] = sums[:, there + 128 : there + HW]
    finish(plane, plane_b)
    got(back)
    keep.wait(kept)
    put.drain()
    keep.drain()


def backward_scan(*operands):
    r = operands[-1].shape[1]
    tall = pltpu.VMEM((TOK, CH), f32)
    return pl.pallas_call(
        backward_kernel,
        out_shape=(
            shape((TOK, CH), bf),
            shape((TOK, CH), bf),
            shape((4, PACKED, 128), f32),
            shape((4 * TOK, 128), bf),
            shape((r, 256), f32),
            shape((r, 256), f32),
        ),
        in_specs=[ANY] * 4 + [VMEM] + [ANY] * 7 + [VMEM] * 2 + [ANY] * 4,
        out_specs=[VMEM] * 6,
        scratch_shapes=[
            tall,
            pltpu.VMEM((TOK + 8, CH), f32),
            pltpu.VMEM((TOK + 8, CH), f32),
            pltpu.VMEM((TOK + 8, CH), f32),
            tall,
            pltpu.VMEM((TOK, 2 * CH), f32),
            pltpu.VMEM((8, CH), f32),
            pltpu.VMEM((8, CH), f32),
            pltpu.VMEM((4, 8, CH), f32),
            pltpu.VMEM((8, 8, CH), f32),
            pltpu.VMEM((8, CH), f32),
            pltpu.VMEM((TOK, 512), f32),
            pltpu.VMEM((TOK, 512), bf),
        ]
        + ring_scratch()
        + [
            tall,
            pltpu.VMEM((CH, 2 * CH), bf),
            pltpu.VMEM((CH, 2 * CH), bf),
            tall,
            tall,
            tall,
            tall,
            pltpu.VMEM((TOK + 8, CH), f32),
            pltpu.VMEM((TOK, D), bf),
            pltpu.VMEM((TOK, 512), f32),
            pltpu.VMEM((CH, 2 * CH), f32),
            pltpu.VMEM((8, CH), f32),
        ]
        + sum_scratch(r)
        + sum_scratch(r)
        + semaphores(11 + 6 + 3 + 2 * SUM_COPIES)
        + [pltpu.SemaphoreType.DMA((14 + 2 * SUM_KEEPS,))],
        compiler_params=params(4),
        name="backward_scan",
    )(*operands)


def dot(p, q):
    return jnp.dot(p, q, preferred_element_type=f32)


def dot_t0(p, q):
    return lax.dot_general(p, q, (((0,), (0,)), ((), ())), preferred_element_type=f32)


def dot_t1(p, q):
    return lax.dot_general(p, q, (((1,), (1,)), ((), ())), preferred_element_type=f32)


def per_device(
    block_in, cotangent, norm_one, rec_in, rec_gate, conv_weight, conv_bias,
    rate_weight, rate_bias, input_weight, input_bias, decay_code, rec_out,
    norm_two, mlp_gate, mlp_up, mlp_down,
):
    decay = decay_code.astype(f32) / 256.0
    vectors = jnp.concatenate(
        [
            conv_weight,
            conv_bias[None],
            rate_bias[None],
            input_bias[None],
            jax.nn.softplus(-decay)[None],
            jax.nn.sigmoid(-decay)[None],
            jnp.zeros((7, HW), f32),
        ],
        axis=0,
    )
    packed = jnp.concatenate(
        [
            pack_square(rate_weight[0]),
            pack_square(input_weight[0]),
            vectors[:, :128],
            jnp.pad(vectors[:, 128:], ((0, 0), (0, 96))),
        ],
        axis=0,
    )
    norms = jnp.concatenate([norm_one[None], norm_two[None], jnp.zeros((6, 128), f32)], axis=0)
    (
        x_full, n_one, xb, yb, c, rate, gin, a, m, h, hy, ext, gate_hi, gate_lo,
        cot_full, w_rec, w_gate, w_up,
        inv_one, gains, vec, state_in, total_a,
    ) = front(
        block_in, cotangent, packed, norms,
        jnp.stack([rec_in.T, rec_gate.T, rec_out]), mlp_gate.T, mlp_up.T,
    )
    z_own, dz_own, dmix, mlp_part, part_down, part_gate, part_up, gain_two_sums = middle(
        hy, w_rec, x_full, cot_full, w_gate, w_up, mlp_down, gains
    )
    w_in, w_gate_rec, w_out = w_rec[0], w_rec[1], w_rec[2]
    dhy = dot_t1(dmix, w_out)
    part_down, part_gate, part_up = (p.reshape(4, 384, D) for p in (part_down, part_gate, part_up))
    dxb, dyb, blocks, block_out, grad_down, grad_gate = backward_scan(
        dhy, yb, gate_hi, gate_lo, vec, c, rate, gin, a, m, h, ext, state_in, total_a,
        mlp_part, z_own, part_down, part_gate,
    )
    gain_one = gains[0:1]
    inv_one = inv_one[:, :1]
    x_rows = x_full.astype(f32)
    gain_two_sums = jnp.sum(gain_two_sums, axis=0)
    inner_one = jnp.sum(dxb.astype(f32) * xb + dyb.astype(f32) * yb, axis=1, keepdims=True)
    dn_one = dot(dxb, w_in) + dot(dyb, w_gate_rec)
    step_one = dn_one * inv_one * gain_one - x_rows * (inv_one * inv_one * inner_one / D)
    gain_one_sums = jnp.sum(dn_one * x_rows * inv_one, axis=0)
    part_rec = [
        dot_t0(p, q).astype(bf).reshape(4, HW, D) for p, q in ((dxb, n_one), (dyb, n_one), (hy, dmix))
    ]
    gains = jnp.stack([gain_one_sums.reshape(4, 4, 128), gain_two_sums.reshape(4, 4, 128)], axis=2)
    gains = jnp.concatenate([gains, jnp.zeros((4, 4, 6, 128), f32)], axis=2)
    grad_in, grad_rec, grad_up, small, gain_sums = last_sums(
        step_one.astype(bf), dz_own, *part_rec, part_up, blocks, gains
    )
    grad_rec_in, grad_rec_gate, grad_out = grad_rec[:HW].T, grad_rec[HW : 2 * HW].T, grad_rec[2 * HW :]
    grad_rate, grad_input = unpack_square(small[:SQUARE]), unpack_square(small[SQUARE : 2 * SQUARE])
    vector_grads = small[2 * SQUARE :]
    vector_grads = jnp.concatenate([vector_grads[:8], vector_grads[16:24, :32]], axis=1)
    return (
        block_out,
        grad_in.astype(f32),
        gain_sums[0],
        grad_rec_in,
        grad_rec_gate,
        vector_grads[0:4],
        vector_grads[4],
        grad_rate[None],
        vector_grads[5],
        grad_input[None],
        vector_grads[6],
        vector_grads[7],
        grad_out,
        gain_sums[1],
        grad_gate.T,
        grad_up.T,
        grad_down,
    )


def solution(mesh):
    fine = Mesh(mesh.devices.reshape(2, 4, 4, 2, 2), ("ylo", "x", "z", "yhi", "core"))
    both = P(SEQ, HEAD)
    swap = P(HEAD, SEQ)
    vector = P(HEAD)
    stack = P(HEAD, None, None)
    taps = P(None, HEAD)
    return jax.shard_map(
        per_device,
        mesh=fine,
        in_specs=(
            both, both, vector, both, both, taps, vector, stack, vector, stack, vector, vector,
            swap, vector, both, both, swap,
        ),
        out_specs=(
            both, both, vector, both, both, taps, vector, stack, vector, stack, vector, vector,
            swap, vector, both, both, swap,
        ),
        check_vma=False,
    )
```

```python
import jax
import jax.numpy as jnp
from jax import lax
from jax.experimental import pallas as pl
from jax.experimental.pallas import tpu as pltpu
from jax.sharding import Mesh, PartitionSpec as P

D = 2048
CONV = 4
EPS = 1e-06
TOK = 512
CH = 640
HW = 160
TAILS = ((0, 48), (48, 48), (96, 48), (144, 16))
SQUARE = 208
PACKED = 2 * SQUARE + 32
MESH = pl.DeviceIdType.MESH
SEQ = ("ylo", "x")
HEAD = ("z", "yhi", "core")
QUAD = ("yhi", "core")
PLANE = ("ylo", "x", "yhi", "core")
bf = jnp.bfloat16
f32 = jnp.float32
VMEM = pl.BlockSpec(memory_space=pltpu.VMEM)
ANY = pl.BlockSpec(memory_space=pl.ANY)


def shape(dims, dtype):
    return jax.ShapeDtypeStruct(dims, dtype)


def params(cid):
    return pltpu.CompilerParams(
        collective_id=cid, has_side_effects=True, vmem_limit_bytes=60 * 2**20
    )


def quad_device(index):
    return {"yhi": index // 2, "core": lax.rem(index, 2)}


def plane_device(block):
    return {
        "ylo": block // 16,
        "x": lax.rem(block // 4, 4),
        "yhi": lax.rem(block // 2, 2),
        "core": lax.rem(block, 2),
    }


def meet(devices):
    barrier = pltpu.get_barrier_semaphore()
    for device in devices:
        pl.semaphore_signal(barrier, inc=1, device_id=device, device_id_type=MESH)
    pl.semaphore_wait(barrier, len(devices))


def place():
    ylo, x, yhi, core = (lax.axis_index(n) for n in ("ylo", "x", "yhi", "core"))
    return ylo, x, yhi, core

def x_device(i):
    return {"x": i}

def y_device(i):
    return {"yhi": i // 2, "ylo": lax.rem(i, 2)}

def around(i):
    return lax.rem(i + 1, 4), lax.rem(i + 3, 4), lax.rem(i + 2, 4)

def plane_neighbours():
    ylo, x, yhi, core = place()
    y = yhi * 2 + ylo
    xr, xl, _ = around(x)
    yr, yl, _ = around(y)
    return [x_device(xr), x_device(xl), y_device(yr), y_device(yl), {"core": 1 - core}]

class Sender:
    def __init__(self, send, recv, base=0):
        self.send, self.recv, self.base, self.all = send, recv, base, []

    def __call__(self, source, target, device):
        i = self.base + len(self.all)
        copy = pltpu.make_async_remote_copy(
            src_ref=source,
            dst_ref=target,
            send_sem=self.send.at[i],
            recv_sem=self.recv.at[i],
            device_id=device,
            device_id_type=MESH,
        )
        copy.start()
        self.all.append(copy)
        return copy

    def drain(self, skip=None):
        for copy in self.all:
            if copy is not skip:
                copy.wait_send()


class Keeper:
    def __init__(self, done):
        self.done, self.count, self.open = done, 0, []

    def __call__(self, source, target):
        copy = pltpu.make_async_copy(source, target, self.done.at[self.count])
        copy.start()
        self.count += 1
        self.open.append(copy)
        return copy

    def wait(self, copy):
        self.open = [c for c in self.open if c is not copy]
        copy.wait()

    def drain(self):
        for copy in self.open:
            copy.wait()


def semaphores(count):
    return [pltpu.SemaphoreType.DMA((count,)), pltpu.SemaphoreType.DMA((count,))]


def got(copies):
    for copy in copies:
        copy.wait_recv()


def step(*plans):
    for plan in plans:
        next(plan, None)


def finish(*plans):
    for plan in plans:
        for _ in plan:
            pass


def z_columns(block):
    return pl.ds(pl.multiple_of(block * 512, 512), 512)


def ring_gather(full, put):
    z = lax.axis_index("z")
    right, left, _ = around(z)
    half = full.shape[0] // 2

    def start(row, block, to):
        part = full.at[pl.ds(row, half), z_columns(block)]
        return put(part, part, {"z": to})

    c0 = start(0, z, right)
    c1 = start(half, z, left)
    c2 = start(half, z, right)
    c3 = start(0, z, left)
    yield
    c0.wait_recv()
    c4 = start(0, left, right)
    c1.wait_recv()
    c5 = start(half, right, left)
    yield
    got([c2, c3, c4, c5])


def ring_sum(part, out, came, sent, put, produce=lambda block: None):
    z = lax.axis_index("z")
    right, left, far = around(z)
    half = part.shape[0] // 2
    lo, hi = pl.ds(0, half), pl.ds(half, half)
    cols = z_columns

    def start(i, source, to):
        return put(source, came.at[i], {"z": to})

    produce(far)
    c0 = start(0, part.at[lo, cols(far)], right)
    c1 = start(1, part.at[hi, cols(far)], left)
    produce(right)
    c2 = start(2, part.at[hi, cols(right)], right)
    produce(left)
    c3 = start(3, part.at[lo, cols(left)], left)
    produce(z)
    yield
    c0.wait_recv()
    sent[0] = came[0] + part[lo, cols(right)]
    c4 = start(4, sent.at[0], right)
    c1.wait_recv()
    sent[1] = came[1] + part[hi, cols(left)]
    c5 = start(5, sent.at[1], left)
    yield
    got([c3, c4])
    out[lo, :] = part[lo, cols(z)].astype(f32) + came[3].astype(f32) + came[4].astype(f32)
    got([c2, c5])
    out[hi, :] = part[hi, cols(z)].astype(f32) + came[2].astype(f32) + came[5].astype(f32)


def ring_scratch():
    return [pltpu.VMEM((6, TOK // 2, 512), bf), pltpu.VMEM((2, TOK // 2, 512), bf)]


def z_others():
    z = lax.axis_index("z")
    return [{"z": lax.rem(z + j, 4)} for j in (1, 2, 3)]


def quad_others():
    me = lax.axis_index("yhi") * 2 + lax.axis_index("core")
    return [quad_device(lax.rem(me + j, 4)) for j in (1, 2, 3)]


def quad_gather(tokens, full, put, keep):
    z = lax.axis_index("z")
    me = lax.axis_index("yhi") * 2 + lax.axis_index("core")
    mine = pl.ds(pl.multiple_of(z * 512 + me * 128, 128), 128)
    copies = []
    for j in (1, 2, 3):
        peer = lax.rem(me + j, 4)
        source = tokens.at[pl.ds(pl.multiple_of(peer * TOK, TOK), TOK), :]
        copies.append(put(source, full.at[:, mine], quad_device(peer)))
    own = keep(tokens.at[pl.ds(pl.multiple_of(me * TOK, TOK), TOK), :], full.at[:, mine])
    return copies, own


def token_gather(tokens, full, put, keep):
    copies, own = quad_gather(tokens, full, put, keep)
    yield
    got(copies)
    keep.wait(own)
    yield from ring_gather(full, put)


def quad_scatter(own, tokens, put, keep):
    me = lax.axis_index("yhi") * 2 + lax.axis_index("core")
    rows = pl.ds(pl.multiple_of(me * TOK, TOK), TOK)
    copies = []
    for j in (1, 2, 3):
        peer = lax.rem(me + j, 4)
        source = own.at[:, pl.ds(pl.multiple_of(peer * 128, 128), 128)]
        copies.append(put(source, tokens.at[rows, :], quad_device(peer)))
    mine = keep(own.at[:, pl.ds(pl.multiple_of(me * 128, 128), 128)], tokens.at[rows, :])
    return copies, mine


GATHER_COPIES = 48
SUM_COPIES = 36
SUM_KEEPS = 8


HALF = TOK // 2
UNIT = 256


CUTS = ((0, 256), (256, 256), (512, 128))


def rec_grad(left, right, into):
    for at, width in CUTS:
        for k in range(4):
            cols = slice(512 * k, 512 * k + 512)
            into[at : at + width, cols] = lax.dot_general(
                left[:, at : at + width], right[:, cols], (((0,), (0,)), ((), ())), preferred_element_type=f32
            ).astype(bf)


def middle_kernel(
    hy_in, rec_in, x_in, cot_in, gate_in, up_in, own_down, gains,
    zown_out, dz_out, dhy_out, mlp_out, out_grad, down_grad, gate_grad, up_grad, gain_sums,
    hy, w_out, x, cot, w_gate, w_up, w_down, normed, mixed, part, part_two, back, act, dg, du, mlp,
    own_one, own_two, inv, inner, dhy, *rest,
):
    rings, (send, recv, done) = rest[:8], rest[8:]
    z = lax.axis_index("z")
    keep = Keeper(done)
    load_mix = [keep(hy_in, hy), keep(rec_in.at[2], w_out)]
    load_norm = [keep(x_in, x)]
    load_mlp = [keep(gate_in, w_gate), keep(up_in, w_up), keep(cot_in, cot)]
    meet(z_others() + plane_neighbours())
    put = Sender(send, recv)
    plane = plane_gather(own_down, w_down, put, keep)
    step(plane)
    puts = [Sender(send, recv, GATHER_COPIES + 12 * i) for i in range(4)]

    def rows_of(half):
        return pl.ds(HALF * half, HALF)

    def view(ref, half):
        return ref.at[rows_of(half), :]

    def wide(ref, rows, times):
        return jnp.concatenate([ref[rows, :]] * times, axis=1)

    def mix_block(half):
        def produce(at):
            part[rows_of(half), z_columns(at)] = jnp.dot(
                hy[rows_of(half), :], w_out[:, z_columns(at)], preferred_element_type=f32
            ).astype(bf)

        return produce

    def sums(i, half, source, own, produce):
        return ring_sum(
            view(source, half), view(own, half), rings[2 * i], rings[2 * i + 1], puts[i], produce
        )

    def spread(i, half, full, own):
        full[rows_of(half), z_columns(z)] = own[rows_of(half), :].astype(bf)
        return ring_gather(view(full, half), puts[i])

    def norm(half):
        def body(i):
            r = pl.ds(pl.multiple_of(HALF * half + i * 16, 16), 16)
            values = x[r, :].astype(f32) + mixed[r, :].astype(f32)
            mean = jnp.sum(values * values, axis=1, keepdims=True) * (1.0 / D)
            scale = lax.rsqrt(mean + EPS)
            inv[r, :] = jnp.broadcast_to(scale, (16, 128))
            normed[r, :] = (values * scale * gains[1:2, :]).astype(bf)

        loop(HALF // 16, body)

    def hidden(half, first, count):
        r = rows_of(half)

        def body(j):
            at = pl.ds(pl.multiple_of((first + j) * UNIT, UNIT), UNIT)

            def against(left, right):
                return lax.dot_general(
                    left, right[at, :], (((1,), (1,)), ((), ())), preferred_element_type=f32
                )

            g = against(normed[r, :], w_gate)
            u = against(normed[r, :], w_up)
            da = against(cot[r, :], w_down)
            value, slope = gelu_parts(g)
            act[r, at] = (value * u).astype(bf)
            low_g = (da * u * slope).astype(bf)
            low_u = (da * value).astype(bf)
            dg[r, at] = low_g
            du[r, at] = low_u
            t = low_g.astype(f32) * g + low_u.astype(f32) * u
            inner[r, :] = inner[r, :] + (t[:, :128] + t[:, 128:])

        loop(count, body)

    def close(half):
        r = rows_of(half)
        total = jnp.sum(inner[r, :], axis=1, keepdims=True) * (1.0 / D)
        inner[r, :] = inv[r, :] * inv[r, :] * total

    def back_block(half):
        r = rows_of(half)

        def produce(at):
            cols = z_columns(at)
            dn = jnp.dot(dg[r, :], w_gate[:, cols], preferred_element_type=f32)
            dn = dn + jnp.dot(du[r, :], w_up[:, cols], preferred_element_type=f32)
            values = x[r, cols].astype(f32) + mixed[r, cols].astype(f32)
            scaled = dn * wide(inv, r, 4)
            part_two[r, cols] = (scaled * gains[1:2, cols] - values * wide(inner, r, 4)).astype(bf)
            gain_sums[:, cols] = gain_sums[:, cols] + jnp.sum(
                (scaled * values).reshape(HALF // 8, 8, 512), axis=0
            )

        return produce

    def mlp_blocks():
        for at in range(4):
            cols = slice(512 * at, 512 * at + 512)
            mlp[:, cols] = jnp.dot(act[...], w_down[:, cols], preferred_element_type=f32).astype(bf)

    def weight_grad(left, right, into, target):
        def body(j):
            at = pl.ds(pl.multiple_of(j * UNIT, UNIT), UNIT)
            for k in range(4):
                cols = slice(512 * k, 512 * k + 512)
                into[at, cols] = lax.dot_general(
                    left[:, at], right[:, cols], (((0,), (0,)), ((), ())), preferred_element_type=f32
                ).astype(bf)

        loop(1536 // UNIT, body)
        keep(into, target)

    def add_own(half, whole, own):
        r = rows_of(half)
        own[r, :] = own[r, :] + whole[r, z_columns(z)].astype(f32)

    def add_cotangent(half):
        def body(i):
            r = pl.ds(pl.multiple_of(HALF * half + i * 16, 16), 16)
            back[r, :] = cot[r, :] + back[r, :]

        loop(HALF // 16, body)

    for copy in load_mix:
        keep.wait(copy)
    inner[...] = jnp.zeros((TOK, 128), f32)
    gain_sums[...] = jnp.zeros((8, D), f32)
    sum_a = sums(0, 0, part, own_one, mix_block(0))
    sum_b = sums(1, 1, part, own_one, mix_block(1))
    step(sum_a, sum_a)
    step(plane, sum_b)
    finish(sum_a)
    spread_a = spread(0, 0, mixed, own_one)
    step(spread_a, sum_b, plane, spread_a)
    finish(sum_b)
    spread_b = spread(1, 1, mixed, own_one)
    step(spread_b)
    finish(spread_a)
    for copy in load_norm:
        keep.wait(copy)
    add_own(0, x, own_one)
    norm(0)
    step(spread_b, plane)
    for copy in load_mlp:
        keep.wait(copy)
    finish(plane)
    hidden(0, 0, 3)
    finish(spread_b)
    add_own(1, x, own_one)
    keep(own_one, zown_out)
    hidden(0, 3, 3)
    close(0)
    total_a = sums(2, 0, part_two, own_two, back_block(0))
    step(total_a)
    norm(1)
    step(total_a)
    hidden(1, 0, 3)
    finish(total_a)
    back_a = spread(2, 0, back, own_two)
    step(back_a)
    hidden(1, 3, 2)
    step(back_a)
    hidden(1, 5, 1)
    close(1)
    total_b = sums(3, 1, part_two, own_two, back_block(1))
    step(total_b)
    finish(back_a)
    puts[2].drain()
    add_cotangent(0)
    add_own(0, cot, own_two)
    step(total_b)
    mlp_blocks()
    keep(mlp, mlp_out)
    put.drain()
    finish(total_b)
    back_b = spread(3, 1, back, own_two)
    step(back_b)
    weight_grad(act, cot, w_down, down_grad)
    step(back_b)
    weight_grad(dg, normed, w_gate, gate_grad)
    weight_grad(du, normed, w_up, up_grad)
    finish(back_b)
    puts[3].drain()
    add_cotangent(1)
    for at, width in CUTS:
        dhy[:, at : at + width] = lax.dot_general(
            back[...], w_out[at : at + width, :], (((1,), (1,)), ((), ())), preferred_element_type=f32
        )
    keep(dhy, dhy_out)
    add_own(1, cot, own_two)
    keep(own_two, dz_out)
    rec_grad(hy, back, w_out)
    keep(w_out, out_grad)
    puts[0].drain()
    puts[1].drain()
    keep.drain()


def middle(*operands):
    mlp = shape((1536, D), bf)
    rows = shape((TOK, D), bf)
    own = shape((TOK, 512), f32)
    row_scratch = pltpu.VMEM((TOK, D), bf)
    weight = pltpu.VMEM((1536, D), bf)
    unit = pltpu.VMEM((TOK, 1536), bf)
    return pl.pallas_call(
        middle_kernel,
        out_shape=(
            own, own, shape((TOK, CH), f32), rows, shape((CH, D), bf), mlp, mlp, mlp, shape((8, D), f32),
        ),
        in_specs=[ANY] * 7 + [VMEM],
        out_specs=[ANY] * 8 + [VMEM],
        scratch_shapes=[
            pltpu.VMEM((TOK, CH), bf),
            pltpu.VMEM((CH, D), bf),
            row_scratch,
            row_scratch,
            weight,
            weight,
            weight,
            row_scratch,
            row_scratch,
            row_scratch,
            row_scratch,
            row_scratch,
            unit,
            unit,
            unit,
            row_scratch,
            pltpu.VMEM((TOK, 512), f32),
            pltpu.VMEM((TOK, 512), f32),
            pltpu.VMEM((TOK, 128), f32),
            pltpu.VMEM((TOK, 128), f32),
            pltpu.VMEM((TOK, CH), f32),
        ]
        + 4 * [pltpu.VMEM((6, HALF // 2, 512), bf), pltpu.VMEM((2, HALF // 2, 512), bf)]
        + semaphores(GATHER_COPIES + 48)
        + [pltpu.SemaphoreType.DMA((16,))],
        compiler_params=params(3),
        name="middle",
    )(*operands)


def cut(r):
    a = (r // 32) * 16
    a1 = ((a // 16 + 1) // 2) * 16
    b1 = (((r - a) // 16 + 1) // 2) * 16
    return a, a1, b1

def plane_gather(own, full, put, keep):
    r = own.shape[-2]
    lead = (slice(None),) * (len(own.shape) - 2)
    ylo, x, yhi, core = place()
    y = yhi * 2 + ylo
    xr, xl, xf = around(x)
    yr, yl, yf = around(y)
    a, a1, b1 = cut(r)
    top, bottom = (0, a), (a, r - a)
    top1, top2 = (0, a1), (a1, a - a1)
    bot1, bot2 = (a, b1), (a + b1, r - a - b1)

    def span(quarter, rows):
        return pl.ds(pl.multiple_of(quarter * r + rows[0], 16), rows[1])

    sib = {"core": 1 - core}
    def cols(lo, xx):
        return pl.ds(pl.multiple_of(lo * 1024 + xx * 256, 256), 256)
    def one(rows, yy, xx):
        return full.at[lead + (span((yy // 2) * 2 + core, rows), cols(lax.rem(yy, 2), xx))]
    def row(rows, yy):
        return full.at[lead + (span((yy // 2) * 2 + core, rows), pl.ds(pl.multiple_of(lax.rem(yy, 2) * 1024, 1024), 1024))]
    kept = keep(own, one((0, r), y, x))
    ha, hb = own.at[lead + (pl.ds(*top),)], own.at[lead + (pl.ds(*bottom),)]
    p = [put(ha, one(top, y, x), x_device(xr)), put(ha, one(top, y, x), x_device(xl)),
         put(hb, one(bottom, y, x), y_device(yr)), put(hb, one(bottom, y, x), y_device(yl))]
    yield
    got(p)
    keep.wait(kept)
    p = [put(one(top1, y, xl), one(top1, y, xl), x_device(xr)), put(one(top2, y, xr), one(top2, y, xr), x_device(xl)),
         put(one(bot1, yl, x), one(bot1, yl, x), y_device(yr)), put(one(bot2, yr, x), one(bot2, yr, x), y_device(yl))]
    yield
    got(p)
    def pieces(rows, xx):
        out = []
        for lo in (0, 1):
            for hi in (0, 1):
                out.append(full.at[lead + (span(2 * hi + core, rows), cols(lo, xx))])
        return out
    def send_row(rows, yy, device):
        return [put(row(rows, yy), row(rows, yy), device)]
    def send_col(rows, xx, device):
        return [put(s, s, device) for s in pieces(rows, xx)]
    p = send_row(top, y, y_device(yr)) + send_row(top, y, y_device(yl))
    p += send_col(bottom, x, x_device(xr)) + send_col(bottom, x, x_device(xl))
    s = send_row(top, y, sib) + send_col(bottom, x, sib)
    yield
    got(p)
    p = send_row(top1, yl, y_device(yr)) + send_row(top2, yr, y_device(yl))
    p += send_col(bot1, xl, x_device(xr)) + send_col(bot2, xr, x_device(xl))
    s += send_row(top, yl, sib) + send_row(top, yr, sib) + send_col(bottom, xl, sib) + send_col(bottom, xr, sib)
    yield
    got(p)
    s += send_row(top, yf, sib) + send_col(bottom, xf, sib)
    yield
    got(s)


def plane_sum(parts, out, scratch, put, keep):
    own, fold, ga, gb, ha, hb, sa, sb, ra2, rb2 = scratch
    r = fold.shape[1]
    ylo, x, yhi, core = place()
    y = yhi * 2 + ylo
    xr, xl, xf = around(x)
    yr, yl, yf = around(y)
    a = -(-r // 64) * 32
    h, g = a // 2, (r - a) // 2
    sib = {"core": 1 - core}
    pieces = ([], [])
    at = 0
    for part in parts:
        size = part.shape[0] // 4
        middle = min(max(a - at, 0), size)
        for group, first, count in ((0, 0, middle), (1, middle, size - middle)):
            if count:
                pieces[group].append((part, size, first, count, at + first))
        at += size
    came = ([], [])
    held = ([], [])
    for group in (0, 1):
        for part, size, first, count, to in pieces[group]:

            def quarter(q):
                return part.at[pl.ds(pl.multiple_of(q * size + first, 16), count), :]

            for hi in (0, 1):
                into = pl.ds(to, count)
                came[group].append(put(quarter(2 * hi + 1 - core), fold.at[hi, into, :], sib))
                held[group].append(keep(quarter(2 * hi + core), own.at[hi, into, :]))
    yield

    def add_cores(group):
        got(came[group])
        for copy in held[group]:
            keep.wait(copy)
        first, count = ((0, a), (a, r - a))[group]
        for hi in (0, 1):

            def body(i, carry, hi=hi):
                rr = pl.ds(pl.multiple_of(first + i * 16, 16), 16)
                fold[hi, rr, :] = fold[hi, rr, :] + own[hi, rr, :]
                return carry

            lax.fori_loop(0, count // 16, body, 0)

    def ycols(yy):
        return pl.ds(pl.multiple_of(lax.rem(yy, 2) * 1024, 1024), 1024)
    def a_block(yy, first):
        return fold.at[yy // 2, pl.ds(0 if first else h, h), ycols(yy)]
    def b_block(xx, first, l):
        return fold.at[:, pl.ds(a + (0 if first else g), g), pl.ds(pl.multiple_of(l * 1024 + xx * 256, 256), 256)]
    yR, yL, xR, xL = y_device(yr), y_device(yl), x_device(xr), x_device(xl)
    def sendb(i, xx, first, dev):
        return [put(b_block(xx, first, l), gb.at[i, l], dev) for l in (0, 1)]
    add_cores(0)
    pa = [put(a_block(yf, True), ga.at[0], yR), put(a_block(yf, False), ga.at[1], yL)]
    pa += [put(a_block(yr, False), ga.at[2], yR), put(a_block(yl, True), ga.at[3], yL)]
    add_cores(1)
    pb = [sendb(0, xf, True, xR), sendb(1, xf, False, xL)]
    pb += [sendb(2, xr, False, xR), sendb(3, xl, True, xL)]
    yield

    def add_a(dst, i, block, n):
        def body(j, carry):
            rr = pl.ds(pl.multiple_of(j * 16, 16), 16)
            dst[rr, :] = ga[i, rr, :] + block[rr, :]
            return carry
        lax.fori_loop(0, n // 16, body, 0)
    def add_b(dst, i, xx, first):
        for l in (0, 1):
            for hi in (0, 1):
                block = fold.at[hi, pl.ds(a + (0 if first else g), g), pl.ds(pl.multiple_of(l * 1024 + xx * 256, 256), 256)]
                def body(j, carry):
                    rr = pl.ds(pl.multiple_of(j * 16, 16), 16)
                    dst[l, hi, rr, :] = gb[i, l, hi, rr, :] + block[rr, :]
                    return carry
                lax.fori_loop(0, g // 16, body, 0)
    pa[0].wait_recv()
    add_a(sa.at[0], 0, a_block(yr, True), h)
    pa.append(put(sa.at[0], ga.at[4], yR))
    got(pb[0])
    add_b(sb.at[0], 0, xr, True)
    pb.append([put(sb.at[0], gb.at[4], xR)])
    pa[1].wait_recv()
    add_a(sa.at[1], 1, a_block(yl, False), h)
    pa.append(put(sa.at[1], ga.at[5], yL))
    got(pb[1])
    add_b(sb.at[1], 1, xl, False)
    pb.append([put(sb.at[1], gb.at[5], xL)])
    yield
    def fin_a(first, i, j):
        def body(n, carry):
            rr = pl.ds(pl.multiple_of(n * 16, 16), 16)
            block = a_block(y, first)
            ra2[pl.ds(pl.multiple_of((0 if first else h) + n * 16, 16), 16), :] = (
                block[rr, :].astype(f32) + ga[i, rr, :].astype(f32) + ga[j, rr, :].astype(f32)).astype(bf)
            return carry
        lax.fori_loop(0, h // 16, body, 0)
    def fin_b(first, i, j):
        for l in (0, 1):
            for hi in (0, 1):
                block = fold.at[hi, pl.ds(a + (0 if first else g), g), pl.ds(pl.multiple_of(l * 1024 + x * 256, 256), 256)]
                def body(n, carry):
                    rr = pl.ds(pl.multiple_of(n * 16, 16), 16)
                    rb2[l, hi, pl.ds(pl.multiple_of((0 if first else g) + n * 16, 16), 16), :] = (
                        block[rr, :].astype(f32) + gb[i, l, hi, rr, :].astype(f32) + gb[j, l, hi, rr, :].astype(f32)).astype(bf)
                    return carry
                lax.fori_loop(0, g // 16, body, 0)
    got([pa[3], pa[4]])
    fin_a(True, 3, 4)
    got([pa[2], pa[5]])
    fin_a(False, 2, 5)
    got(pb[3] + pb[4])
    fin_b(True, 3, 4)
    got(pb[2] + pb[5])
    fin_b(False, 2, 5)
    def a2(xx, first):
        return ra2.at[pl.ds(0 if first else h, h), pl.ds(pl.multiple_of(xx * 256, 256), 256)]
    def b2(yy, first):
        return rb2.at[lax.rem(yy, 2), yy // 2, pl.ds(0 if first else g, g), :]
    qa = [put(a2(xf, True), ha.at[0], xR), put(a2(xf, False), ha.at[1], xL), put(a2(xr, False), ha.at[2], xR), put(a2(xl, True), ha.at[3], xL)]
    qb = [put(b2(yf, True), hb.at[0], yR), put(b2(yf, False), hb.at[1], yL), put(b2(yr, False), hb.at[2], yR), put(b2(yl, True), hb.at[3], yL)]
    yield
    sa2, sb2 = ha.at[pl.ds(6, 2)], hb.at[pl.ds(6, 2)]
    qa[0].wait_recv()
    sa2[0] = ha[0] + a2(xr, True)[...]
    qa.append(put(sa2.at[0], ha.at[4], xR))
    qb[0].wait_recv()
    sb2[0] = hb[0] + b2(yr, True)[...]
    qb.append(put(sb2.at[0], hb.at[4], yR))
    qa[1].wait_recv()
    sa2[1] = ha[1] + a2(xl, False)[...]
    qa.append(put(sa2.at[1], ha.at[5], xL))
    qb[1].wait_recv()
    sb2[1] = hb[1] + b2(yl, False)[...]
    qb.append(put(sb2.at[1], hb.at[5], yL))
    yield
    got(qa[2:] + qb[2:])
    def w(v): return v.astype(f32)
    out[0:h, :] = w(a2(x, True)[...]) + w(ha[3]) + w(ha[4])
    out[h:a, :] = w(a2(x, False)[...]) + w(ha[2]) + w(ha[5])
    out[a:a + g, :] = w(b2(y, True)[...]) + w(hb[3]) + w(hb[4])
    out[a + g:, :] = w(b2(y, False)[...]) + w(hb[2]) + w(hb[5])


SUM_SCRATCH = 10


def sum_scratch(r):
    a = -(-r // 64) * 32
    h, g = a // 2, (r - a) // 2
    V = pltpu.VMEM
    return [V((2, r, 2048), bf), V((2, r, 2048), bf), V((6, h, 1024), bf), V((6, 2, 2, g, 256), bf), V((8, h, 256), bf), V((8, g, 256), bf),
            V((2, h, 1024), bf), V((2, 2, 2, g, 256), bf), V((a, 1024), bf), V((2, 2, r - a, 256), bf)]


def small_sums(blocks, gains, small, gain, scratch, put):
    zgot, sgot, pair, pgot, qgain, rgot, rgain, mine = scratch
    z = lax.axis_index("z")
    yhi, core = lax.axis_index("yhi"), lax.axis_index("core")
    me = yhi * 2 + core
    row = lax.axis_index("ylo") * 4 + lax.axis_index("x")
    zs = []
    near = [put(blocks.at[2 * hi + 1 - core], sgot.at[hi], {"core": 1 - core}) for hi in (0, 1)]
    for j in (1, 2, 3):
        to = lax.rem(z + j, 4)
        zs.append(put(gains.at[to], zgot.at[j - 1], {"z": to}))
    yield
    got(near)
    for hi in (0, 1):
        pair[hi] = blocks[2 * hi + core] + sgot[hi]
    across = put(pair.at[1 - yhi], pgot, {"yhi": 1 - yhi})
    got(zs)
    qgain[3] = gains[z] + zgot[0] + zgot[1] + zgot[2]
    qs = []
    for j in (1, 2, 3):
        to = lax.rem(me + j, 4)
        qs.append(put(qgain.at[3, to], qgain.at[j - 1, 0], quad_device(to)))
    yield
    got(qs)
    across.wait_recv()
    mine[...] = pair[yhi] + pgot[...]
    rgain[7] = qgain[3, me] + qgain[0, 0] + qgain[1, 0] + qgain[2, 0]
    rs = []
    size = PACKED // 8

    def seq(j):
        to = lax.rem(row + j, 8)
        return to, {"ylo": to // 4, "x": lax.rem(to, 4)}

    for j in range(1, 8):
        to, device = seq(j)
        rs.append(put(mine.at[pl.ds(pl.multiple_of(to * size, 8), size), :], rgot.at[j - 1], device))
        rs.append(put(rgain.at[7], rgain.at[j - 1], device))
    yield
    got(rs)
    own = pl.ds(pl.multiple_of(row * size, 8), size)
    total = mine[own, :]
    gain_total = rgain[7]
    for j in range(7):
        total = total + rgot[j]
        gain_total = gain_total + rgain[j]
    small[own, :] = total
    gain[...] = gain_total
    ag = []
    for j in range(1, 8):
        _, device = seq(j)
        ag.append(put(small.at[own, :], small.at[own, :], device))
    yield
    got(ag)


SMALL_SCRATCH = 8
SMALL_COPIES = 30


def small_scratch():
    return [
        pltpu.VMEM((3, 4, 8, 128), f32),
        pltpu.VMEM((2, PACKED, 128), f32),
        pltpu.VMEM((2, PACKED, 128), f32),
        pltpu.VMEM((PACKED, 128), f32),
        pltpu.VMEM((4, 4, 8, 128), f32),
        pltpu.VMEM((7, PACKED // 8, 128), f32),
        pltpu.VMEM((8, 8, 128), f32),
        pltpu.VMEM((PACKED, 128), f32),
    ]


def tail_kernel(
    dxb_in, dyb_in, xb_in, yb_in, rec_weights, x_in, n_in, dz_in, rec_out, up, inv, gains, gain_two, blocks,
    grad_in, in_grad, gate_grad, out_grad, up_grad, rate_grad, input_grad, vec_grad, gain,
    dxb, dyb, xb, yb, w_in, w_gate, x, normed, dz, part, own, low, coef, gain_one, gain_parts,
    part_in, part_gate, rec_sum, up_sum, small, back_low, *rest,
):
    (came, sent), rest = rest[:2], rest[2:]
    plane_refs, rest = rest[:SUM_SCRATCH], rest[SUM_SCRATCH:]
    up_refs, rest = rest[:SUM_SCRATCH], rest[SUM_SCRATCH:]
    small_refs, rest = rest[:SMALL_SCRATCH], rest[SMALL_SCRATCH:]
    send, recv, done = rest
    keep = Keeper(done)
    first = [keep(*pair) for pair in ((dxb_in, dxb), (dyb_in, dyb), (n_in, normed))]
    second = [keep(xb_in, xb), keep(yb_in, yb)]
    third = [
        keep(*pair) for pair in ((rec_weights.at[0], w_in), (rec_weights.at[1], w_gate), (x_in, x))
    ]
    fourth = keep(dz_in, dz)
    meet(z_others() + plane_neighbours() + line_devices())
    put = Sender(send, recv)
    plane_up = plane_sum([up], up_sum, up_refs, put, keep)
    step(plane_up)
    for copy in first:
        keep.wait(copy)
    rec_grad(dxb, normed, part_in)
    rec_grad(dyb, normed, part_gate)
    plane = plane_sum([part_in, part_gate, rec_out], rec_sum, plane_refs, put, keep)
    step(plane)
    for copy in second:
        keep.wait(copy)

    def inner(i):
        r = pl.ds(pl.multiple_of(i * 16, 16), 16)
        terms = dxb[r, :].astype(f32) * xb[r, :] + dyb[r, :].astype(f32) * yb[r, :]
        total = jnp.sum(terms, axis=1, keepdims=True) * (1.0 / D)
        coef[r, :] = inv[r, :] * inv[r, :] * total

    loop(TOK // 16, inner)
    gain_one[...] = jnp.zeros((8, D), f32)
    step(plane_up)
    for copy in third:
        keep.wait(copy)

    def produce(at):
        cols = z_columns(at)
        for half in (0, 1):
            r = slice(HALF * half, HALF * (half + 1))
            dn = jnp.dot(dxb[r, :], w_in[:, cols], preferred_element_type=f32)
            dn = dn + jnp.dot(dyb[r, :], w_gate[:, cols], preferred_element_type=f32)
            values = x[r, cols].astype(f32)
            scaled = dn * jnp.concatenate([inv[r, :]] * 4, axis=1)
            less = values * jnp.concatenate([coef[r, :]] * 4, axis=1)
            part[r, cols] = (scaled * gains[0:1, cols] - less).astype(bf)
            gain_one[:, cols] = gain_one[:, cols] + jnp.sum(
                (scaled * values).reshape(HALF // 8, 8, 512), axis=0
            )

    total = ring_sum(part, own, came, sent, put, produce)
    step(total)
    sums_one = jnp.sum(gain_one[...], axis=0, keepdims=True)
    sums_two = jnp.sum(gain_two[...], axis=0, keepdims=True)
    gain_parts[...] = jnp.zeros((4, 4, 8, 128), f32)
    for i in range(4):
        for j in range(4):
            cols = slice(128 * (4 * i + j), 128 * (4 * i + j + 1))
            gain_parts[i, j, 0:1, :] = sums_one[:, cols]
            gain_parts[i, j, 1:2, :] = sums_two[:, cols]
    little = small_sums(blocks, gain_parts, small, gain, small_refs, put)
    step(little)
    step(plane, total, plane_up, little)
    step(plane_up, plane)
    finish(total)
    keep.wait(fourth)
    low[...] = (own[...] + dz[...]).astype(bf)
    back, mine = quad_scatter(low, back_low, put, keep)
    step(little, plane_up, plane, little)
    finish(plane_up)
    up_grad[...] = up_sum[...].T
    got(back)
    keep.wait(mine)

    def widen(i):
        r = pl.ds(pl.multiple_of(i * 64, 64), 64)
        grad_in[r, :] = back_low[r, :].astype(f32)

    loop(4 * TOK // 64, widen)
    step(plane)
    finish(little)
    for k, target in ((0, rate_grad), (1, input_grad)):
        top = SQUARE * k
        target[:, 0:128] = small[top : top + HW, :]
        for j, (at, size) in enumerate(TAILS):
            target[at : at + size, 128:HW] = small[top + HW : top + HW + size, 32 * j : 32 * j + 32]
    vec_grad[:, 0:128] = small[2 * SQUARE : 2 * SQUARE + 8, :]
    vec_grad[:, 128:HW] = small[2 * SQUARE + 16 : 2 * SQUARE + 24, 0:32]
    finish(plane)
    in_grad[...] = rec_sum[0:HW, :].T
    gate_grad[...] = rec_sum[HW : 2 * HW, :].T
    out_grad[...] = rec_sum[2 * HW :, :]
    put.drain()
    keep.drain()


def tail(*operands):
    rows = pltpu.VMEM((TOK, D), bf)
    tall = pltpu.VMEM((TOK, CH), f32)
    low = pltpu.VMEM((TOK, CH), bf)
    weight = pltpu.VMEM((CH, D), bf)
    return pl.pallas_call(
        tail_kernel,
        out_shape=(
            shape((4 * TOK, 128), f32),
            shape((256, HW), f32),
            shape((256, HW), f32),
            shape((HW, 256), f32),
            shape((256, 384), f32),
            shape((HW, HW), f32),
            shape((HW, HW), f32),
            shape((8, HW), f32),
            shape((8, 128), f32),
        ),
        in_specs=[ANY] * 10 + [VMEM] * 4,
        out_specs=[VMEM] * 9,
        scratch_shapes=[
            low, low, tall, tall, weight, weight, rows, rows,
            pltpu.VMEM((TOK, 512), f32),
            rows,
            pltpu.VMEM((TOK, 512), f32),
            pltpu.VMEM((TOK, 512), bf),
            pltpu.VMEM((TOK, 128), f32),
            pltpu.VMEM((8, D), f32),
            pltpu.VMEM((4, 4, 8, 128), f32),
            weight, weight,
            pltpu.VMEM((3 * HW, 256), f32),
            pltpu.VMEM((384, 256), f32),
            pltpu.VMEM((PACKED, 128), f32),
            pltpu.VMEM((4 * TOK, 128), bf),
        ]
        + ring_scratch()
        + sum_scratch(3 * HW)
        + sum_scratch(384)
        + small_scratch()
        + semaphores(6 + 3 + 2 * SUM_COPIES + SMALL_COPIES)
        + [pltpu.SemaphoreType.DMA((2 * SUM_KEEPS + 10,))],
        compiler_params=params(5),
        name="tail",
    )(*operands)


def line_devices():
    ylo, x = lax.axis_index("ylo"), lax.axis_index("x")
    row = ylo * 4 + x
    rows = [
        {"ylo": lax.rem(row + j, 8) // 4, "x": lax.rem(row + j, 4)} for j in range(1, 8)
    ]
    return quad_others() + rows


def my_block():
    row = lax.axis_index("ylo") * 4 + lax.axis_index("x")
    return row * 4 + lax.axis_index("yhi") * 2 + lax.axis_index("core")


def line_prefix(mine, quad, rows, total, put, backward):
    me = lax.axis_index("yhi") * 2 + lax.axis_index("core")
    row = lax.axis_index("ylo") * 4 + lax.axis_index("x")
    copies = []
    for j in (1, 2, 3):
        copies.append(put(mine, quad.at[me], quad_device(lax.rem(me + j, 4))))
    quad[me] = mine[...]
    got(copies)
    ones = jnp.ones((1, CH), f32)
    zeros = jnp.zeros((1, CH), f32)
    prod, end, prod_all, end_all = ones, zeros, ones, zeros
    for turn in range(4):
        q = 3 - turn if backward else turn
        a, b = quad[q, 0:1, :], quad[q, 1:2, :]
        end_all = a * end_all + b
        prod_all = a * prod_all
        take = (q > me) if backward else (q < me)
        end = jnp.where(take, a * end + b, end)
        prod = jnp.where(take, a * prod, prod)
    total[0:1, :] = prod_all
    total[1:2, :] = end_all
    copies = []
    for j in range(1, 8):
        other = lax.rem(row + j, 8)
        copies.append(put(total, rows.at[row], {"ylo": other // 4, "x": lax.rem(other, 4)}))
    rows[row] = total[...]
    got(copies)
    came = zeros
    for turn in range(8):
        r = 7 - turn if backward else turn
        a, b = rows[r, 0:1, :], rows[r, 1:2, :]
        take = (r > row) if backward else (r < row)
        came = jnp.where(take, a * came + b, came)
    return prod * came + end


def pack_square(weight):
    tail = jnp.pad(weight[:, 128:], ((0, 32), (0, 0))).reshape(4, 48, 32)
    return jnp.concatenate([weight[:, :128], tail.transpose(1, 0, 2).reshape(48, 128)], axis=0)


def split(values):
    high = values.astype(bf)
    return high, (values - high.astype(f32)).astype(bf)


def dot3(a, b, dims):
    (ah, al), (bh, bl) = a, b

    def one(p, q):
        return lax.dot_general(p, q, (dims, ((), ())), preferred_element_type=f32)

    return one(ah, bh) + (one(al, bh) + one(ah, bl))


def minus_expm1(v):
    near = -v * (
        1.0
        + v * (1 / 2) * (1.0 + v * (1 / 3) * (1.0 + v * (1 / 4) * (1.0 + v * (1 / 5) * (1.0 + v * (1 / 6)))))
    )
    return jnp.where(v > -0.3, near, 1.0 - jnp.exp(v))


def gelu_parts(v):
    cdf = 0.5 * (1.0 + lax.erf(v * 0.7071067811865476))
    pdf = 0.3989422804014327 * jnp.exp(-0.5 * v * v)
    return v * cdf, cdf + v * pdf


def shifted(values, by, fill, reverse):
    rows = lax.broadcasted_iota(jnp.int32, values.shape, 0)
    size = values.shape[0]
    if reverse:
        return jnp.where(rows < size - by, pltpu.roll(values, size - by, 0), fill)
    return jnp.where(rows >= by, pltpu.roll(values, by, 0), fill)


def behind(near, by):
    return near[8:24, :] if by == 0 else pltpu.roll(near, by, 0)[8:24, :]


def ahead(near, by):
    size = near.shape[0]
    return pltpu.roll(near, size - by, 0)[0 : size - 8, :]


def scan8(a, b, reverse):
    for by in (1, 2, 4):
        b = b + a * shifted(b, by, 0.0, reverse)
        a = a * shifted(a, by, 1.0, reverse)
    return a, b


def loop(count, body):
    def one(i, carry):
        body(i)
        return carry

    lax.fori_loop(0, count, one, 0)


def front_kernel(
    tokens, cotangent, packed, norms, own_rec, own_gate, own_up,
    x_out, n_out, xb_out, yb_out, c_out, rate_out, gin_out, a_out, m_out, h_out, hy_out, ext_out, hi_out, lo_out,
    cot, rec_out, w_gate, w_up,
    inv, gains, vec, state_in, total_a,
    full, normed, weights, params_all, norms_all,
    xb, yb, c, rate, gin, a, m, h, hy, ext, gate_hi, gate_lo, pre, prod,
    halo, mine, quad, rows, total, send, recv, done,
):
    z = lax.axis_index("z")
    me = lax.axis_index("yhi") * 2 + lax.axis_index("core")
    block = my_block()
    after, before = lax.rem(block + 1, 32), lax.rem(block + 31, 32)
    meet(
        line_devices()
        + [plane_device(after), plane_device(before)]
        + plane_neighbours()
        + z_others()
    )
    put = Sender(send, recv)
    keep = Keeper(done)
    params_all[me] = packed[...]
    tokens_in = token_gather(tokens, full, put, keep)
    plane = plane_gather(own_rec, weights, put, keep)
    step(tokens_in, plane)
    small = []
    for j in (1, 2, 3):
        small.append(put(norms, norms_all.at[z, me], quad_device(lax.rem(me + j, 4))))
    norms_all[z, me] = norms[...]
    gate_hi[...] = jnp.zeros((CH, 2 * CH), bf)
    gate_lo[...] = jnp.zeros((CH, 2 * CH), bf)
    step(plane, tokens_in)
    got(small)
    small = []
    for j in (1, 2, 3):
        small.append(put(norms_all.at[z], norms_all.at[z], {"z": lax.rem(z + j, 4)}))
    step(plane, tokens_in)
    got(small)
    for i in range(4):
        for j in range(4):
            gains[:, 128 * (4 * i + j) : 128 * (4 * i + j + 1)] = norms_all[i, j]
    step(plane)
    finish(tokens_in)
    keep(full, x_out)
    other = token_gather(cotangent, cot, put, keep)
    plane_a = plane_gather(own_gate, w_gate, put, keep)
    plane_b = plane_gather(own_up, w_up, put, keep)
    core, yhi = lax.axis_index("core"), lax.axis_index("yhi")
    own_params = params_all.at[me]
    near = put(own_params, own_params, {"core": 1 - core})
    across = put(own_params, own_params, {"yhi": 1 - yhi})
    step(plane, other, plane_a)

    def norm(i):
        r = pl.ds(pl.multiple_of(i * 16, 16), 16)
        values = full[r, :].astype(f32)
        mean = jnp.sum(values * values, axis=1, keepdims=True) * (1.0 / D)
        scale = lax.rsqrt(mean + EPS)
        inv[r, :] = jnp.broadcast_to(scale, (16, 128))
        normed[r, :] = (values * scale * gains[0:1, :]).astype(bf)

    loop(TOK // 16, norm)
    keep(normed, n_out)
    finish(plane)
    keep(weights, rec_out)
    across.wait_recv()
    peer_params = params_all.at[lax.rem(me + 2, 4)]
    passed = put(peer_params, peer_params, {"core": 1 - core})
    step(plane_a, other)
    for i, into in ((0, xb), (1, yb)):
        for at, width in ((0, 256), (256, 256), (512, 128)):
            into[:, at : at + width] = lax.dot_general(
                normed[...],
                weights[i, at : at + width, :],
                (((1,), (1,)), ((), ())),
                preferred_element_type=f32,
            )
        if i == 0:
            halo_out = pl.ds(TOK - 16, 16)
            hy[halo_out, :] = xb[halo_out, :].astype(bf)
            edge = put(hy.at[halo_out, :], halo, plane_device(after))
            step(plane_a, plane_b)
    keep(xb, xb_out)
    keep(yb, yb_out)
    step(other)

    def widen(i):
        r = pl.multiple_of(i * 16, 16)
        ext[pl.ds(pl.multiple_of(8 + r, 8), 16), :] = xb[pl.ds(r, 16), :].astype(bf).astype(f32)

    loop(TOK // 16, widen)
    got([near, passed])
    for i in range(4):
        there = HW * i
        vec[:, there : there + 128] = params_all[i, 2 * SQUARE : 2 * SQUARE + 16, :]
        vec[:, there + 128 : there + HW] = params_all[i, 2 * SQUARE + 16 : PACKED, 0:32]
        for k in (0, 1):
            top = SQUARE * k
            high, low = split(params_all[i, top : top + HW, :])
            over = CH * k + HW * i
            gate_hi[there : there + HW, over : over + 128] = high
            gate_lo[there : there + HW, over : over + 128] = low
            for j, (at, size) in enumerate(TAILS):
                high, low = split(params_all[i, top + HW : top + HW + size, 32 * j : 32 * j + 32])
                rows_here = slice(there + at, there + at + size)
                gate_hi[rows_here, over + 128 : over + HW] = high
                gate_lo[rows_here, over + 128 : over + HW] = low
    keep(gate_hi, hi_out)
    keep(gate_lo, lo_out)
    edge.wait_recv()
    ext[0:8, :] = jnp.where(block > 0, halo[8:16, :].astype(f32), 0.0)

    def conv(i):
        r = i * 16
        near = ext[pl.ds(pl.multiple_of(r, 16), 24), :]
        acc = vec[4:5, :] + vec[0:1, :] * near[8:24, :]
        for k in (1, 2, 3):
            acc = acc + vec[k : k + 1, :] * behind(near, k)
        c[pl.ds(pl.multiple_of(r, 16), 16), :] = acc

    loop(TOK // 16, conv)
    keep(ext, ext_out)
    keep(c, c_out)
    step(plane_b)

    def gates(i):
        r = pl.ds(pl.multiple_of(i * 128, 128), 128)
        pre[r, :] = dot3(split(c[r, :]), (gate_hi[...], gate_lo[...]), ((1,), (0,)))

    loop(TOK // 128, gates)
    step(plane_a, other, plane_b)

    def point(i, carry):
        prod_in, state = carry
        r = pl.ds(pl.multiple_of(i * 8, 8), 8)
        rr = jax.nn.sigmoid(pre[r, 0:CH] + vec[5:6, :])
        gg = jax.nn.sigmoid(pre[r, CH:] + vec[6:7, :])
        log_a = -8.0 * rr * vec[7:8, :]
        aa = jnp.exp(log_a)
        mm = jnp.sqrt(minus_expm1(2.0 * log_a))
        rate[r, :] = rr
        gin[r, :] = gg
        a[r, :] = aa
        m[r, :] = mm
        pa, hb = scan8(aa, mm * gg * c[r, :], False)
        hb = hb + pa * state
        pa = pa * prod_in
        h[r, :] = hb
        prod[r, :] = pa
        return pa[7:8, :], hb[7:8, :]

    last = (jnp.ones((1, CH), f32), jnp.zeros((1, CH), f32))
    last = lax.fori_loop(0, TOK // 16, point, last)
    step(plane_a, plane_b)
    last = lax.fori_loop(TOK // 16, TOK // 8, point, last)
    for source, target in ((rate, rate_out), (gin, gin_out), (a, a_out), (m, m_out)):
        keep(source, target)
    mine[...] = jnp.zeros((8, CH), f32)
    total[...] = jnp.zeros((8, CH), f32)
    mine[0:1, :] = last[0]
    mine[1:2, :] = last[1]
    came = line_prefix(mine, quad, rows, total, put, False)
    state_in[...] = jnp.broadcast_to(came, (8, CH))
    total_a[...] = jnp.broadcast_to(last[0], (8, CH))
    step(plane_b)
    finish(plane_a, other)
    edge.wait_send()

    def complete(i):
        r = pl.ds(pl.multiple_of(i * 16, 16), 16)
        hh = h[r, :] + prod[r, :] * came
        h[r, :] = hh
        hy[r, :] = (hh * gelu_parts(yb[r, :])[0]).astype(bf)

    loop(TOK // 16, complete)
    keep(h, h_out)
    keep(hy, hy_out)

    finish(plane_b)
    put.drain(skip=edge)
    keep.drain()


def front(*operands):
    wide = shape((TOK, CH), f32)
    rows = shape((TOK, D), bf)
    mlp = shape((1536, D), bf)
    gate = shape((CH, 2 * CH), bf)
    out = (
        rows, rows, wide, wide, wide, wide, wide, wide, wide, wide,
        shape((TOK, CH), bf), shape((TOK + 8, CH), f32), gate, gate,
        rows, shape((3, CH, D), bf), mlp, mlp,
    )
    little = (
        shape((TOK, 128), f32), shape((8, D), f32), shape((16, CH), f32),
        shape((8, CH), f32), shape((8, CH), f32),
    )
    tall = pltpu.VMEM((TOK, CH), f32)
    return pl.pallas_call(
        front_kernel,
        out_shape=out + little,
        in_specs=[VMEM] * 4 + [ANY] * 3,
        out_specs=[ANY] * len(out) + [VMEM] * len(little),
        scratch_shapes=[
            pltpu.VMEM((TOK, D), bf),
            pltpu.VMEM((TOK, D), bf),
            pltpu.VMEM((3, CH, D), bf),
            pltpu.VMEM((4, PACKED, 128), f32),
            pltpu.VMEM((4, 4, 8, 128), f32),
            tall, tall, tall, tall, tall, tall, tall, tall,
            pltpu.VMEM((TOK, CH), bf),
            pltpu.VMEM((TOK + 8, CH), f32),
            pltpu.VMEM((CH, 2 * CH), bf),
            pltpu.VMEM((CH, 2 * CH), bf),
            pltpu.VMEM((TOK, 2 * CH), f32),
            tall,
            pltpu.VMEM((16, CH), bf),
            pltpu.VMEM((8, CH), f32),
            pltpu.VMEM((4, 8, CH), f32),
            pltpu.VMEM((8, 8, CH), f32),
            pltpu.VMEM((8, CH), f32),
        ]
        + semaphores(18 + 9 + 11 + 3 * GATHER_COPIES)
        + [pltpu.SemaphoreType.DMA((26,))],
        compiler_params=params(0),
        name="front",
    )(*operands)


def backward_kernel(
    dhy_in, yb_in, hi_in, lo_in, vec, c_in, rate_in, gin_in, a_in, m_in, h_in, ext_in, state_in, total_a,
    mlp_in, zown_in, down, gate,
    dxb, dyb, blocks, block_out, down_sum, gate_sum,
    e, apad, hpad, q, prod, pri, halo, mine, quad, rows, total, own, low, came_z, sent_z,
    yb, gate_hi, gate_lo, c, rate, gin, m, ext, mlp_part, z_own, dgate, sums, *rest,
):
    dc = q
    block = my_block()
    after, before = lax.rem(block + 1, 32), lax.rem(block + 31, 32)
    send, recv, done = rest[2 * SUM_SCRATCH :]
    keep = Keeper(done)
    load_mlp = keep(mlp_in, mlp_part)
    load_first = [
        keep(dhy_in, e),
        keep(yb_in, yb),
        keep(h_in, hpad.at[pl.ds(8, TOK), :]),
        keep(a_in, apad.at[pl.ds(0, TOK), :]),
    ]
    load_point = [keep(*pair) for pair in ((rate_in, rate), (gin_in, gin), (m_in, m), (c_in, c))]
    load_rest = [keep(*pair) for pair in ((hi_in, gate_hi), (lo_in, gate_lo), (ext_in, ext), (zown_in, z_own))]
    meet(
        line_devices()
        + [plane_device(after), plane_device(before)]
        + plane_neighbours()
        + z_others()
    )
    put = Sender(send, recv)
    whole = ring_sum(mlp_part, own, came_z, sent_z, put)
    plane = plane_sum([down], down_sum, rest[:SUM_SCRATCH], put, keep)
    plane_b = plane_sum([gate], gate_sum, rest[SUM_SCRATCH : 2 * SUM_SCRATCH], put, keep)
    keep.wait(load_mlp)
    step(whole, plane, plane_b)
    for copy in load_first:
        keep.wait(copy)

    def direct(i):
        r = pl.ds(pl.multiple_of(i * 16, 16), 16)
        value, slope = gelu_parts(yb[r, :])
        grad = e[r, :]
        hh = hpad[pl.ds(pl.multiple_of(i * 16 + 8, 8), 16), :]
        e[r, :] = grad * value
        dyb[r, :] = (grad * hh * slope).astype(bf)

    loop(TOK // 16, direct)
    apad[TOK : TOK + 8, :] = jnp.ones((8, CH), f32)
    hpad[0:8, :] = state_in[...]
    step(whole, plane)

    def adjoint(i, carry):
        prod_in, state = carry
        r0 = TOK - 8 - i * 8
        r = pl.ds(pl.multiple_of(r0, 8), 8)
        next_a = ahead(apad[pl.ds(pl.multiple_of(r0, 8), 16), :], 1)
        pa, qb = scan8(next_a, e[r, :], True)
        qb = qb + pa * state
        pa = pa * prod_in
        q[r, :] = qb
        prod[r, :] = pa
        return pa[0:1, :], qb[0:1, :]

    last = (jnp.ones((1, CH), f32), jnp.zeros((1, CH), f32))
    last = lax.fori_loop(0, TOK // 8, adjoint, last)
    step(plane_b, plane)
    mine[...] = jnp.zeros((8, CH), f32)
    total[...] = jnp.zeros((8, CH), f32)
    mine[0:1, :] = total_a[0:1, :]
    mine[1:2, :] = apad[0:1, :] * last[1]
    came = line_prefix(mine, quad, rows, total, put, True)
    step(plane)
    for copy in load_point:
        keep.wait(copy)

    def point(i, carry):
        s_rate, s_input, s_decay = carry
        r = pl.ds(pl.multiple_of(i * 8, 8), 8)
        qq = q[r, :] + prod[r, :] * came
        aa, rr, gg, mm, cc = apad[r, :], rate[r, :], gin[r, :], m[r, :], c[r, :]
        earlier = pltpu.roll(hpad[pl.ds(pl.multiple_of(i * 8, 8), 16), :], 1, 0)[8:16, :]
        grad_log = aa * (qq * earlier - qq * gg * cc * aa / mm)
        pr = -8.0 * vec[7:8, :] * grad_log * rr * (1.0 - rr)
        pi = qq * mm * cc * gg * (1.0 - gg)
        pri[r, 0:CH] = pr
        pri[r, CH:] = pi
        dc[r, :] = qq * mm * gg
        return s_rate + pr, s_input + pi, s_decay + 8.0 * rr * vec[8:9, :] * grad_log

    none = jnp.zeros((8, CH), f32)
    so_far = lax.fori_loop(0, TOK // 16, point, (none, none, none))
    step(plane_b)
    s_rate, s_input, s_decay = lax.fori_loop(TOK // 16, TOK // 8, point, so_far)
    step(plane)

    for copy in load_rest:
        keep.wait(copy)

    def spread(i):
        r = pl.ds(pl.multiple_of(i * 128, 128), 128)
        dc[r, :] = dc[r, :] + dot3(split(pri[r, :]), (gate_hi[...], gate_lo[...]), ((1,), (1,)))

    loop(TOK // 128, spread)
    edge = put(dc.at[pl.ds(0, 8), :], halo, plane_device(before))
    finish(whole)
    low[...] = (own[...] + z_own[...]).astype(bf)
    back, kept = quad_scatter(low, block_out, put, keep)
    step(plane_b)
    dgate[...] = dot3(split(c[...]), split(pri[...]), ((0,), (0,)))
    finish(plane)
    step(plane_b)
    edge.wait_recv()
    dc[TOK : TOK + 8, :] = jnp.where(block < 31, halo[...], 0.0)

    def taps(i, carry):
        r = i * 16
        here = pl.ds(pl.multiple_of(r, 16), 16)
        later = dc[pl.ds(pl.multiple_of(r, 16), 24), :]
        near = ext[pl.ds(pl.multiple_of(r, 16), 24), :]
        dd = later[0:16, :]
        out = vec[0:1, :] * dd
        for k in (1, 2, 3):
            out = out + vec[k : k + 1, :] * ahead(later, k)
        dxb[here, :] = out.astype(bf)

        def fold(v):
            return v[0:8, :] + v[8:16, :]

        new = [carry[0] + fold(dd)]
        for k in range(4):
            new.append(carry[1 + k] + fold(dd * behind(near, k)))
        return tuple(new)

    s_bias, *s_taps = lax.fori_loop(0, TOK // 16, taps, (none,) * 5)

    def place_sum(row, value):
        sums[row : row + 1, :] = jnp.sum(value, axis=0, keepdims=True)

    for k in range(4):
        place_sum(k, s_taps[k])
    place_sum(4, s_bias)
    place_sum(5, s_rate)
    place_sum(6, s_input)
    place_sum(7, s_decay)
    for i in range(4):
        there = HW * i
        for k in (0, 1):
            top, over = SQUARE * k, CH * k + HW * i
            blocks[i, top : top + HW, :] = dgate[there : there + HW, over : over + 128]
            for j, (at, size) in enumerate(TAILS):
                blocks[i, top + HW : top + HW + size, 32 * j : 32 * j + 32] = dgate[
                    there + at : there + at + size, over + 128 : over + HW
                ]
            blocks[i, top + HW + 16 : top + SQUARE, 96:128] = jnp.zeros((32, 32), f32)
        blocks[i, 2 * SQUARE :, :] = jnp.zeros((32, 128), f32)
        blocks[i, 2 * SQUARE : 2 * SQUARE + 8, :] = sums[:, there : there + 128]
        blocks[i, 2 * SQUARE + 16 : 2 * SQUARE + 24, 0:32] = sums[:, there + 128 : there + HW]
    finish(plane, plane_b)
    got(back)
    keep.wait(kept)
    put.drain()
    keep.drain()


def backward_scan(*operands):
    r = operands[-1].shape[0] // 4
    tall = pltpu.VMEM((TOK, CH), f32)
    return pl.pallas_call(
        backward_kernel,
        out_shape=(
            shape((TOK, CH), bf),
            shape((TOK, CH), bf),
            shape((4, PACKED, 128), f32),
            shape((4 * TOK, 128), bf),
            shape((r, 256), f32),
            shape((r, 256), f32),
        ),
        in_specs=[ANY] * 4 + [VMEM] + [ANY] * 7 + [VMEM] * 2 + [ANY] * 4,
        out_specs=[VMEM] * 6,
        scratch_shapes=[
            tall,
            pltpu.VMEM((TOK + 8, CH), f32),
            pltpu.VMEM((TOK + 8, CH), f32),
            pltpu.VMEM((TOK + 8, CH), f32),
            tall,
            pltpu.VMEM((TOK, 2 * CH), f32),
            pltpu.VMEM((8, CH), f32),
            pltpu.VMEM((8, CH), f32),
            pltpu.VMEM((4, 8, CH), f32),
            pltpu.VMEM((8, 8, CH), f32),
            pltpu.VMEM((8, CH), f32),
            pltpu.VMEM((TOK, 512), f32),
            pltpu.VMEM((TOK, 512), bf),
        ]
        + ring_scratch()
        + [
            tall,
            pltpu.VMEM((CH, 2 * CH), bf),
            pltpu.VMEM((CH, 2 * CH), bf),
            tall,
            tall,
            tall,
            tall,
            pltpu.VMEM((TOK + 8, CH), f32),
            pltpu.VMEM((TOK, D), bf),
            pltpu.VMEM((TOK, 512), f32),
            pltpu.VMEM((CH, 2 * CH), f32),
            pltpu.VMEM((8, CH), f32),
        ]
        + sum_scratch(r)
        + sum_scratch(r)
        + semaphores(11 + 6 + 3 + 2 * SUM_COPIES)
        + [pltpu.SemaphoreType.DMA((14 + 2 * SUM_KEEPS,))],
        compiler_params=params(4),
        name="backward_scan",
    )(*operands)


def per_device(
    block_in, cotangent, norm_one, rec_in, rec_gate, conv_weight, conv_bias,
    rate_weight, rate_bias, input_weight, input_bias, decay_code, rec_out,
    norm_two, mlp_gate, mlp_up, mlp_down,
):
    decay = decay_code.astype(f32) / 256.0
    vectors = jnp.concatenate(
        [
            conv_weight,
            conv_bias[None],
            rate_bias[None],
            input_bias[None],
            jax.nn.softplus(-decay)[None],
            jax.nn.sigmoid(-decay)[None],
            jnp.zeros((7, HW), f32),
        ],
        axis=0,
    )
    packed = jnp.concatenate(
        [
            pack_square(rate_weight[0]),
            pack_square(input_weight[0]),
            vectors[:, :128],
            jnp.pad(vectors[:, 128:], ((0, 0), (0, 96))),
        ],
        axis=0,
    )
    norms = jnp.concatenate([norm_one[None], norm_two[None], jnp.zeros((6, 128), f32)], axis=0)
    (
        x_full, n_one, xb, yb, c, rate, gin, a, m, h, hy, ext, gate_hi, gate_lo,
        cot_full, w_rec, w_gate, w_up,
        inv_one, gains, vec, state_in, total_a,
    ) = front(
        block_in, cotangent, packed, norms,
        jnp.stack([rec_in.T, rec_gate.T, rec_out]), mlp_gate.T, mlp_up.T,
    )
    z_own, dz_own, dhy, mlp_part, part_out, part_down, part_gate, part_up, gain_two_sums = middle(
        hy, w_rec, x_full, cot_full, w_gate, w_up, mlp_down, gains
    )
    dxb, dyb, blocks, block_out, grad_down, grad_gate = backward_scan(
        dhy, yb, gate_hi, gate_lo, vec, c, rate, gin, a, m, h, ext, state_in, total_a,
        mlp_part, z_own, part_down, part_gate,
    )
    grad_in, grad_rec_in, grad_rec_gate, grad_out, grad_up, grad_rate, grad_input, vector_grads, gain_sums = tail(
        dxb, dyb, xb, yb, w_rec, x_full, n_one, dz_own, part_out, part_up,
        inv_one, gains, gain_two_sums, blocks,
    )
    return (
        block_out,
        grad_in,
        gain_sums[0],
        grad_rec_in,
        grad_rec_gate,
        vector_grads[0:4],
        vector_grads[4],
        grad_rate[None],
        vector_grads[5],
        grad_input[None],
        vector_grads[6],
        vector_grads[7],
        grad_out,
        gain_sums[1],
        grad_gate.T,
        grad_up,
        grad_down,
    )


def solution(mesh):
    fine = Mesh(mesh.devices.reshape(2, 4, 4, 2, 2), ("ylo", "x", "z", "yhi", "core"))
    both = P(SEQ, HEAD)
    swap = P(HEAD, SEQ)
    vector = P(HEAD)
    stack = P(HEAD, None, None)
    taps = P(None, HEAD)
    return jax.shard_map(
        per_device,
        mesh=fine,
        in_specs=(
            both, both, vector, both, both, taps, vector, stack, vector, stack, vector, vector,
            swap, vector, both, both, swap,
        ),
        out_specs=(
            both, both, vector, both, both, taps, vector, stack, vector, stack, vector, vector,
            swap, vector, both, both, swap,
        ),
        check_vma=False,
    )
```

```python
import jax
import jax.numpy as jnp
from jax import lax
from jax.experimental import pallas as pl
from jax.experimental.pallas import tpu as pltpu
from jax.sharding import Mesh, PartitionSpec as P

D = 2048
CONV = 4
EPS = 1e-06
TOK = 512
CH = 640
HW = 160
TAILS = ((0, 48), (48, 48), (96, 48), (144, 16))
SQUARE = 208
PACKED = 2 * SQUARE + 32
MESH = pl.DeviceIdType.MESH
SEQ = ("ylo", "x")
HEAD = ("z", "yhi", "core")
QUAD = ("yhi", "core")
PLANE = ("ylo", "x", "yhi", "core")
bf = jnp.bfloat16
f32 = jnp.float32
VMEM = pl.BlockSpec(memory_space=pltpu.VMEM)
ANY = pl.BlockSpec(memory_space=pl.ANY)


def shape(dims, dtype):
    return jax.ShapeDtypeStruct(dims, dtype)


def params(cid):
    return pltpu.CompilerParams(
        collective_id=cid, has_side_effects=True, vmem_limit_bytes=60 * 2**20
    )


def quad_device(index):
    return {"yhi": index // 2, "core": lax.rem(index, 2)}


def plane_device(block):
    return {
        "ylo": block // 16,
        "x": lax.rem(block // 4, 4),
        "yhi": lax.rem(block // 2, 2),
        "core": lax.rem(block, 2),
    }


def meet(devices):
    barrier = pltpu.get_barrier_semaphore()
    for device in devices:
        pl.semaphore_signal(barrier, inc=1, device_id=device, device_id_type=MESH)
    pl.semaphore_wait(barrier, len(devices))


def place():
    ylo, x, yhi, core = (lax.axis_index(n) for n in ("ylo", "x", "yhi", "core"))
    return ylo, x, yhi, core

def x_device(i):
    return {"x": i}

def y_device(i):
    return {"yhi": i // 2, "ylo": lax.rem(i, 2)}

def around(i):
    return lax.rem(i + 1, 4), lax.rem(i + 3, 4), lax.rem(i + 2, 4)

def plane_neighbours():
    ylo, x, yhi, core = place()
    y = yhi * 2 + ylo
    xr, xl, _ = around(x)
    yr, yl, _ = around(y)
    return [x_device(xr), x_device(xl), y_device(yr), y_device(yl), {"core": 1 - core}]

class Sender:
    def __init__(self, send, recv, base=0):
        self.send, self.recv, self.base, self.all = send, recv, base, []

    def __call__(self, source, target, device):
        i = self.base + len(self.all)
        copy = pltpu.make_async_remote_copy(
            src_ref=source,
            dst_ref=target,
            send_sem=self.send.at[i],
            recv_sem=self.recv.at[i],
            device_id=device,
            device_id_type=MESH,
        )
        copy.start()
        self.all.append(copy)
        return copy

    def drain(self, skip=None):
        for copy in self.all:
            if copy is not skip:
                copy.wait_send()


class Keeper:
    def __init__(self, done):
        self.done, self.count, self.open = done, 0, []

    def __call__(self, source, target):
        copy = pltpu.make_async_copy(source, target, self.done.at[self.count])
        copy.start()
        self.count += 1
        self.open.append(copy)
        return copy

    def wait(self, copy):
        self.open = [c for c in self.open if c is not copy]
        copy.wait()

    def drain(self):
        for copy in self.open:
            copy.wait()


def semaphores(count):
    return [pltpu.SemaphoreType.DMA((count,)), pltpu.SemaphoreType.DMA((count,))]


def got(copies):
    for copy in copies:
        copy.wait_recv()


def step(*plans):
    for plan in plans:
        next(plan, None)


def finish(*plans):
    for plan in plans:
        for _ in plan:
            pass


def z_columns(block):
    return pl.ds(pl.multiple_of(block * 512, 512), 512)


def ring_gather(full, put):
    z = lax.axis_index("z")
    right, left, _ = around(z)
    half = full.shape[0] // 2

    def start(row, block, to):
        part = full.at[pl.ds(row, half), z_columns(block)]
        return put(part, part, {"z": to})

    c0 = start(0, z, right)
    c1 = start(half, z, left)
    c2 = start(half, z, right)
    c3 = start(0, z, left)
    yield
    c0.wait_recv()
    c4 = start(0, left, right)
    c1.wait_recv()
    c5 = start(half, right, left)
    yield
    got([c2, c3, c4, c5])


def ring_sum(part, out, came, sent, put, produce=lambda block: None):
    z = lax.axis_index("z")
    right, left, far = around(z)
    half = part.shape[0] // 2
    lo, hi = pl.ds(0, half), pl.ds(half, half)
    cols = z_columns

    def start(i, source, to):
        return put(source, came.at[i], {"z": to})

    produce(far)
    c0 = start(0, part.at[lo, cols(far)], right)
    c1 = start(1, part.at[hi, cols(far)], left)
    produce(right)
    c2 = start(2, part.at[hi, cols(right)], right)
    produce(left)
    c3 = start(3, part.at[lo, cols(left)], left)
    produce(z)
    yield
    c0.wait_recv()
    sent[0] = came[0] + part[lo, cols(right)]
    c4 = start(4, sent.at[0], right)
    c1.wait_recv()
    sent[1] = came[1] + part[hi, cols(left)]
    c5 = start(5, sent.at[1], left)
    yield
    got([c3, c4])
    out[lo, :] = part[lo, cols(z)].astype(f32) + came[3].astype(f32) + came[4].astype(f32)
    got([c2, c5])
    out[hi, :] = part[hi, cols(z)].astype(f32) + came[2].astype(f32) + came[5].astype(f32)


def ring_scratch():
    return [pltpu.VMEM((6, TOK // 2, 512), bf), pltpu.VMEM((2, TOK // 2, 512), bf)]


def z_others():
    z = lax.axis_index("z")
    return [{"z": lax.rem(z + j, 4)} for j in (1, 2, 3)]


def quad_others():
    me = lax.axis_index("yhi") * 2 + lax.axis_index("core")
    return [quad_device(lax.rem(me + j, 4)) for j in (1, 2, 3)]


def quad_gather(tokens, full, put, keep):
    z = lax.axis_index("z")
    me = lax.axis_index("yhi") * 2 + lax.axis_index("core")
    mine = pl.ds(pl.multiple_of(z * 512 + me * 128, 128), 128)
    copies = []
    for j in (1, 2, 3):
        peer = lax.rem(me + j, 4)
        source = tokens.at[pl.ds(pl.multiple_of(peer * TOK, TOK), TOK), :]
        copies.append(put(source, full.at[:, mine], quad_device(peer)))
    own = keep(tokens.at[pl.ds(pl.multiple_of(me * TOK, TOK), TOK), :], full.at[:, mine])
    return copies, own


def token_gather(tokens, full, put, keep):
    copies, own = quad_gather(tokens, full, put, keep)
    yield
    got(copies)
    keep.wait(own)
    yield from ring_gather(full, put)


def quad_scatter(own, tokens, put, keep):
    me = lax.axis_index("yhi") * 2 + lax.axis_index("core")
    rows = pl.ds(pl.multiple_of(me * TOK, TOK), TOK)
    copies = []
    for j in (1, 2, 3):
        peer = lax.rem(me + j, 4)
        source = own.at[:, pl.ds(pl.multiple_of(peer * 128, 128), 128)]
        copies.append(put(source, tokens.at[rows, :], quad_device(peer)))
    mine = keep(own.at[:, pl.ds(pl.multiple_of(me * 128, 128), 128)], tokens.at[rows, :])
    return copies, mine


GATHER_COPIES = 48
SUM_COPIES = 36
SUM_KEEPS = 8


HALF = TOK // 2
UNIT = 256


CUTS = ((0, 256), (256, 256), (512, 128))


def rec_grad(left, right, into):
    for at, width in CUTS:
        for k in range(4):
            cols = slice(512 * k, 512 * k + 512)
            into[at : at + width, cols] = lax.dot_general(
                left[:, at : at + width], right[:, cols], (((0,), (0,)), ((), ())), preferred_element_type=f32
            ).astype(bf)


def middle_kernel(
    hy_in, rec_in, x_in, cot_in, gate_in, up_in, own_down, gains,
    zown_out, dz_out, dhy_out, mlp_out, out_grad, down_grad, gate_grad, up_grad, gain_sums,
    hy, w_out, x, cot, w_gate, w_up, w_down, normed, mixed, part, part_two, back, act, dg, du, mlp,
    own_one, own_two, inv, inner, dhy, *rest,
):
    rings, (send, recv, done) = rest[:8], rest[8:]
    z = lax.axis_index("z")
    keep = Keeper(done)
    load_mix = [keep(hy_in, hy), keep(rec_in.at[2], w_out)]
    load_norm = [keep(x_in, x)]
    load_mlp = [keep(gate_in, w_gate), keep(up_in, w_up), keep(cot_in, cot)]
    meet(z_others() + plane_neighbours())
    put = Sender(send, recv)
    plane = plane_gather(own_down, w_down, put, keep)
    step(plane)
    puts = [Sender(send, recv, GATHER_COPIES + 12 * i) for i in range(4)]

    def rows_of(half):
        return pl.ds(HALF * half, HALF)

    def view(ref, half):
        return ref.at[rows_of(half), :]

    def wide(ref, rows, times):
        return jnp.concatenate([ref[rows, :]] * times, axis=1)

    def mix_block(half):
        def produce(at):
            part[rows_of(half), z_columns(at)] = jnp.dot(
                hy[rows_of(half), :], w_out[:, z_columns(at)], preferred_element_type=f32
            ).astype(bf)

        return produce

    def sums(i, half, source, own, produce):
        return ring_sum(
            view(source, half), view(own, half), rings[2 * i], rings[2 * i + 1], puts[i], produce
        )

    def spread(i, half, full, own):
        full[rows_of(half), z_columns(z)] = own[rows_of(half), :].astype(bf)
        return ring_gather(view(full, half), puts[i])

    def norm(half):
        def body(i):
            r = pl.ds(pl.multiple_of(HALF * half + i * 16, 16), 16)
            values = x[r, :].astype(f32) + mixed[r, :].astype(f32)
            mean = jnp.sum(values * values, axis=1, keepdims=True) * (1.0 / D)
            scale = lax.rsqrt(mean + EPS)
            inv[r, :] = jnp.broadcast_to(scale, (16, 128))
            normed[r, :] = (values * scale * gains[1:2, :]).astype(bf)

        loop(HALF // 16, body)

    def hidden(half, first, count):
        r = rows_of(half)

        def body(j):
            at = pl.ds(pl.multiple_of((first + j) * UNIT, UNIT), UNIT)

            def against(left, right):
                return lax.dot_general(
                    left, right[at, :], (((1,), (1,)), ((), ())), preferred_element_type=f32
                )

            g = against(normed[r, :], w_gate)
            u = against(normed[r, :], w_up)
            da = against(cot[r, :], w_down)
            value, slope = gelu_parts(g)
            act[r, at] = (value * u).astype(bf)
            low_g = (da * u * slope).astype(bf)
            low_u = (da * value).astype(bf)
            dg[r, at] = low_g
            du[r, at] = low_u
            t = low_g.astype(f32) * g + low_u.astype(f32) * u
            inner[r, :] = inner[r, :] + (t[:, :128] + t[:, 128:])

        loop(count, body)

    def close(half):
        r = rows_of(half)
        total = jnp.sum(inner[r, :], axis=1, keepdims=True) * (1.0 / D)
        inner[r, :] = inv[r, :] * inv[r, :] * total

    def back_block(half):
        r = rows_of(half)

        def produce(at):
            cols = z_columns(at)
            dn = jnp.dot(dg[r, :], w_gate[:, cols], preferred_element_type=f32)
            dn = dn + jnp.dot(du[r, :], w_up[:, cols], preferred_element_type=f32)
            values = x[r, cols].astype(f32) + mixed[r, cols].astype(f32)
            scaled = dn * wide(inv, r, 4)
            part_two[r, cols] = (scaled * gains[1:2, cols] - values * wide(inner, r, 4)).astype(bf)
            gain_sums[:, cols] = gain_sums[:, cols] + jnp.sum(
                (scaled * values).reshape(HALF // 8, 8, 512), axis=0
            )

        return produce

    def mlp_blocks():
        for at in range(4):
            cols = slice(512 * at, 512 * at + 512)
            mlp[:, cols] = jnp.dot(act[...], w_down[:, cols], preferred_element_type=f32).astype(bf)

    def weight_grad(left, right, into, target):
        def body(j):
            at = pl.ds(pl.multiple_of(j * UNIT, UNIT), UNIT)
            for k in range(4):
                cols = slice(512 * k, 512 * k + 512)
                into[at, cols] = lax.dot_general(
                    left[:, at], right[:, cols], (((0,), (0,)), ((), ())), preferred_element_type=f32
                ).astype(bf)

        loop(1536 // UNIT, body)
        keep(into, target)

    def add_own(half, whole, own):
        r = rows_of(half)
        own[r, :] = own[r, :] + whole[r, z_columns(z)].astype(f32)

    def add_cotangent(half):
        def body(i):
            r = pl.ds(pl.multiple_of(HALF * half + i * 16, 16), 16)
            back[r, :] = cot[r, :] + back[r, :]

        loop(HALF // 16, body)

    for copy in load_mix:
        keep.wait(copy)
    inner[...] = jnp.zeros((TOK, 128), f32)
    gain_sums[...] = jnp.zeros((8, D), f32)
    sum_a = sums(0, 0, part, own_one, mix_block(0))
    sum_b = sums(1, 1, part, own_one, mix_block(1))
    step(sum_a, sum_a)
    step(plane, sum_b)
    finish(sum_a)
    spread_a = spread(0, 0, mixed, own_one)
    step(spread_a, sum_b, plane, spread_a)
    finish(sum_b)
    spread_b = spread(1, 1, mixed, own_one)
    step(spread_b)
    finish(spread_a)
    for copy in load_norm:
        keep.wait(copy)
    add_own(0, x, own_one)
    norm(0)
    step(spread_b, plane)
    for copy in load_mlp:
        keep.wait(copy)
    finish(plane)
    hidden(0, 0, 3)
    finish(spread_b)
    add_own(1, x, own_one)
    keep(own_one, zown_out)
    hidden(0, 3, 3)
    close(0)
    total_a = sums(2, 0, part_two, own_two, back_block(0))
    step(total_a)
    norm(1)
    step(total_a)
    hidden(1, 0, 3)
    finish(total_a)
    back_a = spread(2, 0, back, own_two)
    step(back_a)
    hidden(1, 3, 2)
    step(back_a)
    hidden(1, 5, 1)
    close(1)
    total_b = sums(3, 1, part_two, own_two, back_block(1))
    step(total_b)
    finish(back_a)
    puts[2].drain()
    add_cotangent(0)
    add_own(0, cot, own_two)
    step(total_b)
    mlp_blocks()
    keep(mlp, mlp_out)
    put.drain()
    finish(total_b)
    back_b = spread(3, 1, back, own_two)
    step(back_b)
    weight_grad(act, cot, w_down, down_grad)
    step(back_b)
    weight_grad(dg, normed, w_gate, gate_grad)
    weight_grad(du, normed, w_up, up_grad)
    finish(back_b)
    puts[3].drain()
    add_cotangent(1)
    for at, width in CUTS:
        dhy[:, at : at + width] = lax.dot_general(
            back[...], w_out[at : at + width, :], (((1,), (1,)), ((), ())), preferred_element_type=f32
        )
    keep(dhy, dhy_out)
    add_own(1, cot, own_two)
    keep(own_two, dz_out)
    rec_grad(hy, back, w_out)
    keep(w_out, out_grad)
    puts[0].drain()
    puts[1].drain()
    keep.drain()


def middle(*operands):
    mlp = shape((1536, D), bf)
    rows = shape((TOK, D), bf)
    own = shape((TOK, 512), f32)
    row_scratch = pltpu.VMEM((TOK, D), bf)
    weight = pltpu.VMEM((1536, D), bf)
    unit = pltpu.VMEM((TOK, 1536), bf)
    return pl.pallas_call(
        middle_kernel,
        out_shape=(
            own, own, shape((TOK, CH), f32), rows, shape((CH, D), bf), mlp, mlp, mlp, shape((8, D), f32),
        ),
        in_specs=[ANY] * 7 + [VMEM],
        out_specs=[ANY] * 8 + [VMEM],
        scratch_shapes=[
            pltpu.VMEM((TOK, CH), bf),
            pltpu.VMEM((CH, D), bf),
            row_scratch,
            row_scratch,
            weight,
            weight,
            weight,
            row_scratch,
            row_scratch,
            row_scratch,
            row_scratch,
            row_scratch,
            unit,
            unit,
            unit,
            row_scratch,
            pltpu.VMEM((TOK, 512), f32),
            pltpu.VMEM((TOK, 512), f32),
            pltpu.VMEM((TOK, 128), f32),
            pltpu.VMEM((TOK, 128), f32),
            pltpu.VMEM((TOK, CH), f32),
        ]
        + 4 * [pltpu.VMEM((6, HALF // 2, 512), bf), pltpu.VMEM((2, HALF // 2, 512), bf)]
        + semaphores(GATHER_COPIES + 48)
        + [pltpu.SemaphoreType.DMA((16,))],
        compiler_params=params(3),
        name="middle",
    )(*operands)


def cut(r):
    a = (r // 32) * 16
    a1 = ((a // 16 + 1) // 2) * 16
    b1 = (((r - a) // 16 + 1) // 2) * 16
    return a, a1, b1

def plane_gather(own, full, put, keep):
    r = own.shape[-2]
    lead = (slice(None),) * (len(own.shape) - 2)
    ylo, x, yhi, core = place()
    y = yhi * 2 + ylo
    xr, xl, xf = around(x)
    yr, yl, yf = around(y)
    a, a1, b1 = cut(r)
    top, bottom = (0, a), (a, r - a)
    top1, top2 = (0, a1), (a1, a - a1)
    bot1, bot2 = (a, b1), (a + b1, r - a - b1)

    def span(quarter, rows):
        return pl.ds(pl.multiple_of(quarter * r + rows[0], 16), rows[1])

    sib = {"core": 1 - core}
    def cols(lo, xx):
        return pl.ds(pl.multiple_of(lo * 1024 + xx * 256, 256), 256)
    def one(rows, yy, xx):
        return full.at[lead + (span((yy // 2) * 2 + core, rows), cols(lax.rem(yy, 2), xx))]
    def row(rows, yy):
        return full.at[lead + (span((yy // 2) * 2 + core, rows), pl.ds(pl.multiple_of(lax.rem(yy, 2) * 1024, 1024), 1024))]
    kept = keep(own, one((0, r), y, x))
    ha, hb = own.at[lead + (pl.ds(*top),)], own.at[lead + (pl.ds(*bottom),)]
    p = [put(ha, one(top, y, x), x_device(xr)), put(ha, one(top, y, x), x_device(xl)),
         put(hb, one(bottom, y, x), y_device(yr)), put(hb, one(bottom, y, x), y_device(yl))]
    yield
    got(p)
    keep.wait(kept)
    p = [put(one(top1, y, xl), one(top1, y, xl), x_device(xr)), put(one(top2, y, xr), one(top2, y, xr), x_device(xl)),
         put(one(bot1, yl, x), one(bot1, yl, x), y_device(yr)), put(one(bot2, yr, x), one(bot2, yr, x), y_device(yl))]
    yield
    got(p)
    def pieces(rows, xx):
        out = []
        for lo in (0, 1):
            for hi in (0, 1):
                out.append(full.at[lead + (span(2 * hi + core, rows), cols(lo, xx))])
        return out
    def send_row(rows, yy, device):
        return [put(row(rows, yy), row(rows, yy), device)]
    def send_col(rows, xx, device):
        return [put(s, s, device) for s in pieces(rows, xx)]
    p = send_row(top, y, y_device(yr)) + send_row(top, y, y_device(yl))
    p += send_col(bottom, x, x_device(xr)) + send_col(bottom, x, x_device(xl))
    s = send_row(top, y, sib) + send_col(bottom, x, sib)
    yield
    got(p)
    p = send_row(top1, yl, y_device(yr)) + send_row(top2, yr, y_device(yl))
    p += send_col(bot1, xl, x_device(xr)) + send_col(bot2, xr, x_device(xl))
    s += send_row(top, yl, sib) + send_row(top, yr, sib) + send_col(bottom, xl, sib) + send_col(bottom, xr, sib)
    yield
    got(p)
    s += send_row(top, yf, sib) + send_col(bottom, xf, sib)
    yield
    got(s)


def plane_sum(parts, out, scratch, put, keep):
    own, fold, ga, gb, ha, hb, sa, sb, ra2, rb2 = scratch
    r = fold.shape[1]
    ylo, x, yhi, core = place()
    y = yhi * 2 + ylo
    xr, xl, xf = around(x)
    yr, yl, yf = around(y)
    a = -(-r // 64) * 32
    h, g = a // 2, (r - a) // 2
    sib = {"core": 1 - core}
    pieces = ([], [])
    at = 0
    for part in parts:
        size = part.shape[0] // 4
        middle = min(max(a - at, 0), size)
        for group, first, count in ((0, 0, middle), (1, middle, size - middle)):
            if count:
                pieces[group].append((part, size, first, count, at + first))
        at += size
    came = ([], [])
    held = ([], [])
    for group in (0, 1):
        for part, size, first, count, to in pieces[group]:

            def quarter(q):
                return part.at[pl.ds(pl.multiple_of(q * size + first, 16), count), :]

            for hi in (0, 1):
                into = pl.ds(to, count)
                came[group].append(put(quarter(2 * hi + 1 - core), fold.at[hi, into, :], sib))
                held[group].append(keep(quarter(2 * hi + core), own.at[hi, into, :]))
    yield

    def add_cores(group):
        got(came[group])
        for copy in held[group]:
            keep.wait(copy)
        first, count = ((0, a), (a, r - a))[group]
        for hi in (0, 1):

            def body(i, carry, hi=hi):
                rr = pl.ds(pl.multiple_of(first + i * 16, 16), 16)
                fold[hi, rr, :] = fold[hi, rr, :] + own[hi, rr, :]
                return carry

            lax.fori_loop(0, count // 16, body, 0)

    def ycols(yy):
        return pl.ds(pl.multiple_of(lax.rem(yy, 2) * 1024, 1024), 1024)
    def a_block(yy, first):
        return fold.at[yy // 2, pl.ds(0 if first else h, h), ycols(yy)]
    def b_block(xx, first, l):
        return fold.at[:, pl.ds(a + (0 if first else g), g), pl.ds(pl.multiple_of(l * 1024 + xx * 256, 256), 256)]
    yR, yL, xR, xL = y_device(yr), y_device(yl), x_device(xr), x_device(xl)
    def sendb(i, xx, first, dev):
        return [put(b_block(xx, first, l), gb.at[i, l], dev) for l in (0, 1)]
    add_cores(0)
    pa = [put(a_block(yf, True), ga.at[0], yR), put(a_block(yf, False), ga.at[1], yL)]
    pa += [put(a_block(yr, False), ga.at[2], yR), put(a_block(yl, True), ga.at[3], yL)]
    add_cores(1)
    pb = [sendb(0, xf, True, xR), sendb(1, xf, False, xL)]
    pb += [sendb(2, xr, False, xR), sendb(3, xl, True, xL)]
    yield

    def add_a(dst, i, block, n):
        def body(j, carry):
            rr = pl.ds(pl.multiple_of(j * 16, 16), 16)
            dst[rr, :] = ga[i, rr, :] + block[rr, :]
            return carry
        lax.fori_loop(0, n // 16, body, 0)
    def add_b(dst, i, xx, first):
        for l in (0, 1):
            for hi in (0, 1):
                block = fold.at[hi, pl.ds(a + (0 if first else g), g), pl.ds(pl.multiple_of(l * 1024 + xx * 256, 256), 256)]
                def body(j, carry):
                    rr = pl.ds(pl.multiple_of(j * 16, 16), 16)
                    dst[l, hi, rr, :] = gb[i, l, hi, rr, :] + block[rr, :]
                    return carry
                lax.fori_loop(0, g // 16, body, 0)
    pa[0].wait_recv()
    add_a(sa.at[0], 0, a_block(yr, True), h)
    pa.append(put(sa.at[0], ga.at[4], yR))
    got(pb[0])
    add_b(sb.at[0], 0, xr, True)
    pb.append([put(sb.at[0], gb.at[4], xR)])
    pa[1].wait_recv()
    add_a(sa.at[1], 1, a_block(yl, False), h)
    pa.append(put(sa.at[1], ga.at[5], yL))
    got(pb[1])
    add_b(sb.at[1], 1, xl, False)
    pb.append([put(sb.at[1], gb.at[5], xL)])
    yield
    def fin_a(first, i, j):
        def body(n, carry):
            rr = pl.ds(pl.multiple_of(n * 16, 16), 16)
            block = a_block(y, first)
            ra2[pl.ds(pl.multiple_of((0 if first else h) + n * 16, 16), 16), :] = (
                block[rr, :].astype(f32) + ga[i, rr, :].astype(f32) + ga[j, rr, :].astype(f32)).astype(bf)
            return carry
        lax.fori_loop(0, h // 16, body, 0)
    def fin_b(first, i, j):
        for l in (0, 1):
            for hi in (0, 1):
                block = fold.at[hi, pl.ds(a + (0 if first else g), g), pl.ds(pl.multiple_of(l * 1024 + x * 256, 256), 256)]
                def body(n, carry):
                    rr = pl.ds(pl.multiple_of(n * 16, 16), 16)
                    rb2[l, hi, pl.ds(pl.multiple_of((0 if first else g) + n * 16, 16), 16), :] = (
                        block[rr, :].astype(f32) + gb[i, l, hi, rr, :].astype(f32) + gb[j, l, hi, rr, :].astype(f32)).astype(bf)
                    return carry
                lax.fori_loop(0, g // 16, body, 0)
    got([pa[3], pa[4]])
    fin_a(True, 3, 4)
    got([pa[2], pa[5]])
    fin_a(False, 2, 5)
    got(pb[3] + pb[4])
    fin_b(True, 3, 4)
    got(pb[2] + pb[5])
    fin_b(False, 2, 5)
    def a2(xx, first):
        return ra2.at[pl.ds(0 if first else h, h), pl.ds(pl.multiple_of(xx * 256, 256), 256)]
    def b2(yy, first):
        return rb2.at[lax.rem(yy, 2), yy // 2, pl.ds(0 if first else g, g), :]
    qa = [put(a2(xf, True), ha.at[0], xR), put(a2(xf, False), ha.at[1], xL), put(a2(xr, False), ha.at[2], xR), put(a2(xl, True), ha.at[3], xL)]
    qb = [put(b2(yf, True), hb.at[0], yR), put(b2(yf, False), hb.at[1], yL), put(b2(yr, False), hb.at[2], yR), put(b2(yl, True), hb.at[3], yL)]
    yield
    sa2, sb2 = ha.at[pl.ds(6, 2)], hb.at[pl.ds(6, 2)]
    qa[0].wait_recv()
    sa2[0] = ha[0] + a2(xr, True)[...]
    qa.append(put(sa2.at[0], ha.at[4], xR))
    qb[0].wait_recv()
    sb2[0] = hb[0] + b2(yr, True)[...]
    qb.append(put(sb2.at[0], hb.at[4], yR))
    qa[1].wait_recv()
    sa2[1] = ha[1] + a2(xl, False)[...]
    qa.append(put(sa2.at[1], ha.at[5], xL))
    qb[1].wait_recv()
    sb2[1] = hb[1] + b2(yl, False)[...]
    qb.append(put(sb2.at[1], hb.at[5], yL))
    yield
    got(qa[2:] + qb[2:])
    def w(v): return v.astype(f32)
    out[0:h, :] = w(a2(x, True)[...]) + w(ha[3]) + w(ha[4])
    out[h:a, :] = w(a2(x, False)[...]) + w(ha[2]) + w(ha[5])
    out[a:a + g, :] = w(b2(y, True)[...]) + w(hb[3]) + w(hb[4])
    out[a + g:, :] = w(b2(y, False)[...]) + w(hb[2]) + w(hb[5])


SUM_SCRATCH = 10


def sum_scratch(r):
    a = -(-r // 64) * 32
    h, g = a // 2, (r - a) // 2
    V = pltpu.VMEM
    return [V((2, r, 2048), bf), V((2, r, 2048), bf), V((6, h, 1024), bf), V((6, 2, 2, g, 256), bf), V((8, h, 256), bf), V((8, g, 256), bf),
            V((2, h, 1024), bf), V((2, 2, 2, g, 256), bf), V((a, 1024), bf), V((2, 2, r - a, 256), bf)]


def small_sums(blocks, gains, small, gain, scratch, put):
    zgot, sgot, pair, pgot, qgain, rgot, rgain, mine = scratch
    z = lax.axis_index("z")
    yhi, core = lax.axis_index("yhi"), lax.axis_index("core")
    me = yhi * 2 + core
    row = lax.axis_index("ylo") * 4 + lax.axis_index("x")
    zs = []
    near = [put(blocks.at[2 * hi + 1 - core], sgot.at[hi], {"core": 1 - core}) for hi in (0, 1)]
    for j in (1, 2, 3):
        to = lax.rem(z + j, 4)
        zs.append(put(gains.at[to], zgot.at[j - 1], {"z": to}))
    yield
    got(near)
    for hi in (0, 1):
        pair[hi] = blocks[2 * hi + core] + sgot[hi]
    across = put(pair.at[1 - yhi], pgot, {"yhi": 1 - yhi})
    got(zs)
    qgain[3] = gains[z] + zgot[0] + zgot[1] + zgot[2]
    qs = []
    for j in (1, 2, 3):
        to = lax.rem(me + j, 4)
        qs.append(put(qgain.at[3, to], qgain.at[j - 1, 0], quad_device(to)))
    yield
    got(qs)
    across.wait_recv()
    mine[...] = pair[yhi] + pgot[...]
    rgain[7] = qgain[3, me] + qgain[0, 0] + qgain[1, 0] + qgain[2, 0]
    rs = []
    size = PACKED // 8

    def seq(j):
        to = lax.rem(row + j, 8)
        return to, {"ylo": to // 4, "x": lax.rem(to, 4)}

    for j in range(1, 8):
        to, device = seq(j)
        rs.append(put(mine.at[pl.ds(pl.multiple_of(to * size, 8), size), :], rgot.at[j - 1], device))
        rs.append(put(rgain.at[7], rgain.at[j - 1], device))
    yield
    got(rs)
    own = pl.ds(pl.multiple_of(row * size, 8), size)
    total = mine[own, :]
    gain_total = rgain[7]
    for j in range(7):
        total = total + rgot[j]
        gain_total = gain_total + rgain[j]
    small[own, :] = total
    gain[...] = gain_total
    ag = []
    for j in range(1, 8):
        _, device = seq(j)
        ag.append(put(small.at[own, :], small.at[own, :], device))
    yield
    got(ag)


SMALL_SCRATCH = 8
SMALL_COPIES = 30


def small_scratch():
    return [
        pltpu.VMEM((3, 4, 8, 128), f32),
        pltpu.VMEM((2, PACKED, 128), f32),
        pltpu.VMEM((2, PACKED, 128), f32),
        pltpu.VMEM((PACKED, 128), f32),
        pltpu.VMEM((4, 4, 8, 128), f32),
        pltpu.VMEM((7, PACKED // 8, 128), f32),
        pltpu.VMEM((8, 8, 128), f32),
        pltpu.VMEM((PACKED, 128), f32),
    ]


def tail_kernel(
    dxb_in, dyb_in, xb_in, yb_in, rec_weights, x_in, n_in, dz_in, rec_out, up, inv, gains, gain_two, blocks,
    grad_in, in_grad, gate_grad, out_grad, up_grad, rate_grad, input_grad, vec_grad, gain,
    dxb, dyb, xb, yb, w_in, w_gate, x, normed, dz, part, own, low, coef, gain_one, gain_parts,
    part_in, part_gate, rec_sum, up_sum, small, back_low, *rest,
):
    (came, sent), rest = rest[:2], rest[2:]
    plane_refs, rest = rest[:SUM_SCRATCH], rest[SUM_SCRATCH:]
    up_refs, rest = rest[:SUM_SCRATCH], rest[SUM_SCRATCH:]
    small_refs, rest = rest[:SMALL_SCRATCH], rest[SMALL_SCRATCH:]
    send, recv, done = rest
    keep = Keeper(done)
    first = [keep(*pair) for pair in ((dxb_in, dxb), (dyb_in, dyb), (n_in, normed))]
    second = [keep(xb_in, xb), keep(yb_in, yb)]
    third = [
        keep(*pair) for pair in ((rec_weights.at[0], w_in), (rec_weights.at[1], w_gate), (x_in, x))
    ]
    fourth = keep(dz_in, dz)
    meet(z_others() + plane_neighbours() + line_devices())
    put = Sender(send, recv)
    plane_up = plane_sum([up], up_sum, up_refs, put, keep)
    step(plane_up)
    for copy in first:
        keep.wait(copy)
    rec_grad(dxb, normed, part_in)
    rec_grad(dyb, normed, part_gate)
    plane = plane_sum([part_in, part_gate, rec_out], rec_sum, plane_refs, put, keep)
    step(plane)
    for copy in second:
        keep.wait(copy)

    def inner(i):
        r = pl.ds(pl.multiple_of(i * 16, 16), 16)
        terms = dxb[r, :].astype(f32) * xb[r, :] + dyb[r, :].astype(f32) * yb[r, :]
        total = jnp.sum(terms, axis=1, keepdims=True) * (1.0 / D)
        coef[r, :] = inv[r, :] * inv[r, :] * total

    loop(TOK // 16, inner)
    gain_one[...] = jnp.zeros((8, D), f32)
    step(plane_up)
    for copy in third:
        keep.wait(copy)

    def produce(at):
        cols = z_columns(at)
        for half in (0, 1):
            r = slice(HALF * half, HALF * (half + 1))
            dn = jnp.dot(dxb[r, :], w_in[:, cols], preferred_element_type=f32)
            dn = dn + jnp.dot(dyb[r, :], w_gate[:, cols], preferred_element_type=f32)
            values = x[r, cols].astype(f32)
            scaled = dn * jnp.concatenate([inv[r, :]] * 4, axis=1)
            less = values * jnp.concatenate([coef[r, :]] * 4, axis=1)
            part[r, cols] = (scaled * gains[0:1, cols] - less).astype(bf)
            gain_one[:, cols] = gain_one[:, cols] + jnp.sum(
                (scaled * values).reshape(HALF // 8, 8, 512), axis=0
            )

    total = ring_sum(part, own, came, sent, put, produce)
    step(total)
    sums_one = jnp.sum(gain_one[...], axis=0, keepdims=True)
    sums_two = jnp.sum(gain_two[...], axis=0, keepdims=True)
    gain_parts[...] = jnp.zeros((4, 4, 8, 128), f32)
    for i in range(4):
        for j in range(4):
            cols = slice(128 * (4 * i + j), 128 * (4 * i + j + 1))
            gain_parts[i, j, 0:1, :] = sums_one[:, cols]
            gain_parts[i, j, 1:2, :] = sums_two[:, cols]
    little = small_sums(blocks, gain_parts, small, gain, small_refs, put)
    step(little)
    step(plane, total, plane_up, little)
    step(plane_up, plane)
    finish(total)
    keep.wait(fourth)
    low[...] = (own[...] + dz[...]).astype(bf)
    back, mine = quad_scatter(low, back_low, put, keep)
    step(little, plane_up, plane, little)
    finish(plane_up)
    up_grad[...] = up_sum[...].T
    got(back)
    keep.wait(mine)

    def widen(i):
        r = pl.ds(pl.multiple_of(i * 64, 64), 64)
        grad_in[r, :] = back_low[r, :].astype(f32)

    loop(4 * TOK // 64, widen)
    step(plane)
    finish(little)
    for k, target in ((0, rate_grad), (1, input_grad)):
        top = SQUARE * k
        target[:, 0:128] = small[top : top + HW, :]
        for j, (at, size) in enumerate(TAILS):
            target[at : at + size, 128:HW] = small[top + HW : top + HW + size, 32 * j : 32 * j + 32]
    vec_grad[:, 0:128] = small[2 * SQUARE : 2 * SQUARE + 8, :]
    vec_grad[:, 128:HW] = small[2 * SQUARE + 16 : 2 * SQUARE + 24, 0:32]
    finish(plane)
    in_grad[...] = rec_sum[0:HW, :].T
    gate_grad[...] = rec_sum[HW : 2 * HW, :].T
    out_grad[...] = rec_sum[2 * HW :, :]
    put.drain()
    keep.drain()


def tail(*operands):
    rows = pltpu.VMEM((TOK, D), bf)
    tall = pltpu.VMEM((TOK, CH), f32)
    low = pltpu.VMEM((TOK, CH), bf)
    weight = pltpu.VMEM((CH, D), bf)
    return pl.pallas_call(
        tail_kernel,
        out_shape=(
            shape((4 * TOK, 128), f32),
            shape((256, HW), f32),
            shape((256, HW), f32),
            shape((HW, 256), f32),
            shape((256, 384), f32),
            shape((HW, HW), f32),
            shape((HW, HW), f32),
            shape((8, HW), f32),
            shape((8, 128), f32),
        ),
        in_specs=[ANY] * 10 + [VMEM] * 4,
        out_specs=[VMEM] * 9,
        scratch_shapes=[
            low, low, tall, tall, weight, weight, rows, rows,
            pltpu.VMEM((TOK, 512), f32),
            rows,
            pltpu.VMEM((TOK, 512), f32),
            pltpu.VMEM((TOK, 512), bf),
            pltpu.VMEM((TOK, 128), f32),
            pltpu.VMEM((8, D), f32),
            pltpu.VMEM((4, 4, 8, 128), f32),
            weight, weight,
            pltpu.VMEM((3 * HW, 256), f32),
            pltpu.VMEM((384, 256), f32),
            pltpu.VMEM((PACKED, 128), f32),
            pltpu.VMEM((4 * TOK, 128), bf),
        ]
        + ring_scratch()
        + sum_scratch(3 * HW)
        + sum_scratch(384)
        + small_scratch()
        + semaphores(6 + 3 + 2 * SUM_COPIES + SMALL_COPIES)
        + [pltpu.SemaphoreType.DMA((2 * SUM_KEEPS + 10,))],
        compiler_params=params(5),
        name="tail",
    )(*operands)


def line_devices():
    ylo, x = lax.axis_index("ylo"), lax.axis_index("x")
    row = ylo * 4 + x
    rows = [
        {"ylo": lax.rem(row + j, 8) // 4, "x": lax.rem(row + j, 4)} for j in range(1, 8)
    ]
    return quad_others() + rows


def my_block():
    row = lax.axis_index("ylo") * 4 + lax.axis_index("x")
    return row * 4 + lax.axis_index("yhi") * 2 + lax.axis_index("core")


def line_prefix(mine, quad, rows, total, put, backward, meanwhile=lambda: None):
    me = lax.axis_index("yhi") * 2 + lax.axis_index("core")
    row = lax.axis_index("ylo") * 4 + lax.axis_index("x")
    copies = []
    for j in (1, 2, 3):
        copies.append(put(mine, quad.at[me], quad_device(lax.rem(me + j, 4))))
    quad[me] = mine[...]
    got(copies)
    ones = jnp.ones((1, CH), f32)
    zeros = jnp.zeros((1, CH), f32)
    prod, end, prod_all, end_all = ones, zeros, ones, zeros
    for turn in range(4):
        q = 3 - turn if backward else turn
        a, b = quad[q, 0:1, :], quad[q, 1:2, :]
        end_all = a * end_all + b
        prod_all = a * prod_all
        take = (q > me) if backward else (q < me)
        end = jnp.where(take, a * end + b, end)
        prod = jnp.where(take, a * prod, prod)
    total[0:1, :] = prod_all
    total[1:2, :] = end_all
    copies = []
    for j in range(1, 8):
        other = lax.rem(row + j, 8)
        copies.append(put(total, rows.at[row], {"ylo": other // 4, "x": lax.rem(other, 4)}))
    rows[row] = total[...]
    meanwhile()
    got(copies)
    came = zeros
    for turn in range(8):
        r = 7 - turn if backward else turn
        a, b = rows[r, 0:1, :], rows[r, 1:2, :]
        take = (r > row) if backward else (r < row)
        came = jnp.where(take, a * came + b, came)
    return prod * came + end


def split(values):
    high = values.astype(bf)
    return high, (values - high.astype(f32)).astype(bf)


def dot3(a, b, dims):
    (ah, al), (bh, bl) = a, b

    def one(p, q):
        return lax.dot_general(p, q, (dims, ((), ())), preferred_element_type=f32)

    return one(ah, bh) + (one(al, bh) + one(ah, bl))


def minus_expm1(v):
    near = -v * (
        1.0
        + v * (1 / 2) * (1.0 + v * (1 / 3) * (1.0 + v * (1 / 4) * (1.0 + v * (1 / 5) * (1.0 + v * (1 / 6)))))
    )
    return jnp.where(v > -0.3, near, 1.0 - jnp.exp(v))


def gelu_parts(v):
    cdf = 0.5 * (1.0 + lax.erf(v * 0.7071067811865476))
    pdf = 0.3989422804014327 * jnp.exp(-0.5 * v * v)
    return v * cdf, cdf + v * pdf


def shifted(values, by, fill, reverse):
    rows = lax.broadcasted_iota(jnp.int32, values.shape, 0)
    size = values.shape[0]
    if reverse:
        return jnp.where(rows < size - by, pltpu.roll(values, size - by, 0), fill)
    return jnp.where(rows >= by, pltpu.roll(values, by, 0), fill)


def behind(near, by):
    return near[8:24, :] if by == 0 else pltpu.roll(near, by, 0)[8:24, :]


def ahead(near, by):
    size = near.shape[0]
    return pltpu.roll(near, size - by, 0)[0 : size - 8, :]


def scan8(a, b, reverse):
    for by in (1, 2, 4):
        b = b + a * shifted(b, by, 0.0, reverse)
        a = a * shifted(a, by, 1.0, reverse)
    return a, b


def loop(count, body):
    def one(i, carry):
        body(i)
        return carry

    lax.fori_loop(0, count, one, 0)


def front_kernel(
    tokens, cotangent, rate_w, input_w, vectors, norms, mlp_gate, mlp_up, own_rec,
    x_out, n_out, xb_out, yb_out, c_out, rate_out, gin_out, a_out, m_out, h_out, hy_out, ext_out, hi_out, lo_out,
    cot, rec_out, w_gate, w_up,
    inv, gains, vec, state_in, total_a,
    full, normed, weights, params_all, norms_all, own_gate, own_up,
    xb, yb, c, rate, gin, a, m, h, hy, ext, gate_hi, gate_lo, pre, prod,
    halo, mine, quad, rows, total, send, recv, done,
):
    z = lax.axis_index("z")
    me = lax.axis_index("yhi") * 2 + lax.axis_index("core")
    block = my_block()
    after, before = lax.rem(block + 1, 32), lax.rem(block + 31, 32)
    meet(
        line_devices()
        + [plane_device(after), plane_device(before)]
        + plane_neighbours()
        + z_others()
    )
    put = Sender(send, recv)
    keep = Keeper(done)
    tokens_in = token_gather(tokens, full, put, keep)
    plane = plane_gather(own_rec, weights, put, keep)
    step(tokens_in, plane)
    small = []
    for j in (1, 2, 3):
        small.append(put(norms, norms_all.at[z, me], quad_device(lax.rem(me + j, 4))))
    norms_all[z, me] = norms[...]
    step(tokens_in, plane)
    for weight, top in ((rate_w, 0), (input_w, SQUARE)):
        params_all[me, top : top + HW, :] = weight[:, 0:128]
        params_all[me, top + HW : top + SQUARE, :] = jnp.zeros((48, 128), f32)
        for j, (at, size) in enumerate(TAILS):
            params_all[me, top + HW : top + HW + size, 32 * j : 32 * j + 32] = weight[at : at + size, 128:HW]
    params_all[me, 2 * SQUARE : 2 * SQUARE + 16, :] = vectors[:, 0:128]
    params_all[me, 2 * SQUARE + 16 : PACKED, :] = jnp.zeros((16, 128), f32)
    params_all[me, 2 * SQUARE + 16 : PACKED, 0:32] = vectors[:, 128:HW]
    got(small)
    small = []
    for j in (1, 2, 3):
        small.append(put(norms_all.at[z], norms_all.at[z], {"z": lax.rem(z + j, 4)}))
    step(plane)
    own_gate[...] = mlp_gate[...].astype(f32).T.astype(bf)
    own_up[...] = mlp_up[...].astype(f32).T.astype(bf)
    step(tokens_in)
    gate_hi[...] = jnp.zeros((CH, 2 * CH), bf)
    gate_lo[...] = jnp.zeros((CH, 2 * CH), bf)
    got(small)
    for i in range(4):
        for j in range(4):
            gains[:, 128 * (4 * i + j) : 128 * (4 * i + j + 1)] = norms_all[i, j]
    step(plane)
    plane_a = plane_gather(own_gate, w_gate, put, keep)
    plane_b = plane_gather(own_up, w_up, put, keep)
    step(plane_a, plane_b)
    finish(tokens_in)
    keep(full, x_out)
    other = token_gather(cotangent, cot, put, keep)
    core, yhi = lax.axis_index("core"), lax.axis_index("yhi")
    own_params = params_all.at[me]
    near = put(own_params, own_params, {"core": 1 - core})
    across = put(own_params, own_params, {"yhi": 1 - yhi})
    step(plane, plane_a, plane_b, other)

    def norm(i):
        r = pl.ds(pl.multiple_of(i * 16, 16), 16)
        values = full[r, :].astype(f32)
        mean = jnp.sum(values * values, axis=1, keepdims=True) * (1.0 / D)
        scale = lax.rsqrt(mean + EPS)
        inv[r, :] = jnp.broadcast_to(scale, (16, 128))
        normed[r, :] = (values * scale * gains[0:1, :]).astype(bf)

    loop(TOK // 16, norm)
    keep(normed, n_out)
    finish(plane)
    keep(weights, rec_out)
    across.wait_recv()
    peer_params = params_all.at[lax.rem(me + 2, 4)]
    passed = put(peer_params, peer_params, {"core": 1 - core})
    step(plane_a, other)
    for i, into in ((0, xb), (1, yb)):
        for at, width in ((0, 256), (256, 256), (512, 128)):
            into[:, at : at + width] = lax.dot_general(
                normed[...],
                weights[i, at : at + width, :],
                (((1,), (1,)), ((), ())),
                preferred_element_type=f32,
            )
        if i == 0:
            halo_out = pl.ds(TOK - 16, 16)
            hy[halo_out, :] = xb[halo_out, :].astype(bf)
            edge = put(hy.at[halo_out, :], halo, plane_device(after))
            step(plane_b)
    keep(xb, xb_out)
    keep(yb, yb_out)
    step(other, plane_a)

    def widen(i):
        r = pl.multiple_of(i * 16, 16)
        ext[pl.ds(pl.multiple_of(8 + r, 8), 16), :] = xb[pl.ds(r, 16), :].astype(bf).astype(f32)

    loop(TOK // 16, widen)
    got([near, passed])
    for i in range(4):
        there = HW * i
        vec[:, there : there + 128] = params_all[i, 2 * SQUARE : 2 * SQUARE + 16, :]
        vec[:, there + 128 : there + HW] = params_all[i, 2 * SQUARE + 16 : PACKED, 0:32]
        for k in (0, 1):
            top = SQUARE * k
            high, low = split(params_all[i, top : top + HW, :])
            over = CH * k + HW * i
            gate_hi[there : there + HW, over : over + 128] = high
            gate_lo[there : there + HW, over : over + 128] = low
            for j, (at, size) in enumerate(TAILS):
                high, low = split(params_all[i, top + HW : top + HW + size, 32 * j : 32 * j + 32])
                rows_here = slice(there + at, there + at + size)
                gate_hi[rows_here, over + 128 : over + HW] = high
                gate_lo[rows_here, over + 128 : over + HW] = low
    keep(gate_hi, hi_out)
    keep(gate_lo, lo_out)

    def conv(i):
        r = i * 16
        near = ext[pl.ds(pl.multiple_of(r, 16), 24), :]
        acc = vec[4:5, :] + vec[0:1, :] * near[8:24, :]
        for k in (1, 2, 3):
            acc = acc + vec[k : k + 1, :] * behind(near, k)
        c[pl.ds(pl.multiple_of(r, 16), 16), :] = acc

    lax.fori_loop(1, TOK // 16, lambda i, carry: (conv(i), carry)[1], 0)

    def gates(i):
        r = pl.ds(pl.multiple_of(i * 128, 128), 128)
        pre[r, :] = dot3(split(c[r, :]), (gate_hi[...], gate_lo[...]), ((1,), (0,)))

    lax.fori_loop(1, TOK // 128, lambda i, carry: (gates(i), carry)[1], 0)
    edge.wait_recv()
    ext[0:8, :] = jnp.where(block > 0, halo[8:16, :].astype(f32), 0.0)
    conv(0)
    gates(0)
    keep(ext, ext_out)
    keep(c, c_out)
    step(plane_a, plane_b, other)

    def point(i, carry):
        prod_in, state = carry
        r = pl.ds(pl.multiple_of(i * 8, 8), 8)
        rr = jax.nn.sigmoid(pre[r, 0:CH] + vec[5:6, :])
        gg = jax.nn.sigmoid(pre[r, CH:] + vec[6:7, :])
        log_a = -8.0 * rr * vec[7:8, :]
        aa = jnp.exp(log_a)
        mm = jnp.sqrt(minus_expm1(2.0 * log_a))
        rate[r, :] = rr
        gin[r, :] = gg
        a[r, :] = aa
        m[r, :] = mm
        pa, hb = scan8(aa, mm * gg * c[r, :], False)
        hb = hb + pa * state
        pa = pa * prod_in
        h[r, :] = hb
        prod[r, :] = pa
        return pa[7:8, :], hb[7:8, :]

    last = (jnp.ones((1, CH), f32), jnp.zeros((1, CH), f32))
    last = lax.fori_loop(0, TOK // 16, point, last)
    step(plane_b)
    last = lax.fori_loop(TOK // 16, TOK // 8, point, last)
    for source, target in ((rate, rate_out), (gin, gin_out), (a, a_out), (m, m_out)):
        keep(source, target)
    mine[...] = jnp.zeros((8, CH), f32)
    total[...] = jnp.zeros((8, CH), f32)
    step(plane_a)
    mine[0:1, :] = last[0]
    mine[1:2, :] = last[1]
    came = line_prefix(mine, quad, rows, total, put, False, lambda: step(plane_b))
    state_in[...] = jnp.broadcast_to(came, (8, CH))
    total_a[...] = jnp.broadcast_to(last[0], (8, CH))
    finish(other)
    edge.wait_send()

    def complete(i):
        r = pl.ds(pl.multiple_of(i * 16, 16), 16)
        hh = h[r, :] + prod[r, :] * came
        h[r, :] = hh
        hy[r, :] = (hh * gelu_parts(yb[r, :])[0]).astype(bf)

    loop(TOK // 16, complete)
    keep(h, h_out)
    keep(hy, hy_out)

    finish(plane_a, plane_b)
    put.drain(skip=edge)
    keep.drain()


def front(*operands):
    wide = shape((TOK, CH), f32)
    rows = shape((TOK, D), bf)
    mlp = shape((1536, D), bf)
    gate = shape((CH, 2 * CH), bf)
    out = (
        rows, rows, wide, wide, wide, wide, wide, wide, wide, wide,
        shape((TOK, CH), bf), shape((TOK + 8, CH), f32), gate, gate,
        rows, shape((3, CH, D), bf), mlp, mlp,
    )
    little = (
        shape((TOK, 128), f32), shape((8, D), f32), shape((16, CH), f32),
        shape((8, CH), f32), shape((8, CH), f32),
    )
    tall = pltpu.VMEM((TOK, CH), f32)
    return pl.pallas_call(
        front_kernel,
        out_shape=out + little,
        in_specs=[VMEM] * 8 + [ANY],
        out_specs=[ANY] * len(out) + [VMEM] * len(little),
        scratch_shapes=[
            pltpu.VMEM((TOK, D), bf),
            pltpu.VMEM((TOK, D), bf),
            pltpu.VMEM((3, CH, D), bf),
            pltpu.VMEM((4, PACKED, 128), f32),
            pltpu.VMEM((4, 4, 8, 128), f32),
            pltpu.VMEM((384, 256), bf),
            pltpu.VMEM((384, 256), bf),
            tall, tall, tall, tall, tall, tall, tall, tall,
            pltpu.VMEM((TOK, CH), bf),
            pltpu.VMEM((TOK + 8, CH), f32),
            pltpu.VMEM((CH, 2 * CH), bf),
            pltpu.VMEM((CH, 2 * CH), bf),
            pltpu.VMEM((TOK, 2 * CH), f32),
            tall,
            pltpu.VMEM((16, CH), bf),
            pltpu.VMEM((8, CH), f32),
            pltpu.VMEM((4, 8, CH), f32),
            pltpu.VMEM((8, 8, CH), f32),
            pltpu.VMEM((8, CH), f32),
        ]
        + semaphores(18 + 9 + 11 + 3 * GATHER_COPIES)
        + [pltpu.SemaphoreType.DMA((26,))],
        compiler_params=params(0),
        name="front",
    )(*operands)


def backward_kernel(
    dhy_in, yb_in, hi_in, lo_in, vec, c_in, rate_in, gin_in, a_in, m_in, h_in, ext_in, state_in, total_a,
    mlp_in, zown_in, down, gate,
    dxb, dyb, blocks, block_out, down_sum, gate_sum,
    e, apad, hpad, q, prod, pri, halo, mine, quad, rows, total, own, low, came_z, sent_z,
    yb, gate_hi, gate_lo, c, rate, gin, m, ext, mlp_part, z_own, dgate, sums, *rest,
):
    dc = q
    block = my_block()
    after, before = lax.rem(block + 1, 32), lax.rem(block + 31, 32)
    send, recv, done = rest[2 * SUM_SCRATCH :]
    keep = Keeper(done)
    load_mlp = keep(mlp_in, mlp_part)
    load_first = [
        keep(dhy_in, e),
        keep(yb_in, yb),
        keep(h_in, hpad.at[pl.ds(8, TOK), :]),
        keep(a_in, apad.at[pl.ds(0, TOK), :]),
    ]
    load_point = [keep(*pair) for pair in ((rate_in, rate), (gin_in, gin), (m_in, m), (c_in, c))]
    load_rest = [keep(*pair) for pair in ((hi_in, gate_hi), (lo_in, gate_lo), (ext_in, ext), (zown_in, z_own))]
    meet(
        line_devices()
        + [plane_device(after), plane_device(before)]
        + plane_neighbours()
        + z_others()
    )
    put = Sender(send, recv)
    whole = ring_sum(mlp_part, own, came_z, sent_z, put)
    plane = plane_sum([down], down_sum, rest[:SUM_SCRATCH], put, keep)
    plane_b = plane_sum([gate], gate_sum, rest[SUM_SCRATCH : 2 * SUM_SCRATCH], put, keep)
    keep.wait(load_mlp)
    step(whole, plane)
    for copy in load_first:
        keep.wait(copy)

    def direct(i):
        r = pl.ds(pl.multiple_of(i * 16, 16), 16)
        value, slope = gelu_parts(yb[r, :])
        grad = e[r, :]
        hh = hpad[pl.ds(pl.multiple_of(i * 16 + 8, 8), 16), :]
        e[r, :] = grad * value
        dyb[r, :] = (grad * hh * slope).astype(bf)

    loop(TOK // 16, direct)
    apad[TOK : TOK + 8, :] = jnp.ones((8, CH), f32)
    hpad[0:8, :] = state_in[...]
    step(plane_b)

    def adjoint(i, carry):
        prod_in, state = carry
        r0 = TOK - 8 - i * 8
        r = pl.ds(pl.multiple_of(r0, 8), 8)
        next_a = ahead(apad[pl.ds(pl.multiple_of(r0, 8), 16), :], 1)
        pa, qb = scan8(next_a, e[r, :], True)
        qb = qb + pa * state
        pa = pa * prod_in
        q[r, :] = qb
        prod[r, :] = pa
        return pa[0:1, :], qb[0:1, :]

    last = (jnp.ones((1, CH), f32), jnp.zeros((1, CH), f32))
    last = lax.fori_loop(0, TOK // 8, adjoint, last)
    step(whole)
    mine[...] = jnp.zeros((8, CH), f32)
    total[...] = jnp.zeros((8, CH), f32)
    mine[0:1, :] = total_a[0:1, :]
    mine[1:2, :] = apad[0:1, :] * last[1]
    came = line_prefix(mine, quad, rows, total, put, True, lambda: step(plane, plane_b))
    for copy in load_point:
        keep.wait(copy)

    def point(i, carry):
        s_rate, s_input, s_decay = carry
        r = pl.ds(pl.multiple_of(i * 8, 8), 8)
        qq = q[r, :] + prod[r, :] * came
        aa, rr, gg, mm, cc = apad[r, :], rate[r, :], gin[r, :], m[r, :], c[r, :]
        earlier = pltpu.roll(hpad[pl.ds(pl.multiple_of(i * 8, 8), 16), :], 1, 0)[8:16, :]
        grad_log = aa * (qq * earlier - qq * gg * cc * aa / mm)
        pr = -8.0 * vec[7:8, :] * grad_log * rr * (1.0 - rr)
        pi = qq * mm * cc * gg * (1.0 - gg)
        pri[r, 0:CH] = pr
        pri[r, CH:] = pi
        dc[r, :] = qq * mm * gg
        return s_rate + pr, s_input + pi, s_decay + 8.0 * rr * vec[8:9, :] * grad_log

    none = jnp.zeros((8, CH), f32)
    so_far = lax.fori_loop(0, TOK // 16, point, (none, none, none))
    step(plane)
    s_rate, s_input, s_decay = lax.fori_loop(TOK // 16, TOK // 8, point, so_far)
    step(plane_b)

    for copy in load_rest:
        keep.wait(copy)

    def spread(i):
        r = pl.ds(pl.multiple_of(i * 128, 128), 128)
        dc[r, :] = dc[r, :] + dot3(split(pri[r, :]), (gate_hi[...], gate_lo[...]), ((1,), (1,)))

    loop(TOK // 128, spread)
    edge = put(dc.at[pl.ds(0, 8), :], halo, plane_device(before))
    finish(whole)
    low[...] = (own[...] + z_own[...]).astype(bf)
    back, kept = quad_scatter(low, block_out, put, keep)
    dgate[...] = dot3(split(c[...]), split(pri[...]), ((0,), (0,)))
    step(plane)
    edge.wait_recv()
    dc[TOK : TOK + 8, :] = jnp.where(block < 31, halo[...], 0.0)

    def taps(i, carry):
        r = i * 16
        here = pl.ds(pl.multiple_of(r, 16), 16)
        later = dc[pl.ds(pl.multiple_of(r, 16), 24), :]
        near = ext[pl.ds(pl.multiple_of(r, 16), 24), :]
        dd = later[0:16, :]
        out = vec[0:1, :] * dd
        for k in (1, 2, 3):
            out = out + vec[k : k + 1, :] * ahead(later, k)
        dxb[here, :] = out.astype(bf)

        def fold(v):
            return v[0:8, :] + v[8:16, :]

        new = [carry[0] + fold(dd)]
        for k in range(4):
            new.append(carry[1 + k] + fold(dd * behind(near, k)))
        return tuple(new)

    s_bias, *s_taps = lax.fori_loop(0, TOK // 16, taps, (none,) * 5)

    step(plane_b, plane)

    def place_sum(row, value):
        sums[row : row + 1, :] = jnp.sum(value, axis=0, keepdims=True)

    for k in range(4):
        place_sum(k, s_taps[k])
    place_sum(4, s_bias)
    place_sum(5, s_rate)
    place_sum(6, s_input)
    place_sum(7, s_decay)
    for i in range(4):
        there = HW * i
        for k in (0, 1):
            top, over = SQUARE * k, CH * k + HW * i
            blocks[i, top : top + HW, :] = dgate[there : there + HW, over : over + 128]
            for j, (at, size) in enumerate(TAILS):
                blocks[i, top + HW : top + HW + size, 32 * j : 32 * j + 32] = dgate[
                    there + at : there + at + size, over + 128 : over + HW
                ]
            blocks[i, top + HW + 16 : top + SQUARE, 96:128] = jnp.zeros((32, 32), f32)
        blocks[i, 2 * SQUARE :, :] = jnp.zeros((32, 128), f32)
        blocks[i, 2 * SQUARE : 2 * SQUARE + 8, :] = sums[:, there : there + 128]
        blocks[i, 2 * SQUARE + 16 : 2 * SQUARE + 24, 0:32] = sums[:, there + 128 : there + HW]
    finish(plane, plane_b)
    got(back)
    keep.wait(kept)
    put.drain()
    keep.drain()


def backward_scan(*operands):
    r = operands[-1].shape[0] // 4
    tall = pltpu.VMEM((TOK, CH), f32)
    return pl.pallas_call(
        backward_kernel,
        out_shape=(
            shape((TOK, CH), bf),
            shape((TOK, CH), bf),
            shape((4, PACKED, 128), f32),
            shape((4 * TOK, 128), bf),
            shape((r, 256), f32),
            shape((r, 256), f32),
        ),
        in_specs=[ANY] * 4 + [VMEM] + [ANY] * 7 + [VMEM] * 2 + [ANY] * 4,
        out_specs=[VMEM] * 6,
        scratch_shapes=[
            tall,
            pltpu.VMEM((TOK + 8, CH), f32),
            pltpu.VMEM((TOK + 8, CH), f32),
            pltpu.VMEM((TOK + 8, CH), f32),
            tall,
            pltpu.VMEM((TOK, 2 * CH), f32),
            pltpu.VMEM((8, CH), f32),
            pltpu.VMEM((8, CH), f32),
            pltpu.VMEM((4, 8, CH), f32),
            pltpu.VMEM((8, 8, CH), f32),
            pltpu.VMEM((8, CH), f32),
            pltpu.VMEM((TOK, 512), f32),
            pltpu.VMEM((TOK, 512), bf),
        ]
        + ring_scratch()
        + [
            tall,
            pltpu.VMEM((CH, 2 * CH), bf),
            pltpu.VMEM((CH, 2 * CH), bf),
            tall,
            tall,
            tall,
            tall,
            pltpu.VMEM((TOK + 8, CH), f32),
            pltpu.VMEM((TOK, D), bf),
            pltpu.VMEM((TOK, 512), f32),
            pltpu.VMEM((CH, 2 * CH), f32),
            pltpu.VMEM((8, CH), f32),
        ]
        + sum_scratch(r)
        + sum_scratch(r)
        + semaphores(11 + 6 + 3 + 2 * SUM_COPIES)
        + [pltpu.SemaphoreType.DMA((14 + 2 * SUM_KEEPS,))],
        compiler_params=params(4),
        name="backward_scan",
    )(*operands)


def per_device(
    block_in, cotangent, norm_one, rec_in, rec_gate, conv_weight, conv_bias,
    rate_weight, rate_bias, input_weight, input_bias, decay_code, rec_out,
    norm_two, mlp_gate, mlp_up, mlp_down,
):
    decay = decay_code.astype(f32) / 256.0
    vectors = jnp.concatenate(
        [
            conv_weight,
            conv_bias[None],
            rate_bias[None],
            input_bias[None],
            jax.nn.softplus(-decay)[None],
            jax.nn.sigmoid(-decay)[None],
            jnp.zeros((7, HW), f32),
        ],
        axis=0,
    )
    norms = jnp.concatenate([norm_one[None], norm_two[None], jnp.zeros((6, 128), f32)], axis=0)
    (
        x_full, n_one, xb, yb, c, rate, gin, a, m, h, hy, ext, gate_hi, gate_lo,
        cot_full, w_rec, w_gate, w_up,
        inv_one, gains, vec, state_in, total_a,
    ) = front(
        block_in, cotangent, rate_weight[0], input_weight[0], vectors, norms, mlp_gate, mlp_up,
        jnp.stack([rec_in.T, rec_gate.T, rec_out]),
    )
    z_own, dz_own, dhy, mlp_part, part_out, part_down, part_gate, part_up, gain_two_sums = middle(
        hy, w_rec, x_full, cot_full, w_gate, w_up, mlp_down, gains
    )
    dxb, dyb, blocks, block_out, grad_down, grad_gate = backward_scan(
        dhy, yb, gate_hi, gate_lo, vec, c, rate, gin, a, m, h, ext, state_in, total_a,
        mlp_part, z_own, part_down, part_gate,
    )
    grad_in, grad_rec_in, grad_rec_gate, grad_out, grad_up, grad_rate, grad_input, vector_grads, gain_sums = tail(
        dxb, dyb, xb, yb, w_rec, x_full, n_one, dz_own, part_out, part_up,
        inv_one, gains, gain_two_sums, blocks,
    )
    return (
        block_out,
        grad_in,
        gain_sums[0],
        grad_rec_in,
        grad_rec_gate,
        vector_grads[0:4],
        vector_grads[4],
        grad_rate[None],
        vector_grads[5],
        grad_input[None],
        vector_grads[6],
        vector_grads[7],
        grad_out,
        gain_sums[1],
        grad_gate.T,
        grad_up,
        grad_down,
    )


def solution(mesh):
    fine = Mesh(mesh.devices.reshape(2, 4, 4, 2, 2), ("ylo", "x", "z", "yhi", "core"))
    both = P(SEQ, HEAD)
    swap = P(HEAD, SEQ)
    vector = P(HEAD)
    stack = P(HEAD, None, None)
    taps = P(None, HEAD)
    return jax.shard_map(
        per_device,
        mesh=fine,
        in_specs=(
            both, both, vector, both, both, taps, vector, stack, vector, stack, vector, vector,
            swap, vector, both, both, swap,
        ),
        out_specs=(
            both, both, vector, both, both, taps, vector, stack, vector, stack, vector, vector,
            swap, vector, both, both, swap,
        ),
        check_vma=False,
    )
```

```python
import jax
import jax.numpy as jnp
from jax import lax
from jax.experimental import pallas as pl
from jax.experimental.pallas import tpu as pltpu
from jax.sharding import Mesh, PartitionSpec as P

D = 2048
CONV = 4
EPS = 1e-06
TOK = 512
CH = 640
HW = 160
TAILS = ((0, 48), (48, 48), (96, 48), (144, 16))
SQUARE = 208
PACKED = 2 * SQUARE + 32
MESH = pl.DeviceIdType.MESH
SEQ = ("ylo", "x")
HEAD = ("z", "yhi", "core")
QUAD = ("yhi", "core")
PLANE = ("ylo", "x", "yhi", "core")
bf = jnp.bfloat16
f32 = jnp.float32
VMEM = pl.BlockSpec(memory_space=pltpu.VMEM)
ANY = pl.BlockSpec(memory_space=pl.ANY)


def shape(dims, dtype):
    return jax.ShapeDtypeStruct(dims, dtype)


def params(cid):
    return pltpu.CompilerParams(
        collective_id=cid, has_side_effects=True, vmem_limit_bytes=60 * 2**20
    )


def quad_device(index):
    return {"yhi": index // 2, "core": lax.rem(index, 2)}


def plane_device(block):
    return {
        "ylo": block // 16,
        "x": lax.rem(block // 4, 4),
        "yhi": lax.rem(block // 2, 2),
        "core": lax.rem(block, 2),
    }


def meet(devices):
    barrier = pltpu.get_barrier_semaphore()
    for device in devices:
        pl.semaphore_signal(barrier, inc=1, device_id=device, device_id_type=MESH)
    pl.semaphore_wait(barrier, len(devices))


def place():
    ylo, x, yhi, core = (lax.axis_index(n) for n in ("ylo", "x", "yhi", "core"))
    return ylo, x, yhi, core

def x_device(i):
    return {"x": i}

def y_device(i):
    return {"yhi": i // 2, "ylo": lax.rem(i, 2)}

def around(i):
    return lax.rem(i + 1, 4), lax.rem(i + 3, 4), lax.rem(i + 2, 4)

def plane_neighbours():
    ylo, x, yhi, core = place()
    y = yhi * 2 + ylo
    xr, xl, _ = around(x)
    yr, yl, _ = around(y)
    return [x_device(xr), x_device(xl), y_device(yr), y_device(yl), {"core": 1 - core}]

class Sender:
    def __init__(self, send, recv, base=0):
        self.send, self.recv, self.base, self.all = send, recv, base, []

    def __call__(self, source, target, device):
        i = self.base + len(self.all)
        copy = pltpu.make_async_remote_copy(
            src_ref=source,
            dst_ref=target,
            send_sem=self.send.at[i],
            recv_sem=self.recv.at[i],
            device_id=device,
            device_id_type=MESH,
        )
        copy.start()
        self.all.append(copy)
        return copy

    def drain(self, skip=None):
        for copy in self.all:
            if copy is not skip:
                copy.wait_send()


class Keeper:
    def __init__(self, done):
        self.done, self.count, self.open = done, 0, []

    def __call__(self, source, target):
        copy = pltpu.make_async_copy(source, target, self.done.at[self.count])
        copy.start()
        self.count += 1
        self.open.append(copy)
        return copy

    def wait(self, copy):
        self.open = [c for c in self.open if c is not copy]
        copy.wait()

    def drain(self):
        for copy in self.open:
            copy.wait()


def semaphores(count):
    return [pltpu.SemaphoreType.DMA((count,)), pltpu.SemaphoreType.DMA((count,))]


def got(copies):
    for copy in copies:
        copy.wait_recv()


def step(*plans):
    for plan in plans:
        next(plan, None)


def finish(*plans):
    for plan in plans:
        for _ in plan:
            pass


def z_columns(block):
    return pl.ds(pl.multiple_of(block * 512, 512), 512)


def ring_gather(full, put):
    z = lax.axis_index("z")
    right, left, _ = around(z)
    half = full.shape[0] // 2

    def start(row, block, to):
        part = full.at[pl.ds(row, half), z_columns(block)]
        return put(part, part, {"z": to})

    c0 = start(0, z, right)
    c1 = start(half, z, left)
    c2 = start(half, z, right)
    c3 = start(0, z, left)
    yield
    c0.wait_recv()
    c4 = start(0, left, right)
    c1.wait_recv()
    c5 = start(half, right, left)
    yield
    got([c2, c3, c4, c5])


def ring_sum(part, out, came, sent, put, produce=lambda block: None):
    z = lax.axis_index("z")
    right, left, far = around(z)
    half = part.shape[0] // 2
    lo, hi = pl.ds(0, half), pl.ds(half, half)
    cols = z_columns

    def start(i, source, to):
        return put(source, came.at[i], {"z": to})

    produce(far)
    c0 = start(0, part.at[lo, cols(far)], right)
    c1 = start(1, part.at[hi, cols(far)], left)
    produce(right)
    c2 = start(2, part.at[hi, cols(right)], right)
    produce(left)
    c3 = start(3, part.at[lo, cols(left)], left)
    produce(z)
    yield
    c0.wait_recv()
    sent[0] = came[0] + part[lo, cols(right)]
    c4 = start(4, sent.at[0], right)
    c1.wait_recv()
    sent[1] = came[1] + part[hi, cols(left)]
    c5 = start(5, sent.at[1], left)
    yield
    got([c3, c4])
    out[lo, :] = part[lo, cols(z)].astype(f32) + came[3].astype(f32) + came[4].astype(f32)
    got([c2, c5])
    out[hi, :] = part[hi, cols(z)].astype(f32) + came[2].astype(f32) + came[5].astype(f32)


def ring_scratch():
    return [pltpu.VMEM((6, TOK // 2, 512), bf), pltpu.VMEM((2, TOK // 2, 512), bf)]


def z_others():
    z = lax.axis_index("z")
    return [{"z": lax.rem(z + j, 4)} for j in (1, 2, 3)]


def quad_others():
    me = lax.axis_index("yhi") * 2 + lax.axis_index("core")
    return [quad_device(lax.rem(me + j, 4)) for j in (1, 2, 3)]


def quad_gather(tokens, full, put, keep):
    z = lax.axis_index("z")
    me = lax.axis_index("yhi") * 2 + lax.axis_index("core")
    mine = pl.ds(pl.multiple_of(z * 512 + me * 128, 128), 128)
    copies = []
    for j in (1, 2, 3):
        peer = lax.rem(me + j, 4)
        source = tokens.at[pl.ds(pl.multiple_of(peer * TOK, TOK), TOK), :]
        copies.append(put(source, full.at[:, mine], quad_device(peer)))
    own = keep(tokens.at[pl.ds(pl.multiple_of(me * TOK, TOK), TOK), :], full.at[:, mine])
    return copies, own


def token_gather(tokens, full, put, keep):
    copies, own = quad_gather(tokens, full, put, keep)
    yield
    got(copies)
    keep.wait(own)
    yield from ring_gather(full, put)


def quad_scatter(own, tokens, put, keep):
    me = lax.axis_index("yhi") * 2 + lax.axis_index("core")
    rows = pl.ds(pl.multiple_of(me * TOK, TOK), TOK)
    copies = []
    for j in (1, 2, 3):
        peer = lax.rem(me + j, 4)
        source = own.at[:, pl.ds(pl.multiple_of(peer * 128, 128), 128)]
        copies.append(put(source, tokens.at[rows, :], quad_device(peer)))
    mine = keep(own.at[:, pl.ds(pl.multiple_of(me * 128, 128), 128)], tokens.at[rows, :])
    return copies, mine


GATHER_COPIES = 48
SUM_COPIES = 36
SUM_KEEPS = 8


HALF = TOK // 2
UNIT = 256


CUTS = ((0, 256), (256, 256), (512, 128))


def rec_grad(left, right, into):
    for at, width in CUTS:
        for k in range(4):
            cols = slice(512 * k, 512 * k + 512)
            into[at : at + width, cols] = lax.dot_general(
                left[:, at : at + width], right[:, cols], (((0,), (0,)), ((), ())), preferred_element_type=f32
            ).astype(bf)


def middle_kernel(
    hy_in, rec_in, x_in, cot_in, gate_in, up_in, own_down, gains,
    zown_out, dz_out, dhy_out, mlp_out, out_grad, down_grad, gate_grad, up_grad, gain_sums,
    hy, w_out, x, cot, w_gate, w_up, w_down, normed, mixed, part, part_two, back, act, dg, du, mlp,
    own_one, own_two, inv, inner, dhy, *rest,
):
    rings, (send, recv, done) = rest[:8], rest[8:]
    z = lax.axis_index("z")
    keep = Keeper(done)
    load_mix = [keep(hy_in, hy), keep(rec_in.at[2], w_out)]
    load_norm = [keep(x_in, x)]
    load_mlp = [keep(gate_in, w_gate), keep(up_in, w_up), keep(cot_in, cot)]
    meet(z_others() + plane_neighbours())
    put = Sender(send, recv)
    plane = plane_gather(own_down, w_down, put, keep)
    step(plane)
    puts = [Sender(send, recv, GATHER_COPIES + 12 * i) for i in range(4)]

    def rows_of(half):
        return pl.ds(HALF * half, HALF)

    def view(ref, half):
        return ref.at[rows_of(half), :]

    def wide(ref, rows, times):
        return jnp.concatenate([ref[rows, :]] * times, axis=1)

    def mix_block(half):
        def produce(at):
            part[rows_of(half), z_columns(at)] = jnp.dot(
                hy[rows_of(half), :], w_out[:, z_columns(at)], preferred_element_type=f32
            ).astype(bf)

        return produce

    def sums(i, half, source, own, produce):
        return ring_sum(
            view(source, half), view(own, half), rings[2 * i], rings[2 * i + 1], puts[i], produce
        )

    def spread(i, half, full, own):
        full[rows_of(half), z_columns(z)] = own[rows_of(half), :].astype(bf)
        return ring_gather(view(full, half), puts[i])

    def norm(half):
        def body(i):
            r = pl.ds(pl.multiple_of(HALF * half + i * 16, 16), 16)
            values = x[r, :].astype(f32) + mixed[r, :].astype(f32)
            mean = jnp.sum(values * values, axis=1, keepdims=True) * (1.0 / D)
            scale = lax.rsqrt(mean + EPS)
            inv[r, :] = jnp.broadcast_to(scale, (16, 128))
            normed[r, :] = (values * scale * gains[1:2, :]).astype(bf)

        loop(HALF // 16, body)

    def hidden(half, first, count):
        r = rows_of(half)

        def body(j):
            at = pl.ds(pl.multiple_of((first + j) * UNIT, UNIT), UNIT)

            def against(left, right):
                return lax.dot_general(
                    left, right[at, :], (((1,), (1,)), ((), ())), preferred_element_type=f32
                )

            g = against(normed[r, :], w_gate)
            u = against(normed[r, :], w_up)
            da = against(cot[r, :], w_down)
            value, slope = gelu_parts(g)
            act[r, at] = (value * u).astype(bf)
            low_g = (da * u * slope).astype(bf)
            low_u = (da * value).astype(bf)
            dg[r, at] = low_g
            du[r, at] = low_u
            t = low_g.astype(f32) * g + low_u.astype(f32) * u
            inner[r, :] = inner[r, :] + (t[:, :128] + t[:, 128:])

        loop(count, body)

    def close(half):
        r = rows_of(half)
        total = jnp.sum(inner[r, :], axis=1, keepdims=True) * (1.0 / D)
        inner[r, :] = inv[r, :] * inv[r, :] * total

    def back_block(half):
        r = rows_of(half)

        def produce(at):
            cols = z_columns(at)
            dn = jnp.dot(dg[r, :], w_gate[:, cols], preferred_element_type=f32)
            dn = dn + jnp.dot(du[r, :], w_up[:, cols], preferred_element_type=f32)
            values = x[r, cols].astype(f32) + mixed[r, cols].astype(f32)
            scaled = dn * wide(inv, r, 4)
            part_two[r, cols] = (scaled * gains[1:2, cols] - values * wide(inner, r, 4)).astype(bf)
            gain_sums[:, cols] = gain_sums[:, cols] + jnp.sum(
                (scaled * values).reshape(HALF // 8, 8, 512), axis=0
            )

        return produce

    def mlp_blocks():
        for at in range(4):
            cols = slice(512 * at, 512 * at + 512)
            mlp[:, cols] = jnp.dot(act[...], w_down[:, cols], preferred_element_type=f32).astype(bf)

    def weight_grad(left, right, into, target):
        def body(j):
            at = pl.ds(pl.multiple_of(j * UNIT, UNIT), UNIT)
            for k in range(4):
                cols = slice(512 * k, 512 * k + 512)
                into[at, cols] = lax.dot_general(
                    left[:, at], right[:, cols], (((0,), (0,)), ((), ())), preferred_element_type=f32
                ).astype(bf)

        loop(1536 // UNIT, body)
        keep(into, target)

    def add_own(half, whole, own):
        r = rows_of(half)
        own[r, :] = own[r, :] + whole[r, z_columns(z)].astype(f32)

    def add_cotangent(half):
        def body(i):
            r = pl.ds(pl.multiple_of(HALF * half + i * 16, 16), 16)
            back[r, :] = cot[r, :] + back[r, :]

        loop(HALF // 16, body)

    for copy in load_mix:
        keep.wait(copy)
    inner[...] = jnp.zeros((TOK, 128), f32)
    gain_sums[...] = jnp.zeros((8, D), f32)
    sum_a = sums(0, 0, part, own_one, mix_block(0))
    sum_b = sums(1, 1, part, own_one, mix_block(1))
    step(sum_a, sum_a)
    step(plane, sum_b)
    finish(sum_a)
    spread_a = spread(0, 0, mixed, own_one)
    step(spread_a, sum_b, plane, spread_a)
    finish(sum_b)
    spread_b = spread(1, 1, mixed, own_one)
    step(spread_b)
    finish(spread_a)
    for copy in load_norm:
        keep.wait(copy)
    add_own(0, x, own_one)
    norm(0)
    step(spread_b, plane)
    for copy in load_mlp:
        keep.wait(copy)
    finish(plane)
    hidden(0, 0, 3)
    finish(spread_b)
    add_own(1, x, own_one)
    keep(own_one, zown_out)
    hidden(0, 3, 3)
    close(0)
    total_a = sums(2, 0, part_two, own_two, back_block(0))
    step(total_a)
    norm(1)
    step(total_a)
    hidden(1, 0, 3)
    finish(total_a)
    back_a = spread(2, 0, back, own_two)
    step(back_a)
    hidden(1, 3, 2)
    step(back_a)
    hidden(1, 5, 1)
    close(1)
    total_b = sums(3, 1, part_two, own_two, back_block(1))
    step(total_b)
    finish(back_a)
    puts[2].drain()
    add_cotangent(0)
    add_own(0, cot, own_two)
    step(total_b)
    mlp_blocks()
    keep(mlp, mlp_out)
    put.drain()
    finish(total_b)
    back_b = spread(3, 1, back, own_two)
    step(back_b)
    weight_grad(act, cot, w_down, down_grad)
    step(back_b)
    weight_grad(dg, normed, w_gate, gate_grad)
    weight_grad(du, normed, w_up, up_grad)
    finish(back_b)
    puts[3].drain()
    add_cotangent(1)
    for at, width in CUTS:
        dhy[:, at : at + width] = lax.dot_general(
            back[...], w_out[at : at + width, :], (((1,), (1,)), ((), ())), preferred_element_type=f32
        )
    keep(dhy, dhy_out)
    add_own(1, cot, own_two)
    keep(own_two, dz_out)
    rec_grad(hy, back, w_out)
    keep(w_out, out_grad)
    puts[0].drain()
    puts[1].drain()
    keep.drain()


def middle(*operands):
    mlp = shape((1536, D), bf)
    rows = shape((TOK, D), bf)
    own = shape((TOK, 512), f32)
    row_scratch = pltpu.VMEM((TOK, D), bf)
    weight = pltpu.VMEM((1536, D), bf)
    unit = pltpu.VMEM((TOK, 1536), bf)
    return pl.pallas_call(
        middle_kernel,
        out_shape=(
            own, own, shape((TOK, CH), f32), rows, shape((CH, D), bf), mlp, mlp, mlp, shape((8, D), f32),
        ),
        in_specs=[ANY] * 7 + [VMEM],
        out_specs=[ANY] * 8 + [VMEM],
        scratch_shapes=[
            pltpu.VMEM((TOK, CH), bf),
            pltpu.VMEM((CH, D), bf),
            row_scratch,
            row_scratch,
            weight,
            weight,
            weight,
            row_scratch,
            row_scratch,
            row_scratch,
            row_scratch,
            row_scratch,
            unit,
            unit,
            unit,
            row_scratch,
            pltpu.VMEM((TOK, 512), f32),
            pltpu.VMEM((TOK, 512), f32),
            pltpu.VMEM((TOK, 128), f32),
            pltpu.VMEM((TOK, 128), f32),
            pltpu.VMEM((TOK, CH), f32),
        ]
        + 4 * [pltpu.VMEM((6, HALF // 2, 512), bf), pltpu.VMEM((2, HALF // 2, 512), bf)]
        + semaphores(GATHER_COPIES + 48)
        + [pltpu.SemaphoreType.DMA((16,))],
        compiler_params=params(3),
        name="middle",
    )(*operands)


def cut(r):
    a = (r // 32) * 16
    a1 = ((a // 16 + 1) // 2) * 16
    b1 = (((r - a) // 16 + 1) // 2) * 16
    return a, a1, b1

def plane_gather(own, full, put, keep):
    r = own.shape[-2]
    lead = (slice(None),) * (len(own.shape) - 2)
    ylo, x, yhi, core = place()
    y = yhi * 2 + ylo
    xr, xl, xf = around(x)
    yr, yl, yf = around(y)
    a, a1, b1 = cut(r)
    top, bottom = (0, a), (a, r - a)
    top1, top2 = (0, a1), (a1, a - a1)
    bot1, bot2 = (a, b1), (a + b1, r - a - b1)

    def span(quarter, rows):
        return pl.ds(pl.multiple_of(quarter * r + rows[0], 16), rows[1])

    sib = {"core": 1 - core}
    def cols(lo, xx):
        return pl.ds(pl.multiple_of(lo * 1024 + xx * 256, 256), 256)
    def one(rows, yy, xx):
        return full.at[lead + (span((yy // 2) * 2 + core, rows), cols(lax.rem(yy, 2), xx))]
    def row(rows, yy):
        return full.at[lead + (span((yy // 2) * 2 + core, rows), pl.ds(pl.multiple_of(lax.rem(yy, 2) * 1024, 1024), 1024))]
    kept = keep(own, one((0, r), y, x))
    ha, hb = own.at[lead + (pl.ds(*top),)], own.at[lead + (pl.ds(*bottom),)]
    p = [put(ha, one(top, y, x), x_device(xr)), put(ha, one(top, y, x), x_device(xl)),
         put(hb, one(bottom, y, x), y_device(yr)), put(hb, one(bottom, y, x), y_device(yl))]
    yield
    got(p)
    keep.wait(kept)
    p = [put(one(top1, y, xl), one(top1, y, xl), x_device(xr)), put(one(top2, y, xr), one(top2, y, xr), x_device(xl)),
         put(one(bot1, yl, x), one(bot1, yl, x), y_device(yr)), put(one(bot2, yr, x), one(bot2, yr, x), y_device(yl))]
    yield
    got(p)
    def pieces(rows, xx):
        out = []
        for lo in (0, 1):
            for hi in (0, 1):
                out.append(full.at[lead + (span(2 * hi + core, rows), cols(lo, xx))])
        return out
    def send_row(rows, yy, device):
        return [put(row(rows, yy), row(rows, yy), device)]
    def send_col(rows, xx, device):
        return [put(s, s, device) for s in pieces(rows, xx)]
    p = send_row(top, y, y_device(yr)) + send_row(top, y, y_device(yl))
    p += send_col(bottom, x, x_device(xr)) + send_col(bottom, x, x_device(xl))
    s = send_row(top, y, sib) + send_col(bottom, x, sib)
    yield
    got(p)
    p = send_row(top1, yl, y_device(yr)) + send_row(top2, yr, y_device(yl))
    p += send_col(bot1, xl, x_device(xr)) + send_col(bot2, xr, x_device(xl))
    s += send_row(top, yl, sib) + send_row(top, yr, sib) + send_col(bottom, xl, sib) + send_col(bottom, xr, sib)
    yield
    got(p)
    s += send_row(top, yf, sib) + send_col(bottom, xf, sib)
    yield
    got(s)


def plane_sum(parts, out, scratch, put, keep):
    own, fold, ga, gb, ha, hb, sa, sb, ra2, rb2 = scratch
    r = fold.shape[1]
    ylo, x, yhi, core = place()
    y = yhi * 2 + ylo
    xr, xl, xf = around(x)
    yr, yl, yf = around(y)
    a = -(-r // 64) * 32
    h, g = a // 2, (r - a) // 2
    sib = {"core": 1 - core}
    pieces = ([], [])
    at = 0
    for part in parts:
        size = part.shape[0] // 4
        middle = min(max(a - at, 0), size)
        for group, first, count in ((0, 0, middle), (1, middle, size - middle)):
            if count:
                pieces[group].append((part, size, first, count, at + first))
        at += size
    came = ([], [])
    held = ([], [])
    for group in (0, 1):
        for part, size, first, count, to in pieces[group]:

            def quarter(q):
                return part.at[pl.ds(pl.multiple_of(q * size + first, 16), count), :]

            for hi in (0, 1):
                into = pl.ds(to, count)
                came[group].append(put(quarter(2 * hi + 1 - core), fold.at[hi, into, :], sib))
                held[group].append(keep(quarter(2 * hi + core), own.at[hi, into, :]))
    yield

    def add_cores(group):
        got(came[group])
        for copy in held[group]:
            keep.wait(copy)
        first, count = ((0, a), (a, r - a))[group]
        for hi in (0, 1):

            def body(i, carry, hi=hi):
                rr = pl.ds(pl.multiple_of(first + i * 16, 16), 16)
                fold[hi, rr, :] = fold[hi, rr, :] + own[hi, rr, :]
                return carry

            lax.fori_loop(0, count // 16, body, 0)

    def ycols(yy):
        return pl.ds(pl.multiple_of(lax.rem(yy, 2) * 1024, 1024), 1024)
    def a_block(yy, first):
        return fold.at[yy // 2, pl.ds(0 if first else h, h), ycols(yy)]
    def b_block(xx, first, l):
        return fold.at[:, pl.ds(a + (0 if first else g), g), pl.ds(pl.multiple_of(l * 1024 + xx * 256, 256), 256)]
    yR, yL, xR, xL = y_device(yr), y_device(yl), x_device(xr), x_device(xl)
    def sendb(i, xx, first, dev):
        return [put(b_block(xx, first, l), gb.at[i, l], dev) for l in (0, 1)]
    add_cores(0)
    pa = [put(a_block(yf, True), ga.at[0], yR), put(a_block(yf, False), ga.at[1], yL)]
    pa += [put(a_block(yr, False), ga.at[2], yR), put(a_block(yl, True), ga.at[3], yL)]
    add_cores(1)
    pb = [sendb(0, xf, True, xR), sendb(1, xf, False, xL)]
    pb += [sendb(2, xr, False, xR), sendb(3, xl, True, xL)]
    yield

    def add_a(dst, i, block, n):
        def body(j, carry):
            rr = pl.ds(pl.multiple_of(j * 16, 16), 16)
            dst[rr, :] = ga[i, rr, :] + block[rr, :]
            return carry
        lax.fori_loop(0, n // 16, body, 0)
    def add_b(dst, i, xx, first):
        for l in (0, 1):
            for hi in (0, 1):
                block = fold.at[hi, pl.ds(a + (0 if first else g), g), pl.ds(pl.multiple_of(l * 1024 + xx * 256, 256), 256)]
                def body(j, carry):
                    rr = pl.ds(pl.multiple_of(j * 16, 16), 16)
                    dst[l, hi, rr, :] = gb[i, l, hi, rr, :] + block[rr, :]
                    return carry
                lax.fori_loop(0, g // 16, body, 0)
    pa[0].wait_recv()
    add_a(sa.at[0], 0, a_block(yr, True), h)
    pa.append(put(sa.at[0], ga.at[4], yR))
    got(pb[0])
    add_b(sb.at[0], 0, xr, True)
    pb.append([put(sb.at[0], gb.at[4], xR)])
    pa[1].wait_recv()
    add_a(sa.at[1], 1, a_block(yl, False), h)
    pa.append(put(sa.at[1], ga.at[5], yL))
    got(pb[1])
    add_b(sb.at[1], 1, xl, False)
    pb.append([put(sb.at[1], gb.at[5], xL)])
    yield
    def fin_a(first, i, j):
        def body(n, carry):
            rr = pl.ds(pl.multiple_of(n * 16, 16), 16)
            block = a_block(y, first)
            ra2[pl.ds(pl.multiple_of((0 if first else h) + n * 16, 16), 16), :] = (
                block[rr, :].astype(f32) + ga[i, rr, :].astype(f32) + ga[j, rr, :].astype(f32)).astype(bf)
            return carry
        lax.fori_loop(0, h // 16, body, 0)
    def fin_b(first, i, j):
        for l in (0, 1):
            for hi in (0, 1):
                block = fold.at[hi, pl.ds(a + (0 if first else g), g), pl.ds(pl.multiple_of(l * 1024 + x * 256, 256), 256)]
                def body(n, carry):
                    rr = pl.ds(pl.multiple_of(n * 16, 16), 16)
                    rb2[l, hi, pl.ds(pl.multiple_of((0 if first else g) + n * 16, 16), 16), :] = (
                        block[rr, :].astype(f32) + gb[i, l, hi, rr, :].astype(f32) + gb[j, l, hi, rr, :].astype(f32)).astype(bf)
                    return carry
                lax.fori_loop(0, g // 16, body, 0)
    got([pa[3], pa[4]])
    fin_a(True, 3, 4)
    got([pa[2], pa[5]])
    fin_a(False, 2, 5)
    got(pb[3] + pb[4])
    fin_b(True, 3, 4)
    got(pb[2] + pb[5])
    fin_b(False, 2, 5)
    def a2(xx, first):
        return ra2.at[pl.ds(0 if first else h, h), pl.ds(pl.multiple_of(xx * 256, 256), 256)]
    def b2(yy, first):
        return rb2.at[lax.rem(yy, 2), yy // 2, pl.ds(0 if first else g, g), :]
    qa = [put(a2(xf, True), ha.at[0], xR), put(a2(xf, False), ha.at[1], xL), put(a2(xr, False), ha.at[2], xR), put(a2(xl, True), ha.at[3], xL)]
    qb = [put(b2(yf, True), hb.at[0], yR), put(b2(yf, False), hb.at[1], yL), put(b2(yr, False), hb.at[2], yR), put(b2(yl, True), hb.at[3], yL)]
    yield
    sa2, sb2 = ha.at[pl.ds(6, 2)], hb.at[pl.ds(6, 2)]
    qa[0].wait_recv()
    sa2[0] = ha[0] + a2(xr, True)[...]
    qa.append(put(sa2.at[0], ha.at[4], xR))
    qb[0].wait_recv()
    sb2[0] = hb[0] + b2(yr, True)[...]
    qb.append(put(sb2.at[0], hb.at[4], yR))
    qa[1].wait_recv()
    sa2[1] = ha[1] + a2(xl, False)[...]
    qa.append(put(sa2.at[1], ha.at[5], xL))
    qb[1].wait_recv()
    sb2[1] = hb[1] + b2(yl, False)[...]
    qb.append(put(sb2.at[1], hb.at[5], yL))
    yield
    got(qa[2:] + qb[2:])
    def w(v): return v.astype(f32)
    out[0:h, :] = w(a2(x, True)[...]) + w(ha[3]) + w(ha[4])
    out[h:a, :] = w(a2(x, False)[...]) + w(ha[2]) + w(ha[5])
    out[a:a + g, :] = w(b2(y, True)[...]) + w(hb[3]) + w(hb[4])
    out[a + g:, :] = w(b2(y, False)[...]) + w(hb[2]) + w(hb[5])


SUM_SCRATCH = 10


def sum_scratch(r):
    a = -(-r // 64) * 32
    h, g = a // 2, (r - a) // 2
    V = pltpu.VMEM
    return [V((2, r, 2048), bf), V((2, r, 2048), bf), V((6, h, 1024), bf), V((6, 2, 2, g, 256), bf), V((8, h, 256), bf), V((8, g, 256), bf),
            V((2, h, 1024), bf), V((2, 2, 2, g, 256), bf), V((a, 1024), bf), V((2, 2, r - a, 256), bf)]


def small_sums(blocks, gains, small, gain, scratch, put):
    zgot, sgot, pair, pgot, qgain, rgot, rgain, mine = scratch
    z = lax.axis_index("z")
    yhi, core = lax.axis_index("yhi"), lax.axis_index("core")
    me = yhi * 2 + core
    row = lax.axis_index("ylo") * 4 + lax.axis_index("x")
    zs = []
    near = [put(blocks.at[2 * hi + 1 - core], sgot.at[hi], {"core": 1 - core}) for hi in (0, 1)]
    for j in (1, 2, 3):
        to = lax.rem(z + j, 4)
        zs.append(put(gains.at[to], zgot.at[j - 1], {"z": to}))
    yield
    got(near)
    for hi in (0, 1):
        pair[hi] = blocks[2 * hi + core] + sgot[hi]
    across = put(pair.at[1 - yhi], pgot, {"yhi": 1 - yhi})
    got(zs)
    qgain[3] = gains[z] + zgot[0] + zgot[1] + zgot[2]
    qs = []
    for j in (1, 2, 3):
        to = lax.rem(me + j, 4)
        qs.append(put(qgain.at[3, to], qgain.at[j - 1, 0], quad_device(to)))
    yield
    got(qs)
    across.wait_recv()
    mine[...] = pair[yhi] + pgot[...]
    rgain[7] = qgain[3, me] + qgain[0, 0] + qgain[1, 0] + qgain[2, 0]
    rs = []
    size = PACKED // 8

    def seq(j):
        to = lax.rem(row + j, 8)
        return to, {"ylo": to // 4, "x": lax.rem(to, 4)}

    for j in range(1, 8):
        to, device = seq(j)
        rs.append(put(mine.at[pl.ds(pl.multiple_of(to * size, 8), size), :], rgot.at[j - 1], device))
        rs.append(put(rgain.at[7], rgain.at[j - 1], device))
    yield
    got(rs)
    own = pl.ds(pl.multiple_of(row * size, 8), size)
    total = mine[own, :]
    gain_total = rgain[7]
    for j in range(7):
        total = total + rgot[j]
        gain_total = gain_total + rgain[j]
    small[own, :] = total
    gain[...] = gain_total
    ag = []
    for j in range(1, 8):
        _, device = seq(j)
        ag.append(put(small.at[own, :], small.at[own, :], device))
    yield
    got(ag)


SMALL_SCRATCH = 8
SMALL_COPIES = 30


def small_scratch():
    return [
        pltpu.VMEM((3, 4, 8, 128), f32),
        pltpu.VMEM((2, PACKED, 128), f32),
        pltpu.VMEM((2, PACKED, 128), f32),
        pltpu.VMEM((PACKED, 128), f32),
        pltpu.VMEM((4, 4, 8, 128), f32),
        pltpu.VMEM((7, PACKED // 8, 128), f32),
        pltpu.VMEM((8, 8, 128), f32),
        pltpu.VMEM((PACKED, 128), f32),
    ]


def tail_kernel(
    dxb_in, dyb_in, xb_in, yb_in, rec_weights, x_in, n_in, dz_in, rec_out, up, inv, gains, gain_two, blocks,
    grad_in, in_grad, gate_grad, out_grad, up_grad, rate_grad, input_grad, vec_grad, gain,
    dxb, dyb, xb, yb, w_in, w_gate, x, normed, dz, part, own, low, coef, gain_one, gain_parts,
    part_in, part_gate, rec_sum, up_sum, small, back_low, *rest,
):
    (came, sent), rest = rest[:2], rest[2:]
    plane_refs, rest = rest[:SUM_SCRATCH], rest[SUM_SCRATCH:]
    up_refs, rest = rest[:SUM_SCRATCH], rest[SUM_SCRATCH:]
    small_refs, rest = rest[:SMALL_SCRATCH], rest[SMALL_SCRATCH:]
    send, recv, done = rest
    keep = Keeper(done)
    first = [keep(*pair) for pair in ((dxb_in, dxb), (dyb_in, dyb), (n_in, normed))]
    second = [keep(xb_in, xb), keep(yb_in, yb)]
    third = [
        keep(*pair) for pair in ((rec_weights.at[0], w_in), (rec_weights.at[1], w_gate), (x_in, x))
    ]
    fourth = keep(dz_in, dz)
    meet(z_others() + plane_neighbours() + line_devices())
    put = Sender(send, recv)
    plane_up = plane_sum([up], up_sum, up_refs, put, keep)
    step(plane_up)
    for copy in first:
        keep.wait(copy)
    rec_grad(dxb, normed, part_in)
    rec_grad(dyb, normed, part_gate)
    plane = plane_sum([part_in, part_gate, rec_out], rec_sum, plane_refs, put, keep)
    step(plane)
    for copy in second:
        keep.wait(copy)

    def inner(i):
        r = pl.ds(pl.multiple_of(i * 16, 16), 16)
        terms = dxb[r, :].astype(f32) * xb[r, :] + dyb[r, :].astype(f32) * yb[r, :]
        total = jnp.sum(terms, axis=1, keepdims=True) * (1.0 / D)
        coef[r, :] = inv[r, :] * inv[r, :] * total

    loop(TOK // 16, inner)
    gain_one[...] = jnp.zeros((8, D), f32)
    step(plane_up)
    for copy in third:
        keep.wait(copy)

    def produce(at):
        cols = z_columns(at)
        for half in (0, 1):
            r = slice(HALF * half, HALF * (half + 1))
            dn = jnp.dot(dxb[r, :], w_in[:, cols], preferred_element_type=f32)
            dn = dn + jnp.dot(dyb[r, :], w_gate[:, cols], preferred_element_type=f32)
            values = x[r, cols].astype(f32)
            scaled = dn * jnp.concatenate([inv[r, :]] * 4, axis=1)
            less = values * jnp.concatenate([coef[r, :]] * 4, axis=1)
            part[r, cols] = (scaled * gains[0:1, cols] - less).astype(bf)
            gain_one[:, cols] = gain_one[:, cols] + jnp.sum(
                (scaled * values).reshape(HALF // 8, 8, 512), axis=0
            )

    total = ring_sum(part, own, came, sent, put, produce)
    step(total)
    sums_one = jnp.sum(gain_one[...], axis=0, keepdims=True)
    sums_two = jnp.sum(gain_two[...], axis=0, keepdims=True)
    gain_parts[...] = jnp.zeros((4, 4, 8, 128), f32)
    for i in range(4):
        for j in range(4):
            cols = slice(128 * (4 * i + j), 128 * (4 * i + j + 1))
            gain_parts[i, j, 0:1, :] = sums_one[:, cols]
            gain_parts[i, j, 1:2, :] = sums_two[:, cols]
    little = small_sums(blocks, gain_parts, small, gain, small_refs, put)
    step(little)
    step(plane, total, plane_up, little)
    step(plane_up, plane)
    finish(total)
    keep.wait(fourth)
    low[...] = (own[...] + dz[...]).astype(bf)
    back, mine = quad_scatter(low, back_low, put, keep)
    step(little, plane_up, plane, little)
    finish(plane_up)
    up_grad[...] = up_sum[...].T
    got(back)
    keep.wait(mine)

    def widen(i):
        r = pl.ds(pl.multiple_of(i * 64, 64), 64)
        grad_in[r, :] = back_low[r, :].astype(f32)

    loop(4 * TOK // 64, widen)
    step(plane)
    finish(little)
    for k, target in ((0, rate_grad), (1, input_grad)):
        top = SQUARE * k
        target[:, 0:128] = small[top : top + HW, :]
        for j, (at, size) in enumerate(TAILS):
            target[at : at + size, 128:HW] = small[top + HW : top + HW + size, 32 * j : 32 * j + 32]
    vec_grad[:, 0:128] = small[2 * SQUARE : 2 * SQUARE + 8, :]
    vec_grad[:, 128:HW] = small[2 * SQUARE + 16 : 2 * SQUARE + 24, 0:32]
    finish(plane)
    in_grad[...] = rec_sum[0:HW, :].T
    gate_grad[...] = rec_sum[HW : 2 * HW, :].T
    out_grad[...] = rec_sum[2 * HW :, :]
    put.drain()
    keep.drain()


def tail(*operands):
    rows = pltpu.VMEM((TOK, D), bf)
    tall = pltpu.VMEM((TOK, CH), f32)
    low = pltpu.VMEM((TOK, CH), bf)
    weight = pltpu.VMEM((CH, D), bf)
    return pl.pallas_call(
        tail_kernel,
        out_shape=(
            shape((4 * TOK, 128), f32),
            shape((256, HW), f32),
            shape((256, HW), f32),
            shape((HW, 256), f32),
            shape((256, 384), f32),
            shape((HW, HW), f32),
            shape((HW, HW), f32),
            shape((8, HW), f32),
            shape((8, 128), f32),
        ),
        in_specs=[ANY] * 10 + [VMEM] * 4,
        out_specs=[VMEM] * 9,
        scratch_shapes=[
            low, low, tall, tall, weight, weight, rows, rows,
            pltpu.VMEM((TOK, 512), f32),
            rows,
            pltpu.VMEM((TOK, 512), f32),
            pltpu.VMEM((TOK, 512), bf),
            pltpu.VMEM((TOK, 128), f32),
            pltpu.VMEM((8, D), f32),
            pltpu.VMEM((4, 4, 8, 128), f32),
            weight, weight,
            pltpu.VMEM((3 * HW, 256), f32),
            pltpu.VMEM((384, 256), f32),
            pltpu.VMEM((PACKED, 128), f32),
            pltpu.VMEM((4 * TOK, 128), bf),
        ]
        + ring_scratch()
        + sum_scratch(3 * HW)
        + sum_scratch(384)
        + small_scratch()
        + semaphores(6 + 3 + 2 * SUM_COPIES + SMALL_COPIES)
        + [pltpu.SemaphoreType.DMA((2 * SUM_KEEPS + 10,))],
        compiler_params=params(5),
        name="tail",
    )(*operands)


def line_devices():
    ylo, x = lax.axis_index("ylo"), lax.axis_index("x")
    row = ylo * 4 + x
    rows = [
        {"ylo": lax.rem(row + j, 8) // 4, "x": lax.rem(row + j, 4)} for j in range(1, 8)
    ]
    return quad_others() + rows


def my_block():
    row = lax.axis_index("ylo") * 4 + lax.axis_index("x")
    return row * 4 + lax.axis_index("yhi") * 2 + lax.axis_index("core")


def line_prefix(mine, quad, rows, total, put, backward, meanwhile=lambda: None):
    me = lax.axis_index("yhi") * 2 + lax.axis_index("core")
    row = lax.axis_index("ylo") * 4 + lax.axis_index("x")
    copies = []
    for j in (1, 2, 3):
        copies.append(put(mine, quad.at[me], quad_device(lax.rem(me + j, 4))))
    quad[me] = mine[...]
    got(copies)
    ones = jnp.ones((1, CH), f32)
    zeros = jnp.zeros((1, CH), f32)
    prod, end, prod_all, end_all = ones, zeros, ones, zeros
    for turn in range(4):
        q = 3 - turn if backward else turn
        a, b = quad[q, 0:1, :], quad[q, 1:2, :]
        end_all = a * end_all + b
        prod_all = a * prod_all
        take = (q > me) if backward else (q < me)
        end = jnp.where(take, a * end + b, end)
        prod = jnp.where(take, a * prod, prod)
    total[0:1, :] = prod_all
    total[1:2, :] = end_all
    copies = []
    for j in range(1, 8):
        other = lax.rem(row + j, 8)
        copies.append(put(total, rows.at[row], {"ylo": other // 4, "x": lax.rem(other, 4)}))
    rows[row] = total[...]
    meanwhile()
    got(copies)
    came = zeros
    for turn in range(8):
        r = 7 - turn if backward else turn
        a, b = rows[r, 0:1, :], rows[r, 1:2, :]
        take = (r > row) if backward else (r < row)
        came = jnp.where(take, a * came + b, came)
    return prod * came + end


def split(values):
    high = values.astype(bf)
    return high, (values - high.astype(f32)).astype(bf)


def dot3(a, b, dims):
    (ah, al), (bh, bl) = a, b

    def one(p, q):
        return lax.dot_general(p, q, (dims, ((), ())), preferred_element_type=f32)

    return one(ah, bh) + (one(al, bh) + one(ah, bl))


def minus_expm1(v):
    near = -v * (
        1.0
        + v * (1 / 2) * (1.0 + v * (1 / 3) * (1.0 + v * (1 / 4) * (1.0 + v * (1 / 5) * (1.0 + v * (1 / 6)))))
    )
    return jnp.where(v > -0.3, near, 1.0 - jnp.exp(v))


def gelu_parts(v):
    cdf = 0.5 * (1.0 + lax.erf(v * 0.7071067811865476))
    pdf = 0.3989422804014327 * jnp.exp(-0.5 * v * v)
    return v * cdf, cdf + v * pdf


def shifted(values, by, fill, reverse):
    rows = lax.broadcasted_iota(jnp.int32, values.shape, 0)
    size = values.shape[0]
    if reverse:
        return jnp.where(rows < size - by, pltpu.roll(values, size - by, 0), fill)
    return jnp.where(rows >= by, pltpu.roll(values, by, 0), fill)


def behind(near, by):
    return near[8:24, :] if by == 0 else pltpu.roll(near, by, 0)[8:24, :]


def ahead(near, by):
    size = near.shape[0]
    return pltpu.roll(near, size - by, 0)[0 : size - 8, :]


def scan8(a, b, reverse):
    for by in (1, 2, 4):
        b = b + a * shifted(b, by, 0.0, reverse)
        a = a * shifted(a, by, 1.0, reverse)
    return a, b


def loop(count, body):
    def one(i, carry):
        body(i)
        return carry

    lax.fori_loop(0, count, one, 0)


def front_kernel(
    tokens, cotangent, rate_w, input_w, vectors, norms, mlp_gate, mlp_up, own_rec,
    x_out, n_out, xb_out, yb_out, c_out, rate_out, gin_out, a_out, m_out, h_out, hy_out, ext_out, hi_out, lo_out,
    cot, rec_out, w_gate, w_up,
    inv, gains, vec, state_in, total_a,
    full, normed, weights, params_all, norms_all, own_gate, own_up,
    xb, yb, c, rate, gin, a, m, h, hy, ext, gate_hi, gate_lo, pre, prod,
    halo, mine, quad, rows, total, send, recv, done,
):
    z = lax.axis_index("z")
    me = lax.axis_index("yhi") * 2 + lax.axis_index("core")
    block = my_block()
    after, before = lax.rem(block + 1, 32), lax.rem(block + 31, 32)
    meet(
        line_devices()
        + [plane_device(after), plane_device(before)]
        + plane_neighbours()
        + z_others()
    )
    put = Sender(send, recv)
    keep = Keeper(done)
    tokens_in = token_gather(tokens, full, put, keep)
    other = token_gather(cotangent, cot, put, keep)
    plane = plane_gather(own_rec, weights, put, keep)
    step(tokens_in, plane, other)
    small = []
    for j in (1, 2, 3):
        small.append(put(norms, norms_all.at[z, me], quad_device(lax.rem(me + j, 4))))
    norms_all[z, me] = norms[...]
    step(tokens_in, plane)
    for weight, top in ((rate_w, 0), (input_w, SQUARE)):
        params_all[me, top : top + HW, :] = weight[:, 0:128]
        params_all[me, top + HW : top + SQUARE, :] = jnp.zeros((48, 128), f32)
        for j, (at, size) in enumerate(TAILS):
            params_all[me, top + HW : top + HW + size, 32 * j : 32 * j + 32] = weight[at : at + size, 128:HW]
    params_all[me, 2 * SQUARE : 2 * SQUARE + 16, :] = vectors[:, 0:128]
    params_all[me, 2 * SQUARE + 16 : PACKED, :] = jnp.zeros((16, 128), f32)
    params_all[me, 2 * SQUARE + 16 : PACKED, 0:32] = vectors[:, 128:HW]
    got(small)
    small = []
    for j in (1, 2, 3):
        small.append(put(norms_all.at[z], norms_all.at[z], {"z": lax.rem(z + j, 4)}))
    step(plane)
    own_gate[...] = mlp_gate[...].astype(f32).T.astype(bf)
    own_up[...] = mlp_up[...].astype(f32).T.astype(bf)
    step(tokens_in)
    gate_hi[...] = jnp.zeros((CH, 2 * CH), bf)
    gate_lo[...] = jnp.zeros((CH, 2 * CH), bf)
    got(small)
    for i in range(4):
        for j in range(4):
            gains[:, 128 * (4 * i + j) : 128 * (4 * i + j + 1)] = norms_all[i, j]
    step(plane)
    plane_a = plane_gather(own_gate, w_gate, put, keep)
    plane_b = plane_gather(own_up, w_up, put, keep)
    step(plane_a, plane_b)
    finish(tokens_in)
    keep(full, x_out)
    core, yhi = lax.axis_index("core"), lax.axis_index("yhi")
    own_params = params_all.at[me]
    near = put(own_params, own_params, {"core": 1 - core})
    across = put(own_params, own_params, {"yhi": 1 - yhi})
    step(plane, other, plane_a, plane_b)

    def norm(i):
        r = pl.ds(pl.multiple_of(i * 16, 16), 16)
        values = full[r, :].astype(f32)
        mean = jnp.sum(values * values, axis=1, keepdims=True) * (1.0 / D)
        scale = lax.rsqrt(mean + EPS)
        inv[r, :] = jnp.broadcast_to(scale, (16, 128))
        normed[r, :] = (values * scale * gains[0:1, :]).astype(bf)

    loop(TOK // 16, norm)
    keep(normed, n_out)
    finish(plane)
    keep(weights, rec_out)
    across.wait_recv()
    peer_params = params_all.at[lax.rem(me + 2, 4)]
    passed = put(peer_params, peer_params, {"core": 1 - core})
    step(plane_a, other)
    for i, into in ((0, xb), (1, yb)):
        for at, width in ((0, 256), (256, 256), (512, 128)):
            into[:, at : at + width] = lax.dot_general(
                normed[...],
                weights[i, at : at + width, :],
                (((1,), (1,)), ((), ())),
                preferred_element_type=f32,
            )
        if i == 0:
            halo_out = pl.ds(TOK - 16, 16)
            hy[halo_out, :] = xb[halo_out, :].astype(bf)
            edge = put(hy.at[halo_out, :], halo, plane_device(after))
            step(plane_b)
    keep(xb, xb_out)
    keep(yb, yb_out)
    step(other, plane_a)

    def widen(i):
        r = pl.multiple_of(i * 16, 16)
        ext[pl.ds(pl.multiple_of(8 + r, 8), 16), :] = xb[pl.ds(r, 16), :].astype(bf).astype(f32)

    loop(TOK // 16, widen)
    got([near, passed])
    for i in range(4):
        there = HW * i
        vec[:, there : there + 128] = params_all[i, 2 * SQUARE : 2 * SQUARE + 16, :]
        vec[:, there + 128 : there + HW] = params_all[i, 2 * SQUARE + 16 : PACKED, 0:32]
        for k in (0, 1):
            top = SQUARE * k
            high, low = split(params_all[i, top : top + HW, :])
            over = CH * k + HW * i
            gate_hi[there : there + HW, over : over + 128] = high
            gate_lo[there : there + HW, over : over + 128] = low
            for j, (at, size) in enumerate(TAILS):
                high, low = split(params_all[i, top + HW : top + HW + size, 32 * j : 32 * j + 32])
                rows_here = slice(there + at, there + at + size)
                gate_hi[rows_here, over + 128 : over + HW] = high
                gate_lo[rows_here, over + 128 : over + HW] = low
    keep(gate_hi, hi_out)
    keep(gate_lo, lo_out)

    def conv(i):
        r = i * 16
        near = ext[pl.ds(pl.multiple_of(r, 16), 24), :]
        acc = vec[4:5, :] + vec[0:1, :] * near[8:24, :]
        for k in (1, 2, 3):
            acc = acc + vec[k : k + 1, :] * behind(near, k)
        c[pl.ds(pl.multiple_of(r, 16), 16), :] = acc

    lax.fori_loop(1, TOK // 16, lambda i, carry: (conv(i), carry)[1], 0)

    def gates(i):
        r = pl.ds(pl.multiple_of(i * 128, 128), 128)
        pre[r, :] = dot3(split(c[r, :]), (gate_hi[...], gate_lo[...]), ((1,), (0,)))

    lax.fori_loop(1, TOK // 128, lambda i, carry: (gates(i), carry)[1], 0)
    edge.wait_recv()
    ext[0:8, :] = jnp.where(block > 0, halo[8:16, :].astype(f32), 0.0)
    conv(0)
    gates(0)
    keep(ext, ext_out)
    keep(c, c_out)
    step(plane_a, plane_b, other)

    def point(i, carry):
        prod_in, state = carry
        r = pl.ds(pl.multiple_of(i * 8, 8), 8)
        rr = jax.nn.sigmoid(pre[r, 0:CH] + vec[5:6, :])
        gg = jax.nn.sigmoid(pre[r, CH:] + vec[6:7, :])
        log_a = -8.0 * rr * vec[7:8, :]
        aa = jnp.exp(log_a)
        mm = jnp.sqrt(minus_expm1(2.0 * log_a))
        rate[r, :] = rr
        gin[r, :] = gg
        a[r, :] = aa
        m[r, :] = mm
        pa, hb = scan8(aa, mm * gg * c[r, :], False)
        hb = hb + pa * state
        pa = pa * prod_in
        h[r, :] = hb
        prod[r, :] = pa
        return pa[7:8, :], hb[7:8, :]

    last = (jnp.ones((1, CH), f32), jnp.zeros((1, CH), f32))
    last = lax.fori_loop(0, TOK // 16, point, last)
    step(plane_b)
    last = lax.fori_loop(TOK // 16, TOK // 8, point, last)
    for source, target in ((rate, rate_out), (gin, gin_out), (a, a_out), (m, m_out)):
        keep(source, target)
    mine[...] = jnp.zeros((8, CH), f32)
    total[...] = jnp.zeros((8, CH), f32)
    step(plane_a)
    mine[0:1, :] = last[0]
    mine[1:2, :] = last[1]
    came = line_prefix(mine, quad, rows, total, put, False, lambda: step(plane_b))
    state_in[...] = jnp.broadcast_to(came, (8, CH))
    total_a[...] = jnp.broadcast_to(last[0], (8, CH))
    finish(other)
    edge.wait_send()

    def complete(i):
        r = pl.ds(pl.multiple_of(i * 16, 16), 16)
        hh = h[r, :] + prod[r, :] * came
        h[r, :] = hh
        hy[r, :] = (hh * gelu_parts(yb[r, :])[0]).astype(bf)

    loop(TOK // 16, complete)
    keep(h, h_out)
    keep(hy, hy_out)

    finish(plane_a, plane_b)
    put.drain(skip=edge)
    keep.drain()


def front(*operands):
    wide = shape((TOK, CH), f32)
    rows = shape((TOK, D), bf)
    mlp = shape((1536, D), bf)
    gate = shape((CH, 2 * CH), bf)
    out = (
        rows, rows, wide, wide, wide, wide, wide, wide, wide, wide,
        shape((TOK, CH), bf), shape((TOK + 8, CH), f32), gate, gate,
        rows, shape((3, CH, D), bf), mlp, mlp,
    )
    little = (
        shape((TOK, 128), f32), shape((8, D), f32), shape((16, CH), f32),
        shape((8, CH), f32), shape((8, CH), f32),
    )
    tall = pltpu.VMEM((TOK, CH), f32)
    return pl.pallas_call(
        front_kernel,
        out_shape=out + little,
        in_specs=[VMEM] * 8 + [ANY],
        out_specs=[ANY] * len(out) + [VMEM] * len(little),
        scratch_shapes=[
            pltpu.VMEM((TOK, D), bf),
            pltpu.VMEM((TOK, D), bf),
            pltpu.VMEM((3, CH, D), bf),
            pltpu.VMEM((4, PACKED, 128), f32),
            pltpu.VMEM((4, 4, 8, 128), f32),
            pltpu.VMEM((384, 256), bf),
            pltpu.VMEM((384, 256), bf),
            tall, tall, tall, tall, tall, tall, tall, tall,
            pltpu.VMEM((TOK, CH), bf),
            pltpu.VMEM((TOK + 8, CH), f32),
            pltpu.VMEM((CH, 2 * CH), bf),
            pltpu.VMEM((CH, 2 * CH), bf),
            pltpu.VMEM((TOK, 2 * CH), f32),
            tall,
            pltpu.VMEM((16, CH), bf),
            pltpu.VMEM((8, CH), f32),
            pltpu.VMEM((4, 8, CH), f32),
            pltpu.VMEM((8, 8, CH), f32),
            pltpu.VMEM((8, CH), f32),
        ]
        + semaphores(18 + 9 + 11 + 3 * GATHER_COPIES)
        + [pltpu.SemaphoreType.DMA((26,))],
        compiler_params=params(0),
        name="front",
    )(*operands)


def backward_kernel(
    dhy_in, yb_in, hi_in, lo_in, vec, c_in, rate_in, gin_in, a_in, m_in, h_in, ext_in, state_in, total_a,
    mlp_in, zown_in, down, gate,
    dxb, dyb, blocks, block_out, down_sum, gate_sum,
    e, apad, hpad, q, prod, pri, halo, mine, quad, rows, total, own, low, came_z, sent_z,
    yb, gate_hi, gate_lo, c, rate, gin, m, ext, mlp_part, z_own, dgate, sums, *rest,
):
    dc = q
    block = my_block()
    after, before = lax.rem(block + 1, 32), lax.rem(block + 31, 32)
    send, recv, done = rest[2 * SUM_SCRATCH :]
    keep = Keeper(done)
    load_mlp = keep(mlp_in, mlp_part)
    load_first = [
        keep(dhy_in, e),
        keep(yb_in, yb),
        keep(h_in, hpad.at[pl.ds(8, TOK), :]),
        keep(a_in, apad.at[pl.ds(0, TOK), :]),
    ]
    load_point = [keep(*pair) for pair in ((rate_in, rate), (gin_in, gin), (m_in, m), (c_in, c))]
    load_rest = [keep(*pair) for pair in ((hi_in, gate_hi), (lo_in, gate_lo), (ext_in, ext), (zown_in, z_own))]
    meet(
        line_devices()
        + [plane_device(after), plane_device(before)]
        + plane_neighbours()
        + z_others()
    )
    put = Sender(send, recv)
    whole = ring_sum(mlp_part, own, came_z, sent_z, put)
    plane = plane_sum([down], down_sum, rest[:SUM_SCRATCH], put, keep)
    plane_b = plane_sum([gate], gate_sum, rest[SUM_SCRATCH : 2 * SUM_SCRATCH], put, keep)
    keep.wait(load_mlp)
    step(whole, plane)
    for copy in load_first:
        keep.wait(copy)

    def direct(i):
        r = pl.ds(pl.multiple_of(i * 16, 16), 16)
        value, slope = gelu_parts(yb[r, :])
        grad = e[r, :]
        hh = hpad[pl.ds(pl.multiple_of(i * 16 + 8, 8), 16), :]
        e[r, :] = grad * value
        dyb[r, :] = (grad * hh * slope).astype(bf)

    loop(TOK // 16, direct)
    apad[TOK : TOK + 8, :] = jnp.ones((8, CH), f32)
    hpad[0:8, :] = state_in[...]
    step(plane_b)

    def adjoint(i, carry):
        prod_in, state = carry
        r0 = TOK - 8 - i * 8
        r = pl.ds(pl.multiple_of(r0, 8), 8)
        next_a = ahead(apad[pl.ds(pl.multiple_of(r0, 8), 16), :], 1)
        pa, qb = scan8(next_a, e[r, :], True)
        qb = qb + pa * state
        pa = pa * prod_in
        q[r, :] = qb
        prod[r, :] = pa
        return pa[0:1, :], qb[0:1, :]

    last = (jnp.ones((1, CH), f32), jnp.zeros((1, CH), f32))
    last = lax.fori_loop(0, TOK // 8, adjoint, last)
    step(whole)
    mine[...] = jnp.zeros((8, CH), f32)
    total[...] = jnp.zeros((8, CH), f32)
    mine[0:1, :] = total_a[0:1, :]
    mine[1:2, :] = apad[0:1, :] * last[1]
    came = line_prefix(mine, quad, rows, total, put, True, lambda: step(plane, plane_b))
    for copy in load_point:
        keep.wait(copy)

    def point(i, carry):
        s_rate, s_input, s_decay = carry
        r = pl.ds(pl.multiple_of(i * 8, 8), 8)
        qq = q[r, :] + prod[r, :] * came
        aa, rr, gg, mm, cc = apad[r, :], rate[r, :], gin[r, :], m[r, :], c[r, :]
        earlier = pltpu.roll(hpad[pl.ds(pl.multiple_of(i * 8, 8), 16), :], 1, 0)[8:16, :]
        grad_log = aa * (qq * earlier - qq * gg * cc * aa / mm)
        pr = -8.0 * vec[7:8, :] * grad_log * rr * (1.0 - rr)
        pi = qq * mm * cc * gg * (1.0 - gg)
        pri[r, 0:CH] = pr
        pri[r, CH:] = pi
        dc[r, :] = qq * mm * gg
        return s_rate + pr, s_input + pi, s_decay + 8.0 * rr * vec[8:9, :] * grad_log

    none = jnp.zeros((8, CH), f32)
    so_far = lax.fori_loop(0, TOK // 16, point, (none, none, none))
    step(plane)
    s_rate, s_input, s_decay = lax.fori_loop(TOK // 16, TOK // 8, point, so_far)
    step(plane_b)

    for copy in load_rest:
        keep.wait(copy)

    def spread(i):
        r = pl.ds(pl.multiple_of(i * 128, 128), 128)
        dc[r, :] = dc[r, :] + dot3(split(pri[r, :]), (gate_hi[...], gate_lo[...]), ((1,), (1,)))

    loop(TOK // 128, spread)
    edge = put(dc.at[pl.ds(0, 8), :], halo, plane_device(before))
    finish(whole)
    low[...] = (own[...] + z_own[...]).astype(bf)
    back, kept = quad_scatter(low, block_out, put, keep)
    dgate[...] = dot3(split(c[...]), split(pri[...]), ((0,), (0,)))
    step(plane)
    edge.wait_recv()
    dc[TOK : TOK + 8, :] = jnp.where(block < 31, halo[...], 0.0)

    def taps(i, carry):
        r = i * 16
        here = pl.ds(pl.multiple_of(r, 16), 16)
        later = dc[pl.ds(pl.multiple_of(r, 16), 24), :]
        near = ext[pl.ds(pl.multiple_of(r, 16), 24), :]
        dd = later[0:16, :]
        out = vec[0:1, :] * dd
        for k in (1, 2, 3):
            out = out + vec[k : k + 1, :] * ahead(later, k)
        dxb[here, :] = out.astype(bf)

        def fold(v):
            return v[0:8, :] + v[8:16, :]

        new = [carry[0] + fold(dd)]
        for k in range(4):
            new.append(carry[1 + k] + fold(dd * behind(near, k)))
        return tuple(new)

    s_bias, *s_taps = lax.fori_loop(0, TOK // 16, taps, (none,) * 5)

    step(plane_b, plane)

    def place_sum(row, value):
        sums[row : row + 1, :] = jnp.sum(value, axis=0, keepdims=True)

    for k in range(4):
        place_sum(k, s_taps[k])
    place_sum(4, s_bias)
    place_sum(5, s_rate)
    place_sum(6, s_input)
    place_sum(7, s_decay)
    for i in range(4):
        there = HW * i
        for k in (0, 1):
            top, over = SQUARE * k, CH * k + HW * i
            blocks[i, top : top + HW, :] = dgate[there : there + HW, over : over + 128]
            for j, (at, size) in enumerate(TAILS):
                blocks[i, top + HW : top + HW + size, 32 * j : 32 * j + 32] = dgate[
                    there + at : there + at + size, over + 128 : over + HW
                ]
            blocks[i, top + HW + 16 : top + SQUARE, 96:128] = jnp.zeros((32, 32), f32)
        blocks[i, 2 * SQUARE :, :] = jnp.zeros((32, 128), f32)
        blocks[i, 2 * SQUARE : 2 * SQUARE + 8, :] = sums[:, there : there + 128]
        blocks[i, 2 * SQUARE + 16 : 2 * SQUARE + 24, 0:32] = sums[:, there + 128 : there + HW]
    finish(plane, plane_b)
    got(back)
    keep.wait(kept)
    put.drain()
    keep.drain()


def backward_scan(*operands):
    r = operands[-1].shape[0] // 4
    tall = pltpu.VMEM((TOK, CH), f32)
    return pl.pallas_call(
        backward_kernel,
        out_shape=(
            shape((TOK, CH), bf),
            shape((TOK, CH), bf),
            shape((4, PACKED, 128), f32),
            shape((4 * TOK, 128), bf),
            shape((r, 256), f32),
            shape((r, 256), f32),
        ),
        in_specs=[ANY] * 4 + [VMEM] + [ANY] * 7 + [VMEM] * 2 + [ANY] * 4,
        out_specs=[VMEM] * 6,
        scratch_shapes=[
            tall,
            pltpu.VMEM((TOK + 8, CH), f32),
            pltpu.VMEM((TOK + 8, CH), f32),
            pltpu.VMEM((TOK + 8, CH), f32),
            tall,
            pltpu.VMEM((TOK, 2 * CH), f32),
            pltpu.VMEM((8, CH), f32),
            pltpu.VMEM((8, CH), f32),
            pltpu.VMEM((4, 8, CH), f32),
            pltpu.VMEM((8, 8, CH), f32),
            pltpu.VMEM((8, CH), f32),
            pltpu.VMEM((TOK, 512), f32),
            pltpu.VMEM((TOK, 512), bf),
        ]
        + ring_scratch()
        + [
            tall,
            pltpu.VMEM((CH, 2 * CH), bf),
            pltpu.VMEM((CH, 2 * CH), bf),
            tall,
            tall,
            tall,
            tall,
            pltpu.VMEM((TOK + 8, CH), f32),
            pltpu.VMEM((TOK, D), bf),
            pltpu.VMEM((TOK, 512), f32),
            pltpu.VMEM((CH, 2 * CH), f32),
            pltpu.VMEM((8, CH), f32),
        ]
        + sum_scratch(r)
        + sum_scratch(r)
        + semaphores(11 + 6 + 3 + 2 * SUM_COPIES)
        + [pltpu.SemaphoreType.DMA((14 + 2 * SUM_KEEPS,))],
        compiler_params=params(4),
        name="backward_scan",
    )(*operands)


def per_device(
    block_in, cotangent, norm_one, rec_in, rec_gate, conv_weight, conv_bias,
    rate_weight, rate_bias, input_weight, input_bias, decay_code, rec_out,
    norm_two, mlp_gate, mlp_up, mlp_down,
):
    decay = decay_code.astype(f32) / 256.0
    vectors = jnp.concatenate(
        [
            conv_weight,
            conv_bias[None],
            rate_bias[None],
            input_bias[None],
            jax.nn.softplus(-decay)[None],
            jax.nn.sigmoid(-decay)[None],
            jnp.zeros((7, HW), f32),
        ],
        axis=0,
    )
    norms = jnp.concatenate([norm_one[None], norm_two[None], jnp.zeros((6, 128), f32)], axis=0)
    (
        x_full, n_one, xb, yb, c, rate, gin, a, m, h, hy, ext, gate_hi, gate_lo,
        cot_full, w_rec, w_gate, w_up,
        inv_one, gains, vec, state_in, total_a,
    ) = front(
        block_in, cotangent, rate_weight[0], input_weight[0], vectors, norms, mlp_gate, mlp_up,
        jnp.stack([rec_in.T, rec_gate.T, rec_out]),
    )
    z_own, dz_own, dhy, mlp_part, part_out, part_down, part_gate, part_up, gain_two_sums = middle(
        hy, w_rec, x_full, cot_full, w_gate, w_up, mlp_down, gains
    )
    dxb, dyb, blocks, block_out, grad_down, grad_gate = backward_scan(
        dhy, yb, gate_hi, gate_lo, vec, c, rate, gin, a, m, h, ext, state_in, total_a,
        mlp_part, z_own, part_down, part_gate,
    )
    grad_in, grad_rec_in, grad_rec_gate, grad_out, grad_up, grad_rate, grad_input, vector_grads, gain_sums = tail(
        dxb, dyb, xb, yb, w_rec, x_full, n_one, dz_own, part_out, part_up,
        inv_one, gains, gain_two_sums, blocks,
    )
    return (
        block_out,
        grad_in,
        gain_sums[0],
        grad_rec_in,
        grad_rec_gate,
        vector_grads[0:4],
        vector_grads[4],
        grad_rate[None],
        vector_grads[5],
        grad_input[None],
        vector_grads[6],
        vector_grads[7],
        grad_out,
        gain_sums[1],
        grad_gate.T,
        grad_up,
        grad_down,
    )


def solution(mesh):
    fine = Mesh(mesh.devices.reshape(2, 4, 4, 2, 2), ("ylo", "x", "z", "yhi", "core"))
    both = P(SEQ, HEAD)
    swap = P(HEAD, SEQ)
    vector = P(HEAD)
    stack = P(HEAD, None, None)
    taps = P(None, HEAD)
    return jax.shard_map(
        per_device,
        mesh=fine,
        in_specs=(
            both, both, vector, both, both, taps, vector, stack, vector, stack, vector, vector,
            swap, vector, both, both, swap,
        ),
        out_specs=(
            both, both, vector, both, both, taps, vector, stack, vector, stack, vector, vector,
            swap, vector, both, both, swap,
        ),
        check_vma=False,
    )
```
